32 devices in a mesh: shot: 2 (over core), space: 16 (over z, y, x).
Axes of the slice: x: 2, y: 2, z: 4, core: 2. Of those that a mesh axis runs over, the one named last changes fastest.
Arguments:
- wavefields: float32 [4, 2, 2, 64, 128, 256], P('shot', None, None, 'space'), may hold values from -6 to 6
- courant: float32 [64, 192, 256], P('space'), may hold values from 0.03 to 0.2
- offsets: int32 [4], P('shot'), may hold values from 0 to 64
- strip_lines: bfloat16 [4, 2048, 256], P('shot', 'space'), may hold values from -6 to 6
- strip_ids: int32 [4, 2048], P('shot', 'space'), may hold values from -1 to 1023, as said below
- receiver_pos: int32 [4, 1024], P('shot', 'space'), may hold values from 0 to 511
- traces: float32 [4, 4, 1024], P('shot', None, 'space'), may hold values from -12 to 12
Outputs:
- wavefields_out: float32 [4, 2, 2, 64, 128, 256], P('shot', None, None, 'space')
- image: float32 [64, 192, 256], P('space')
The draws below stay inside these ranges and needn't reach their ends.
Inputs may be any that keep to these rules, and one draw needn't show every extreme that they name: `strip_ids`: -1 marks an empty slot. For each shot every line number from 0 to 64 times the devices of space, minus 1, appears exactly once. Of the 128 slots of one device (an aligned block), at most 8 hold lines of one owner o = j // 64, and in every draw some device holds exactly 8 lines of one owner.
All inputs are finite; a program needn't handle non-finite values.
Results may differ from the reference program's by a relative error of at most 0.00105.
Values may be sent and summed in bfloat16 or wider, within the bound.
No kernel may reach another device: no remote copies, remote signals or barrier semaphores. Data moves between devices by JAX's collectives and lax.ppermute only.
A program may use at most 128 MiB of HBM per device.

```python
import math
import jax
import jax.numpy as jnp
from jax import lax

CX = 4
AY = 128
AZ = 256
SPANY = 64
STEPS = 4
RDEPTH = 4
REC_DEV = 64
NX = 64
MY = 192
SHOTS = 4
NEED = 64
CAP = 8
HOLD = 128
NRX = 1024
N_SPACE = 16


def draw_strip_ids(key, part):
    holders = N_SPACE
    capacity = CAP

    def one_shot(shot_key):
        owner_key, slot_key = jax.random.split(shot_key)

        def one_owner(okey, owner_dev):
            first_key, second_key, third_key = jax.random.split(okey, 3)
            order = jax.random.permutation(first_key, NEED).astype(jnp.int32)
            halves = jax.random.randint(second_key, (holders // 2,), 0, capacity + 1).astype(jnp.int32)
            halves = halves.at[0].set(capacity)
            paired = jnp.stack([halves, capacity - halves], axis=1).reshape(holders)
            counts = jax.random.permutation(third_key, paired)
            starts = jnp.cumsum(counts) - counts
            slot_index = jnp.arange(capacity, dtype=jnp.int32)
            picked = jnp.clip(starts[:, None] + slot_index[None, :], 0, NEED - 1)
            line_of = order[picked]
            return jnp.where(slot_index[None, :] < counts[:, None], owner_dev * NEED + line_of, -1)
        owner_keys = jax.random.split(owner_key, holders)
        table = jax.vmap(one_owner)(owner_keys, jnp.arange(holders, dtype=jnp.int32))
        held = jnp.transpose(table, (1, 0, 2)).reshape(holders, holders * capacity)
        holder_keys = jax.random.split(slot_key, holders)
        held = jax.vmap(lambda hkey, row_ids: jax.random.permutation(hkey, row_ids))(holder_keys, held)
        return held.reshape(holders * holders * capacity)
    shot_keys = jax.random.split(key, SHOTS)
    return jax.vmap(one_shot)(shot_keys).astype(jnp.int32)


def with_ends(drawn, rng, low, high):
    extent = drawn.shape
    spot = [jax.random.randint(jax.random.fold_in(rng, axis), (), 0, extent[axis]) for axis in range(len(extent))]
    drawn = drawn.at[tuple(spot)].set(low)
    longest = extent.index(max(extent))
    spot[longest] = (spot[longest] + 1) % extent[longest]
    return drawn.at[tuple(spot)].set(high)


def steps_of(own_key, dims, cuts, least, largest):
    def one(position, blocks):
        draws = jax.random.uniform(jax.random.fold_in(jax.random.fold_in(own_key, 6), position), (blocks,), jnp.float32, least / len(cuts), largest / len(cuts))
        return jnp.repeat(jnp.exp(draws), dims[position] // blocks).reshape((-1,) + (1,) * (len(dims) - position - 1))

    factor_of = one(*cuts[0])
    for cut in cuts[1:]:
        factor_of = factor_of * one(*cut)
    return factor_of


def centred(rng, shape, scale, reach, cuts=(), kind=jnp.bfloat16):
    gain = steps_of(rng, shape, cuts, -0.22, 0.18) if cuts else 1.0
    drawn = jax.random.normal(rng, shape, jnp.float32) * scale * gain
    return jnp.minimum(jnp.maximum(drawn, -reach), reach).astype(kind)


def setup_inputs(seed: int = 0) -> dict:
    splits = jax.random.split(jax.random.key(seed), 8)
    wavefields = centred(splits[0], (SHOTS, 2, 2, NX, AY, AZ), 1.0, 6.0, ((0, 2), (3, 16)), jnp.float32)
    courant = jnp.clip(jnp.exp(math.log(0.2) - 1.89712 * jax.random.uniform(splits[1], (NX, MY, AZ), jnp.float32) ** steps_of(splits[1], (NX, MY, AZ), ((0, 16),), -0.2, 0.2)), 0.03, 0.2)
    offsets = with_ends(jax.random.randint(splits[2], (SHOTS,), 0, SPANY + 1), jax.random.fold_in(splits[2], 1), 0, SPANY).astype(jnp.int32)
    strip_lines = centred(splits[3], (SHOTS, N_SPACE * HOLD, AZ), 1.0, 6.0, ((0, 2), (1, 16)))
    strip_ids = draw_strip_ids(jax.random.fold_in(splits[7], 71), 0)
    receiver_pos = with_ends(jax.random.randint(splits[5], (SHOTS, NRX), 0, CX * AY), jax.random.fold_in(splits[5], 1), 0, (CX * AY) - 1).astype(jnp.int32)
    traces = centred(splits[6], (SHOTS, STEPS, NRX), 2.0, 12.0, ((0, 2), (2, 16)), jnp.float32)
    return {"wavefields": wavefields, "courant": courant, "offsets": offsets, "strip_lines": strip_lines, "strip_ids": strip_ids, "receiver_pos": receiver_pos, "traces": traces}


FAR_COEF = -1.0 / 12.0
NEAR_COEF = 4.0 / 3.0
MID_COEF = -2.5


def second_diff(wavefield, direction):
    padding = [(0, 0)] * wavefield.ndim
    padding[direction] = (2, 2)
    padded = jnp.pad(wavefield, padding)
    length = wavefield.shape[direction]

    def shifted(offset_at):
        return lax.slice_in_dim(padded, offset_at, offset_at + length, axis=direction)

    return FAR_COEF * (shifted(0) + shifted(4)) + NEAR_COEF * (shifted(1) + shifted(3)) + MID_COEF * wavefield


def laplacian(current):
    return second_diff(current, 1) + second_diff(current, 2) + second_diff(current, 3)


def reference(wavefields, courant, offsets, strip_lines, strip_ids, receiver_pos, traces):
    per_owner = STEPS * 4 * CX
    zero_index = jnp.zeros((), jnp.int32)
    block_of = jnp.arange(NRX, dtype=jnp.int32) // REC_DEV

    def one_shot(total, inputs):
        fields, start_y, row_data, line_ids, spots, trace_rows = inputs
        slot_of = jnp.where(line_ids >= 0, line_ids, N_SPACE * per_owner).astype(jnp.int32)
        lines = jnp.zeros((N_SPACE * per_owner, AZ), jnp.float32).at[slot_of].set(row_data.astype(jnp.float32), mode="drop")
        lines = lines.reshape(N_SPACE, STEPS, CX, 4, AZ).transpose(1, 0, 2, 3, 4).reshape(STEPS, NX, 4, AZ)
        speed = lax.dynamic_slice(courant, (zero_index, start_y.astype(jnp.int32), zero_index), (NX, AY, AZ))
        cells = ((block_of * CX + spots // AY) * AY + spots % AY).astype(jnp.int32)
        current = fields[0]
        previous = fields[1]
        contrib = jnp.zeros((NX, AY, AZ), jnp.float32)
        for time_step in range(STEPS):
            plane = jnp.zeros((NX * AY,), jnp.float32).at[cells].add(trace_rows[time_step]).reshape(NX, AY)
            growth = laplacian(current).at[1, :, :, RDEPTH].add(plane)
            earlier = 2.0 * current - previous + speed * growth
            boundary = lines[time_step]
            earlier = earlier.at[0, :, 0:2].set(boundary[:, 0:2])
            earlier = earlier.at[0, :, AY - 2:].set(boundary[:, 2:4])
            contrib = contrib + current[0] * (earlier[1] - 2.0 * current[1] + previous[1])
            previous = current
            current = earlier
        window = lax.dynamic_slice(total, (zero_index, start_y.astype(jnp.int32), zero_index), (NX, AY, AZ))
        total = lax.dynamic_update_slice(total, window + contrib, (zero_index, start_y.astype(jnp.int32), zero_index))
        return total, jnp.stack([current, previous], axis=0)

    total, outputs = lax.scan(one_shot, jnp.zeros((NX, MY, AZ), jnp.float32),
                              (wavefields, offsets, strip_lines, strip_ids, receiver_pos, traces))
    return outputs, total * (1.0 / SHOTS)
```

```python
import functools

import jax
import jax.numpy as jnp
from jax import lax
from jax.experimental import pallas as pl
from jax.experimental.pallas import tpu as pltpu
from jax.sharding import PartitionSpec as P

STEPS = 4
RDEPTH = 4
EDGE = 4
LANES = 128
VMEM_LIMIT = 40 * 1024 * 1024
VMEM = pltpu.VMEM
SMEM = pltpu.SMEM


def params():
    return pltpu.CompilerParams(vmem_limit_bytes=VMEM_LIMIT)


def cost(flops, moved):
    return pl.CostEstimate(flops=flops, bytes_accessed=moved, transcendentals=0)


def swap_pairs(value, first):
    count = lax.axis_size("space")
    routes = []
    for at in range(first, count - 1, 2):
        routes += [(at, at + 1), (at + 1, at)]
    return lax.ppermute(value, "space", routes)


def band(rows, centre):
    gap = jnp.abs(
        lax.broadcasted_iota(jnp.int32, (rows, rows), 0)
        - lax.broadcasted_iota(jnp.int32, (rows, rows), 1)
    )
    weights = jnp.where(gap == 0, centre, jnp.where(gap == 1, 16.0, jnp.where(gap == 2, -1.0, 0.0)))
    return weights.astype(jnp.bfloat16)


def mm(left, right, dims=((1,), (0,))):
    return lax.dot_general(left, right, (dims, ((), ())), preferred_element_type=jnp.float32)


def window_at(offset, model_y, rows_y):
    start = jnp.minimum(lax.div(offset, 8), (model_y - rows_y - 8) // 8) * 8
    return pl.multiple_of(start, 8), offset - start


def add_window(target_ref, lead, part, offset):
    rows_y = part.shape[0]
    start, gap = window_at(offset, target_ref.shape[-2], rows_y)
    moved = jnp.concatenate([part, jnp.zeros((8, part.shape[1]), part.dtype)], axis=0)
    at = lead + (pl.ds(start, rows_y + 8), slice(None))
    target_ref[at] = target_ref[at] + pltpu.roll(moved, gap, 0)


def is_odd():
    return lax.rem(lax.axis_index("space"), 2) == 1


def write_sends(field_ref, lead, send0_ref, send1_ref):
    odd = is_odd()
    for comp in range(2):
        for at in range(2):
            low = field_ref[lead + (comp, at)]
            high = field_ref[lead + (comp, at + field_ref.shape[-3] - 2)]
            send0_ref[comp, at] = jnp.where(odd, low, high).astype(jnp.bfloat16)
            send1_ref[comp, at] = jnp.where(odd, high, low).astype(jnp.bfloat16)


def pack_kernel(field_ref, send0_ref, send1_ref):
    write_sends(field_ref, (0, 0), send0_ref, send1_ref)


def pack_halo(wavefields, shot):
    _, _, comps, layers, rows_y, cells_z = wavefields.shape
    half = jax.ShapeDtypeStruct((comps, 2, rows_y, cells_z), jnp.bfloat16)
    whole = pl.BlockSpec(half.shape, lambda i: (0, 0, 0, 0))
    return pl.pallas_call(
        pack_kernel,
        grid=(1,),
        in_specs=[
            pl.BlockSpec((1, 1, comps, layers, rows_y, cells_z), lambda i: (shot, 0, 0, 0, 0, 0))
        ],
        out_specs=[whole, whole],
        out_shape=[half, half],
        compiler_params=params(),
        cost_estimate=cost(10**6, 2 * 2**20),
        name="pack_halo",
    )(wavefields)


def pack_lines_kernel(cap, per_owner, ids_ref, lines_ref, out_ref):
    shots, hold = ids_ref.shape
    total = shots * hold
    ids = jnp.concatenate([ids_ref[shot : shot + 1] for shot in range(shots)], axis=1)
    ids = ids.astype(jnp.float32)
    row_at = lax.broadcasted_iota(jnp.int32, (total, total), 0)
    col_at = lax.broadcasted_iota(jnp.int32, (total, total), 1)
    slot_at = lax.broadcasted_iota(jnp.int32, (1, total), 1)
    shot_of = jnp.zeros((1, total), jnp.float32)
    for shot in range(1, shots):
        shot_of = shot_of + (slot_at >= shot * hold).astype(jnp.float32)
    owner = jnp.floor((ids + 0.5) * (1.0 / per_owner))
    inside = ids - owner * per_owner
    used = ids >= 0.0
    key = jnp.where(used, owner * shots + shot_of, -1.0)
    wide_key = jnp.broadcast_to(key, (total, total))
    same = jnp.where(row_at == col_at, wide_key, 0.0)
    tall_key = jnp.sum(same, axis=1, keepdims=True)
    earlier_one = (tall_key == wide_key) & (row_at < col_at)
    rank = jnp.sum(earlier_one.astype(jnp.float32), axis=0, keepdims=True)
    target = jnp.where(used, key * cap + rank, -1.0)
    hot = jnp.where(row_at.astype(jnp.float32) == target, 1.0, 0.0)
    tags = jnp.sum(hot * (inside + 1.0), axis=1, keepdims=True)
    hot = hot.astype(jnp.bfloat16)
    cells_z = lines_ref.shape[2]
    rows = mm(hot[:, :hold], lines_ref[0])
    for shot in range(1, shots):
        rows = rows + mm(hot[:, shot * hold : (shot + 1) * hold], lines_ref[shot])
    out_ref[:, :cells_z] = rows.astype(jnp.bfloat16)
    out_ref[:, cells_z:] = jnp.broadcast_to(tags, (total, LANES)).astype(jnp.bfloat16)


def unpack_lines_kernel(cap, shots, per_owner, got_ref, out_ref):
    total = got_ref.shape[0]
    cells_z = out_ref.shape[1]
    tags = got_ref[:, cells_z : cells_z + LANES].astype(jnp.float32)[:, 0:1]
    row_at = lax.broadcasted_iota(jnp.int32, (total, 1), 0).astype(jnp.float32)
    block = jnp.floor((row_at + 0.5) * (1.0 / cap))
    shot_of = block - shots * jnp.floor((block + 0.5) * (1.0 / shots))
    target = jnp.where(tags > 0.5, tags - 1.0 + shot_of * per_owner, -1.0)
    line_at = lax.broadcasted_iota(jnp.int32, (total, shots * per_owner), 1).astype(jnp.float32)
    hot = jnp.where(line_at == target, 1.0, 0.0).astype(jnp.bfloat16)
    out_ref[...] = mm(hot, got_ref[:, :cells_z], ((0,), (0,)))


def deliver(strip_lines, strip_ids, per_owner):
    shots, hold, cells_z = strip_lines.shape
    holders = lax.axis_size("space")
    cap = hold // holders
    total = shots * hold
    wide = cells_z + LANES
    message = pl.pallas_call(
        functools.partial(pack_lines_kernel, cap, per_owner),
        out_shape=jax.ShapeDtypeStruct((total, wide), jnp.bfloat16),
        compiler_params=params(),
        cost_estimate=cost(10**6, 2**19),
        name="pack_lines",
    )(strip_ids, strip_lines)
    message = message.reshape(holders, shots * cap, wide)
    got = lax.all_to_all(message, "space", 0, 0, tiled=False)
    got = got.reshape(total, wide)
    return pl.pallas_call(
        functools.partial(unpack_lines_kernel, cap, shots, per_owner),
        out_shape=jax.ShapeDtypeStruct((shots * per_owner, cells_z), jnp.float32),
        compiler_params=params(),
        cost_estimate=cost(10**6, 2**19),
        name="unpack_lines",
    )(got)


def split3(value):
    parts = []
    for _ in range(3):
        part = value.astype(jnp.bfloat16)
        parts.append(part)
        value = value - part.astype(jnp.float32)
    return parts


def step_kernel(shot, step, first, last, *refs):
    refs = list(refs)
    take = lambda: refs.pop(0)
    offsets_ref = take() if first else None
    now_ref, later_ref = take(), take()
    got0_ref, got1_ref = take(), take()
    saved_ref, pos_ref, traces_ref = take(), take(), take()
    speed_from = take()
    contrib_from = None if first else take()
    if last and shot > 0:
        take()
    if last:
        out_ref, contrib_ref, new_ref, sems = take(), take(), take(), take()
    else:
        new_ref, send0_ref, send1_ref, contrib_ref = take(), take(), take(), take()
        speed_out = take() if first else None
    lead = (0, 0) if first else ()
    lead_later = (0, 0) if step < 2 else ()
    layers, rows_y, cells_z = new_ref.shape[-3:]
    if last:
        keep = pltpu.make_async_copy(now_ref, out_ref.at[shot, 1], sems.at[0])
        keep.start()
    odd = is_odd()
    across_z = band(cells_z, -90.0)
    across_y = band(rows_y, 0.0)
    trace_row = traces_ref[shot, step : step + 1, :]
    lane_of = lax.broadcasted_iota(jnp.int32, (LANES, trace_row.shape[1]), 0)
    trace_parts = [
        jnp.where(lane_of == RDEPTH, part.astype(jnp.float32), 0.0).astype(jnp.bfloat16)
        for part in split3(trace_row)
    ]
    spots = pos_ref[shot : shot + 1, :]
    cell_of = lax.broadcasted_iota(jnp.int32, (rows_y, trace_row.shape[1]), 0)

    for layer in range(layers):
        if first:
            start_y, gap = window_at(offsets_ref[shot], speed_from.shape[1], rows_y)
            speed = speed_from[layer, pl.ds(start_y, rows_y + 8), :]
            speed = pltpu.roll(speed, lax.rem(rows_y + 8 - gap, rows_y + 8), 0)[:rows_y]
            speed_out[layer] = speed
        else:
            speed = speed_from[layer]
        for comp in range(2):
            def layer_of(at):
                if at < 0:
                    both = (got1_ref[comp, 2 + at], got0_ref[comp, 2 + at])
                elif at >= layers:
                    both = (got0_ref[comp, at - layers], got1_ref[comp, at - layers])
                else:
                    return now_ref[lead + (comp, at)]
                even_one, odd_one = (part.astype(jnp.float32) for part in both)
                return jnp.where(odd, odd_one, even_one)

            here = layer_of(layer)
            high = here.astype(jnp.bfloat16)
            low = (here - high.astype(jnp.float32)).astype(jnp.bfloat16)
            growth = mm(high, across_z) + mm(low, across_z)
            growth = growth + (mm(across_y, high) + mm(across_y, low))
            growth = growth + 16.0 * (layer_of(layer - 1) + layer_of(layer + 1))
            growth = growth - (layer_of(layer - 2) + layer_of(layer + 2))
            growth = growth * (1.0 / 12.0)
            if comp == 1:
                hot = jnp.where(spots == cell_of + layer * rows_y, 1.0, 0.0).astype(jnp.bfloat16)
                plane = mm(hot, trace_parts[0], ((1,), (1,)))
                plane = plane + mm(hot, trace_parts[1], ((1,), (1,)))
                plane = plane + mm(hot, trace_parts[2], ((1,), (1,)))
                growth = jnp.concatenate(
                    [growth[:, :LANES] + plane, growth[:, LANES:]], axis=1
                )
            change = speed * growth
            new_ref[comp, layer] = 2.0 * here - later_ref[lead_later + (comp, layer)] + change
            if comp == 1:
                term = now_ref[lead + (0, layer)] * change
                contrib_ref[layer] = term if first else contrib_from[layer] + term
        per_step = layers * EDGE
        base = (shot * STEPS + step) * per_step + layer * EDGE
        new_ref[0, layer, 0:2, :] = saved_ref[base : base + 2, :]
        new_ref[0, layer, rows_y - 2 :, :] = saved_ref[base + 2 : base + 4, :]
    if last:
        give = pltpu.make_async_copy(new_ref, out_ref.at[shot, 0], sems.at[1])
        give.start()
        give.wait()
        keep.wait()
    else:
        write_sends(new_ref, (), send0_ref, send1_ref)


def one_step(shot, step, shots, offsets, now, later, got, saved, pos, traces, speed, contrib, out):
    first, last = step == 0, step == STEPS - 1
    comps, layers, rows_y, cells_z = now.shape[-4:]
    vmem = pl.BlockSpec(memory_space=VMEM)
    state = jax.ShapeDtypeStruct((comps, layers, rows_y, cells_z), jnp.float32)
    half = jax.ShapeDtypeStruct((comps, 2, rows_y, cells_z), jnp.bfloat16)
    image = jax.ShapeDtypeStruct((layers, rows_y, cells_z), jnp.float32)
    args, specs, aliases = [], [], {}
    scratch = []
    block = (1, 1) + state.shape
    if first:
        args.append(offsets)
        specs.append(pl.BlockSpec(memory_space=SMEM))
    for at, field in enumerate((now, later)):
        args.append(field)
        if field.ndim == 6:
            at = at if first else 0
            specs.append(pl.BlockSpec(block, lambda i, at=at: (shot, at, 0, 0, 0, 0)))
        else:
            specs.append(vmem)
    args += [*got, saved, pos, traces, speed]
    specs += [vmem] * 6
    if not first:
        args.append(contrib)
        specs.append(vmem)
    if last:
        shape_out = jax.ShapeDtypeStruct((shots, 2) + state.shape, jnp.float32)
        if shot > 0:
            aliases[len(args)] = 0
            args.append(out)
            specs.append(pl.BlockSpec(memory_space=pl.ANY))
        outs = [shape_out, image]
        out_specs = [pl.BlockSpec(memory_space=pl.ANY), vmem]
        scratch = [pltpu.VMEM(state.shape, jnp.float32), pltpu.SemaphoreType.DMA((2,))]
    else:
        outs = [state, half, half, image] + ([image] if first else [])
        out_specs = [vmem] * len(outs)
    return pl.pallas_call(
        functools.partial(step_kernel, shot, step, first, last),
        grid=(1,),
        in_specs=specs,
        out_specs=out_specs,
        out_shape=outs,
        scratch_shapes=scratch,
        input_output_aliases=aliases,
        compiler_params=params(),
        cost_estimate=cost(10**9, 5 * 2**20),
        name="step",
    )(*args)


def frame_kernel(scale, sides, offsets_ref, *refs):
    image_ref = refs[-1]
    shots = (len(refs) - 1) // sides
    layers = image_ref.shape[0]
    image_ref[...] = jnp.zeros_like(image_ref)
    for layer in range(layers):
        for shot in range(shots):
            add_window(image_ref, (layer,), refs[shot][layer], offsets_ref[shot])


def image_kernel(scale, offsets_ref, others_ref, *refs):
    image_ref, frame_ref = refs[-2:]
    shots = (len(refs) - 2) // 2
    layers = image_ref.shape[0]
    for layer in range(layers):
        for side, places in ((0, offsets_ref), (1, others_ref)):
            frame_ref[side] = jnp.zeros_like(frame_ref[side])
            for shot in range(shots):
                add_window(frame_ref, (side,), refs[side * shots + shot][layer], places[shot])
        image_ref[layer] = (frame_ref[0] + frame_ref[1]) * scale


def body(wavefields, courant, offsets, strip_lines, strip_ids, receiver_pos, traces):
    shots = wavefields.shape[0]
    layers, rows_y, cells_z = wavefields.shape[3:]
    model_y = courant.shape[1]
    per_owner = STEPS * EDGE * layers
    shot_devices = lax.axis_size("shot")
    scale = 1.0 / (shots * shot_devices)

    def exchange(sends):
        return swap_pairs(sends[0], 0), swap_pairs(sends[1], 1)

    got = [exchange(pack_halo(wavefields, shot)) for shot in range(shots)]
    saved = deliver(strip_lines, strip_ids, per_owner)
    swap = [(0, 1), (1, 0)]
    paired = shot_devices == 2
    if paired:
        others_at = lax.ppermute(offsets, "shot", swap)
    now = [wavefields] * shots
    later = [wavefields] * shots
    contrib = [None] * shots
    speed = [courant] * shots
    out = None
    others = []
    for step in range(STEPS):
        for shot in range(shots):
            made = one_step(
                shot, step, shots, offsets, now[shot], later[shot], got[shot], saved, receiver_pos,
                traces, speed[shot], contrib[shot], out,
            )
            if step == STEPS - 1:
                out, contrib[shot] = made
                if paired:
                    others.append(lax.ppermute(contrib[shot], "shot", swap))
                continue
            got[shot] = exchange(made[1:3])
            contrib[shot] = made[3]
            if step == 0:
                speed[shot] = made[4]
            later[shot], now[shot] = now[shot], made[0]
    smem, vmem = pl.BlockSpec(memory_space=SMEM), pl.BlockSpec(memory_space=VMEM)
    shape_out = jax.ShapeDtypeStruct((layers, model_y, cells_z), jnp.float32)
    if paired:
        image = pl.pallas_call(
            functools.partial(image_kernel, scale),
            in_specs=[smem, smem] + [vmem] * (2 * shots),
            out_specs=vmem,
            out_shape=shape_out,
            scratch_shapes=[pltpu.VMEM((2, model_y, cells_z), jnp.float32)],
            compiler_params=params(),
            cost_estimate=cost(10**6, 3 * 2**20),
            name="image",
        )(offsets, others_at, *contrib, *others)
    else:
        frame = pl.pallas_call(
            functools.partial(frame_kernel, scale, 1),
            in_specs=[smem] + [vmem] * shots,
            out_specs=vmem,
            out_shape=shape_out,
            compiler_params=params(),
            cost_estimate=cost(10**6, 3 * 2**20),
            name="frame",
        )(offsets, *contrib)
        image = lax.psum(frame, "shot") * scale
    return (out, image)


def solution(mesh):
    placed = (
        P("shot", None, None, "space", None, None),
        P("space", None, None),
        P("shot"),
        P("shot", "space", None),
        P("shot", "space"),
        P("shot", "space"),
        P("shot", None, "space"),
    )
    return jax.shard_map(
        body,
        mesh=mesh,
        in_specs=placed,
        out_specs=(P("shot", None, None, "space", None, None), P("space", None, None)),
        check_vma=False,
    )
```

```python
import functools

import jax
import jax.numpy as jnp
from jax import lax
from jax.experimental import pallas as pl
from jax.experimental.pallas import tpu as pltpu
from jax.sharding import PartitionSpec as P

STEPS = 4
RDEPTH = 4
EDGE = 4
LANES = 128
VMEM_LIMIT = 24 * 1024 * 1024
VMEM = pltpu.VMEM
SMEM = pltpu.SMEM
HBM = pltpu.HBM
BOTH = ((0, 1),)
SPLIT = ((1,), (0,))
HEAVY = 10**13


def params():
    return pltpu.CompilerParams(vmem_limit_bytes=VMEM_LIMIT)


def cost(weight=0):
    return pl.CostEstimate(flops=1 + weight, bytes_accessed=1, transcendentals=0)


def swap_pairs(value, first):
    count = lax.axis_size("space")
    routes = []
    for at in range(first, count - 1, 2):
        routes += [(at, at + 1), (at + 1, at)]
    return lax.ppermute(value, "space", routes)


def band(rows, centre):
    gap = jnp.abs(
        lax.broadcasted_iota(jnp.int32, (rows, rows), 0)
        - lax.broadcasted_iota(jnp.int32, (rows, rows), 1)
    )
    weights = jnp.where(gap == 0, centre, jnp.where(gap == 1, 16.0, jnp.where(gap == 2, -1.0, 0.0)))
    return weights.astype(jnp.bfloat16)


def mm(left, right, dims=((1,), (0,))):
    return lax.dot_general(left, right, (dims, ((), ())), preferred_element_type=jnp.float32)


def window_at(offset, model_y, rows_y):
    start = jnp.minimum(lax.div(offset, 8), (model_y - rows_y - 8) // 8) * 8
    return pl.multiple_of(start, 8), offset - start


def add_window(target_ref, lead, part, offset):
    rows_y = part.shape[0]
    start, gap = window_at(offset, target_ref.shape[-2], rows_y)
    moved = jnp.concatenate([part, jnp.zeros((8, part.shape[1]), part.dtype)], axis=0)
    at = lead + (pl.ds(start, rows_y + 8), slice(None))
    target_ref[at] = target_ref[at] + pltpu.roll(moved, gap, 0)


def is_odd():
    return lax.rem(lax.axis_index("space"), 2) == 1


def write_sends(field_ref, groups, send_refs):
    odd = is_odd()
    for at_group, group in enumerate(groups):
        send0_ref, send1_ref = send_refs[2 * at_group : 2 * at_group + 2]
        for place, comp in enumerate(group):
            for at in range(2):
                low = field_ref[comp, at]
                high = field_ref[comp, at + field_ref.shape[-3] - 2]
                send0_ref[place, at] = jnp.where(odd, low, high).astype(jnp.bfloat16)
                send1_ref[place, at] = jnp.where(odd, high, low).astype(jnp.bfloat16)


def pack_kernel(shot, field_ref, *refs):
    send0_ref, send1_ref, own_ref, sem = refs[-4:]
    load = pltpu.make_async_copy(field_ref.at[shot, 0], own_ref, sem)
    load.start()
    load.wait()
    write_sends(own_ref, BOTH, (send0_ref, send1_ref))


def pack_halo(wavefields, shot, after):
    _, _, comps, layers, rows_y, cells_z = wavefields.shape
    half = jax.ShapeDtypeStruct((comps, 2, rows_y, cells_z), jnp.bfloat16)
    return pl.pallas_call(
        functools.partial(pack_kernel, shot),
        in_specs=[pl.BlockSpec(memory_space=HBM)] + [pl.BlockSpec(memory_space=pl.ANY)] * len(after),
        out_specs=[pl.BlockSpec(memory_space=VMEM)] * 2,
        out_shape=[half, half],
        scratch_shapes=[
            pltpu.VMEM((comps, layers, rows_y, cells_z), jnp.float32),
            pltpu.SemaphoreType.DMA,
        ],
        compiler_params=params(),
        cost_estimate=cost(),
        name="pack_halo",
    )(pltpu.with_memory_space_constraint(wavefields, HBM), *after)


def pack_lines_kernel(cap, per_owner, ids_ref, lines_ref, after_ref, out_ref):
    shots, hold = ids_ref.shape
    total = shots * hold
    ids = jnp.concatenate([ids_ref[shot : shot + 1] for shot in range(shots)], axis=1)
    ids = ids.astype(jnp.float32)
    row_at = lax.broadcasted_iota(jnp.int32, (total, total), 0)
    col_at = lax.broadcasted_iota(jnp.int32, (total, total), 1)
    slot_at = lax.broadcasted_iota(jnp.int32, (1, total), 1)
    shot_of = jnp.zeros((1, total), jnp.float32)
    for shot in range(1, shots):
        shot_of = shot_of + (slot_at >= shot * hold).astype(jnp.float32)
    owner = jnp.floor((ids + 0.5) * (1.0 / per_owner))
    inside = ids - owner * per_owner
    used = ids >= 0.0
    key = jnp.where(used, owner * shots + shot_of, -1.0)
    wide_key = jnp.broadcast_to(key, (total, total))
    same = jnp.where(row_at == col_at, wide_key, 0.0)
    tall_key = jnp.sum(same, axis=1, keepdims=True)
    earlier_one = (tall_key == wide_key) & (row_at < col_at)
    rank = jnp.sum(earlier_one.astype(jnp.float32), axis=0, keepdims=True)
    target = jnp.where(used, key * cap + rank, -1.0)
    hot = jnp.where(row_at.astype(jnp.float32) == target, 1.0, 0.0)
    tags = jnp.sum(hot * (inside + 1.0), axis=1, keepdims=True)
    hot = hot.astype(jnp.bfloat16)
    cells_z = lines_ref.shape[2]
    rows = mm(hot[:, :hold], lines_ref[0])
    for shot in range(1, shots):
        rows = rows + mm(hot[:, shot * hold : (shot + 1) * hold], lines_ref[shot])
    out_ref[:, :cells_z] = rows.astype(jnp.bfloat16)
    out_ref[:, cells_z:] = jnp.broadcast_to(tags, (total, LANES)).astype(jnp.bfloat16)


def unpack_lines_kernel(cap, shots, per_owner, got_ref, out_ref):
    total = got_ref.shape[0]
    cells_z = out_ref.shape[1]
    tags = got_ref[:, cells_z : cells_z + LANES].astype(jnp.float32)[:, 0:1]
    row_at = lax.broadcasted_iota(jnp.int32, (total, 1), 0).astype(jnp.float32)
    block = jnp.floor((row_at + 0.5) * (1.0 / cap))
    shot_of = block - shots * jnp.floor((block + 0.5) * (1.0 / shots))
    target = jnp.where(tags > 0.5, tags - 1.0 + shot_of * per_owner, -1.0)
    line_at = lax.broadcasted_iota(jnp.int32, (total, shots * per_owner), 1).astype(jnp.float32)
    hot = jnp.where(line_at == target, 1.0, 0.0).astype(jnp.bfloat16)
    out_ref[...] = mm(hot, got_ref[:, :cells_z], ((0,), (0,)))


def pack_lines(strip_lines, strip_ids, per_owner, cap, after):
    shots, hold, cells_z = strip_lines.shape
    vmem = pl.BlockSpec(memory_space=VMEM)
    return pl.pallas_call(
        functools.partial(pack_lines_kernel, cap, per_owner),
        in_specs=[vmem, vmem, pl.BlockSpec(memory_space=pl.ANY)],
        out_specs=vmem,
        out_shape=jax.ShapeDtypeStruct((shots * hold, cells_z + LANES), jnp.bfloat16),
        compiler_params=params(),
        cost_estimate=cost(),
        name="pack_lines",
    )(strip_ids, strip_lines, after)


def deliver(message, cap, shots, per_owner):
    total, wide = message.shape
    message = message.reshape(lax.axis_size("space"), shots * cap, wide)
    got = lax.all_to_all(message, "space", 0, 0, tiled=False)
    return pl.pallas_call(
        functools.partial(unpack_lines_kernel, cap, shots, per_owner),
        out_shape=jax.ShapeDtypeStruct((shots * per_owner, wide - LANES), jnp.float32),
        compiler_params=params(),
        cost_estimate=cost(),
        name="unpack_lines",
    )(got.reshape(total, wide))


def split3(value):
    parts = []
    for _ in range(3):
        part = value.astype(jnp.bfloat16)
        parts.append(part)
        value = value - part.astype(jnp.float32)
    return parts


def take_lines(new_ref, saved_ref, shot, step, layer):
    _, layers, rows_y, _ = new_ref.shape
    base = ((shot * STEPS + step) * layers + layer) * EDGE
    new_ref[0, layer, 0:2, :] = saved_ref[base : base + 2, :]
    new_ref[0, layer, rows_y - 2 :, :] = saved_ref[base + 2 : base + 4, :]


def finish_kernel(shot, new_from, saved_ref, new_ref, send0_ref, send1_ref):
    del new_from
    for layer in range(new_ref.shape[1]):
        take_lines(new_ref, saved_ref, shot, 0, layer)
    write_sends(new_ref, BOTH, (send0_ref, send1_ref))


def finish_first(shot, new, saved):
    comps, _, rows_y, cells_z = new.shape
    half = jax.ShapeDtypeStruct((comps, 2, rows_y, cells_z), jnp.bfloat16)
    vmem = pl.BlockSpec(memory_space=VMEM)
    return pl.pallas_call(
        functools.partial(finish_kernel, shot),
        in_specs=[vmem, vmem],
        out_specs=[vmem] * 3,
        out_shape=[jax.ShapeDtypeStruct(new.shape, new.dtype), half, half],
        input_output_aliases={0: 0},
        compiler_params=params(),
        cost_estimate=cost(),
        name="finish_first_%d" % shot,
    )(new, saved)


def step_kernel(shot, step, comps, got_groups, send_groups, create, lines, waits, *refs):
    refs = list(refs)

    def take(count):
        taken, refs[:] = refs[:count], refs[count:]
        return taken

    first, last = step == 0, step == STEPS - 1
    with_image = 1 in comps
    now_ref, later_ref = take(2)
    got_of = {}
    for group in got_groups:
        got0_ref, got1_ref = take(2)
        for place, comp in enumerate(group):
            got_of[comp] = (got0_ref, got1_ref, place)
    [saved_ref] = take(1) if lines else [None]
    pos_ref, traces_ref = take(2) if with_image else (None, None)
    framing = last and with_image
    [offsets_ref] = take(1) if first or framing else [None]
    [speed_from] = take(1)
    [contrib_from] = take(1) if with_image and not first else [None]
    [frame_from] = take(1) if framing and not create else [None]
    take(waits)
    if last:
        take(0 if create else 1)
        [out_ref] = take(1)
    else:
        [new_ref] = take(1)
        send_refs = take(2 * len(send_groups))
    [contrib_ref] = take(1) if with_image else [None]
    [speed_out] = take(1) if first else [None]
    if last:
        new_ref, out_sems = take(2)
    loads = []
    if first:
        state_ref, load_sems = take(2)
        loads = [pltpu.make_async_copy(now_ref.at[shot], state_ref, load_sems.at[0])]
        now_ref, later_ref = state_ref.at[0], state_ref.at[1]
    elif step == 1:
        state_ref, load_sems = take(2)
        loads = [pltpu.make_async_copy(later_ref.at[shot, 0], state_ref, load_sems.at[0])]
        later_ref = state_ref
    for load in loads:
        load.start()
    layers, rows_y, cells_z = new_ref.shape[-3:]
    stores = []
    if last and with_image:
        stores.append(pltpu.make_async_copy(now_ref, out_ref.at[shot, 1], out_sems.at[0]))
        stores[0].start()
    odd = is_odd()
    across_z = band(cells_z, -90.0)
    across_y = band(rows_y, 0.0)
    if with_image:
        trace_row = traces_ref[shot, step : step + 1, :]
        lane_of = lax.broadcasted_iota(jnp.int32, (LANES, trace_row.shape[1]), 0)
        trace_parts = [
            jnp.where(lane_of == RDEPTH, part.astype(jnp.float32), 0.0).astype(jnp.bfloat16)
            for part in split3(trace_row)
        ]
        spots = pos_ref[shot : shot + 1, :]
        cell_of = lax.broadcasted_iota(jnp.int32, (rows_y, trace_row.shape[1]), 0)
    for load in loads:
        load.wait()

    for comp in comps:
        got0_ref, got1_ref, place = got_of[comp]

        def layer_of(at):
            if at < 0:
                both = (got1_ref[place, 2 + at], got0_ref[place, 2 + at])
            elif at >= layers:
                both = (got0_ref[place, at - layers], got1_ref[place, at - layers])
            else:
                return now_ref[comp, at]
            even_one, odd_one = (part.astype(jnp.float32) for part in both)
            return jnp.where(odd, odd_one, even_one)

        for layer in range(layers):
            if first and comp == comps[0]:
                start_y, gap = window_at(offsets_ref[shot], speed_from.shape[1], rows_y)
                speed = speed_from[layer, pl.ds(start_y, rows_y + 8), :]
                speed = pltpu.roll(speed, lax.rem(rows_y + 8 - gap, rows_y + 8), 0)[:rows_y]
                speed_out[layer] = speed
            else:
                speed = (speed_out if first else speed_from)[layer]
            here = layer_of(layer)
            high = here.astype(jnp.bfloat16)
            low = (here - high.astype(jnp.float32)).astype(jnp.bfloat16)
            growth = mm(high, across_z) + mm(low, across_z)
            growth = growth + (mm(across_y, high) + mm(across_y, low))
            growth = growth + 16.0 * (layer_of(layer - 1) + layer_of(layer + 1))
            growth = growth - (layer_of(layer - 2) + layer_of(layer + 2))
            growth = growth * (1.0 / 12.0)
            if comp == 1:
                hot = jnp.where(spots == cell_of + layer * rows_y, 1.0, 0.0).astype(jnp.bfloat16)
                plane = mm(hot, trace_parts[0], ((1,), (1,)))
                plane = plane + mm(hot, trace_parts[1], ((1,), (1,)))
                plane = plane + mm(hot, trace_parts[2], ((1,), (1,)))
                growth = jnp.concatenate(
                    [growth[:, :LANES] + plane, growth[:, LANES:]], axis=1
                )
            change = speed * growth
            new_ref[comp, layer] = 2.0 * here - later_ref[comp, layer] + change
            if comp == 1:
                term = now_ref[0, layer] * change
                if not first:
                    term = contrib_from[layer] + term
                if framing:
                    if create:
                        contrib_ref[layer] = jnp.zeros_like(contrib_ref[layer])
                    else:
                        contrib_ref[layer] = frame_from[layer]
                    add_window(contrib_ref, (layer,), term, offsets_ref[shot])
                else:
                    contrib_ref[layer] = term
            elif lines:
                take_lines(new_ref, saved_ref, shot, step, layer)
        if last:
            stores.append(
                pltpu.make_async_copy(
                    new_ref.at[comp], out_ref.at[shot, 0, comp], out_sems.at[1 + comp]
                )
            )
            stores[-1].start()
    for store in stores:
        store.wait()
    if not last:
        write_sends(new_ref, send_groups, send_refs)


def one_step(
    shot, step, comps, got_groups, send_groups,
    wavefields, offsets, now, later, got, saved, pos, traces, speed, contrib, frame, out, after, heavy, model_y,
):
    first, last = step == 0, step == STEPS - 1
    with_image = 1 in comps
    shots = wavefields.shape[0]
    both, layers, rows_y, cells_z = wavefields.shape[2:]
    vmem, hbm = pl.BlockSpec(memory_space=VMEM), pl.BlockSpec(memory_space=HBM)
    state = jax.ShapeDtypeStruct((both, layers, rows_y, cells_z), jnp.float32)
    image = jax.ShapeDtypeStruct((layers, rows_y, cells_z), jnp.float32)
    aliases = {}
    scratch = []
    args = [
        pltpu.with_memory_space_constraint(field, HBM) if field is wavefields else field
        for field in (now, later)
    ]
    specs = [hbm if first else vmem, hbm if step < 2 else vmem]
    args += [value for pair in got for value in pair]
    specs += [vmem] * (2 * len(got))
    lines = saved is not None and 0 in comps
    if lines:
        args.append(saved)
        specs.append(vmem)
    if with_image:
        args += [pos, traces]
        specs += [vmem, vmem]
    framing = last and with_image
    if first or framing:
        args.append(offsets)
        specs.append(pl.BlockSpec(memory_space=SMEM))
    args.append(speed)
    specs.append(vmem)
    if with_image and not first:
        args.append(contrib)
        specs.append(vmem)
    if framing and out is not None:
        args.append(frame)
        specs.append(vmem)
    args += after
    specs += [pl.BlockSpec(memory_space=pl.ANY)] * len(after)
    if last:
        if out is not None:
            aliases[len(args)] = 0
            args.append(out)
            specs.append(hbm)
        outs = [jax.ShapeDtypeStruct((shots, 2) + state.shape, jnp.float32)]
        out_specs = [hbm]
        scratch = [pltpu.VMEM(state.shape, jnp.float32), pltpu.SemaphoreType.DMA((3,))]
    else:
        outs = [state]
        for group in send_groups:
            half = jax.ShapeDtypeStruct((len(group), 2, rows_y, cells_z), jnp.bfloat16)
            outs += [half, half]
        out_specs = [vmem] * len(outs)
    if framing:
        outs.append(jax.ShapeDtypeStruct((layers, model_y, cells_z), jnp.float32))
        out_specs.append(vmem)
    elif with_image:
        outs.append(image)
        out_specs.append(vmem)
    if first:
        outs.append(image)
        out_specs.append(vmem)
    if step < 2:
        lead = (2,) if first else ()
        scratch = [pltpu.VMEM(lead + state.shape, jnp.float32), pltpu.SemaphoreType.DMA((1,))]
    return pl.pallas_call(
        functools.partial(
            step_kernel, shot, step, comps, got_groups, send_groups, out is None, lines, len(after)
        ),
        in_specs=specs,
        out_specs=out_specs,
        out_shape=outs,
        scratch_shapes=scratch,
        input_output_aliases=aliases,
        compiler_params=params(),
        cost_estimate=cost(HEAVY if heavy else 0),
        name="step_%d_shot_%d" % (step, shot),
    )(*args)


def sum_kernel(scale, own_ref, other_ref, *refs):
    refs[-1][...] = (own_ref[...] + other_ref[...]) * scale


def sum_frames(own, other, scale, after):
    vmem, hbm = pl.BlockSpec(memory_space=VMEM), pl.BlockSpec(memory_space=HBM)
    return pl.pallas_call(
        functools.partial(sum_kernel, scale),
        in_specs=[vmem, vmem, hbm],
        out_specs=vmem,
        out_shape=jax.ShapeDtypeStruct(own.shape, jnp.float32),
        compiler_params=params(),
        cost_estimate=cost(),
        name="sum_frames",
    )(own, other, pltpu.with_memory_space_constraint(after, HBM))


def body(wavefields, courant, offsets, strip_lines, strip_ids, receiver_pos, traces):
    shots = wavefields.shape[0]
    layers = wavefields.shape[3]
    cells_z = wavefields.shape[5]
    model_y = courant.shape[1]
    per_owner = STEPS * EDGE * layers
    shot_devices = lax.axis_size("shot")
    scale = 1.0 / (shots * shot_devices)
    cap = strip_lines.shape[1] // lax.axis_size("space")

    def exchange(sends):
        return [
            (swap_pairs(sends[at], 0), swap_pairs(sends[at + 1], 1)) for at in range(0, len(sends), 2)
        ]

    sends = pack_halo(wavefields, 0, [])
    got = [exchange(sends)]
    message = pack_lines(strip_lines, strip_ids, per_owner, cap, sends[0])
    saved = deliver(message, cap, shots, per_owner)
    for shot in range(1, shots):
        got.append(exchange(pack_halo(wavefields, shot, [message])))
    groups = [BOTH] * shots
    now = [wavefields] * shots
    later = [wavefields] * shots
    contrib = [None] * shots
    speed = [courant] * shots
    out = None
    frame = None
    after = []
    for step in range(STEPS):
        for shot in range(shots):
            split = shot == shots - 1
            send_groups = SPLIT if split and step == STEPS - 2 else BOTH
            common = (wavefields, offsets, now[shot], later[shot])
            fixed = (receiver_pos, traces, speed[shot])
            if step < STEPS - 1:
                early = step == 0 and shot == 0
                made = one_step(
                    shot, step, BOTH[0], groups[shot], () if early else send_groups, *common,
                    got[shot], None if early else saved, *fixed, contrib[shot], None, None, after, early,
                    model_y,
                )
                later[shot], now[shot] = now[shot], made[0]
                if early:
                    made = [*finish_first(shot, made[0], saved), *made[1:]]
                    now[shot] = made[0]
                ends = 1 + 2 * len(send_groups)
                got[shot] = exchange(made[1:ends])
                groups[shot] = send_groups
                contrib[shot] = made[ends]
                if step == 0:
                    speed[shot] = made[ends + 1]
                after = [made[1]]
                continue
            for part, group in enumerate(groups[shot]):
                made = one_step(
                    shot, step, group, (group,), (), *common, got[shot][part : part + 1], saved,
                    *fixed, contrib[shot], frame, out, after, part > 0, model_y,
                )
                out = made[0]
                if 1 in group:
                    frame = made[1]
                    after = [frame]
    if shot_devices == 2:
        other = lax.ppermute(frame, "shot", [(0, 1), (1, 0)])
        image = sum_frames(frame, other, scale, out)
    else:
        image = lax.psum(frame, "shot") * scale
    return (out, image)


def solution(mesh):
    placed = (
        P("shot", None, None, "space", None, None),
        P("space", None, None),
        P("shot"),
        P("shot", "space", None),
        P("shot", "space"),
        P("shot", "space"),
        P("shot", None, "space"),
    )
    return jax.shard_map(
        body,
        mesh=mesh,
        in_specs=placed,
        out_specs=(P("shot", None, None, "space", None, None), P("space", None, None)),
        check_vma=False,
    )
```

```python
import functools

import jax
import jax.numpy as jnp
from jax import lax
from jax.experimental import pallas as pl
from jax.experimental.pallas import tpu as pltpu
from jax.sharding import PartitionSpec as P

STEPS = 4
RDEPTH = 4
EDGE = 4
LANES = 128
VMEM_LIMIT = 24 * 1024 * 1024
VMEM = pltpu.VMEM
SMEM = pltpu.SMEM
HBM = pltpu.HBM
BOTH = ((0, 1),)
SPLIT = ((1,), (0,))
HEAVY = 10**13


def params():
    return pltpu.CompilerParams(vmem_limit_bytes=VMEM_LIMIT)


def cost(weight=0):
    return pl.CostEstimate(flops=1 + weight, bytes_accessed=1, transcendentals=0)


def swap_pairs(value, first):
    count = lax.axis_size("space")
    routes = []
    for at in range(first, count - 1, 2):
        routes += [(at, at + 1), (at + 1, at)]
    return lax.ppermute(value, "space", routes)


def band(rows, centre):
    gap = jnp.abs(
        lax.broadcasted_iota(jnp.int32, (rows, rows), 0)
        - lax.broadcasted_iota(jnp.int32, (rows, rows), 1)
    )
    weights = jnp.where(gap == 0, centre, jnp.where(gap == 1, 16.0, jnp.where(gap == 2, -1.0, 0.0)))
    return weights.astype(jnp.bfloat16)


def mm(left, right, dims=((1,), (0,))):
    return lax.dot_general(left, right, (dims, ((), ())), preferred_element_type=jnp.float32)


def window_at(offset, model_y, rows_y):
    start = jnp.minimum(lax.div(offset, 8), (model_y - rows_y - 8) // 8) * 8
    return pl.multiple_of(start, 8), offset - start


def add_window(target_ref, lead, part, offset):
    rows_y = part.shape[0]
    start, gap = window_at(offset, target_ref.shape[-2], rows_y)
    moved = jnp.concatenate([part, jnp.zeros((8, part.shape[1]), part.dtype)], axis=0)
    at = lead + (pl.ds(start, rows_y + 8), slice(None))
    target_ref[at] = target_ref[at] + pltpu.roll(moved, gap, 0)


def is_odd():
    return lax.rem(lax.axis_index("space"), 2) == 1


def write_sends(field_ref, groups, send_refs):
    odd = is_odd()
    for at_group, group in enumerate(groups):
        send0_ref, send1_ref = send_refs[2 * at_group : 2 * at_group + 2]
        for place, comp in enumerate(group):
            for at in range(2):
                low = field_ref[comp, at]
                high = field_ref[comp, at + field_ref.shape[-3] - 2]
                send0_ref[place, at] = jnp.where(odd, low, high).astype(jnp.bfloat16)
                send1_ref[place, at] = jnp.where(odd, high, low).astype(jnp.bfloat16)


def pack_kernel(shot, field_ref, *refs):
    send0_ref, send1_ref, own_ref, sems = refs[-4:]
    comps = own_ref.shape[0]
    loads = [
        pltpu.make_async_copy(field_ref.at[shot, 0, comp], own_ref.at[comp], sems.at[comp])
        for comp in range(comps)
    ]
    for load in loads:
        load.start()
    for comp, load in enumerate(loads):
        load.wait()
        write_sends(own_ref, ((comp,),), (send0_ref.at[comp : comp + 1], send1_ref.at[comp : comp + 1]))


def pack_halo(wavefields, shot, after):
    _, _, comps, layers, rows_y, cells_z = wavefields.shape
    half = jax.ShapeDtypeStruct((comps, 2, rows_y, cells_z), jnp.bfloat16)
    return pl.pallas_call(
        functools.partial(pack_kernel, shot),
        in_specs=[pl.BlockSpec(memory_space=HBM)] + [pl.BlockSpec(memory_space=pl.ANY)] * len(after),
        out_specs=[pl.BlockSpec(memory_space=VMEM)] * 2,
        out_shape=[half, half],
        scratch_shapes=[
            pltpu.VMEM((comps, layers, rows_y, cells_z), jnp.float32),
            pltpu.SemaphoreType.DMA((comps,)),
        ],
        compiler_params=params(),
        cost_estimate=cost(),
        name="pack_halo",
    )(pltpu.with_memory_space_constraint(wavefields, HBM), *after)


def pack_lines_kernel(cap, per_owner, ids_ref, lines_ref, after_ref, out_ref):
    shots, hold = ids_ref.shape
    total = shots * hold
    ids = jnp.concatenate([ids_ref[shot : shot + 1] for shot in range(shots)], axis=1)
    ids = ids.astype(jnp.float32)
    row_at = lax.broadcasted_iota(jnp.int32, (total, total), 0)
    col_at = lax.broadcasted_iota(jnp.int32, (total, total), 1)
    slot_at = lax.broadcasted_iota(jnp.int32, (1, total), 1)
    shot_of = jnp.zeros((1, total), jnp.float32)
    for shot in range(1, shots):
        shot_of = shot_of + (slot_at >= shot * hold).astype(jnp.float32)
    owner = jnp.floor((ids + 0.5) * (1.0 / per_owner))
    inside = ids - owner * per_owner
    used = ids >= 0.0
    key = jnp.where(used, owner * shots + shot_of, -1.0)
    wide_key = jnp.broadcast_to(key, (total, total))
    same = jnp.where(row_at == col_at, wide_key, 0.0)
    tall_key = jnp.sum(same, axis=1, keepdims=True)
    earlier_one = (tall_key == wide_key) & (row_at < col_at)
    rank = jnp.sum(earlier_one.astype(jnp.float32), axis=0, keepdims=True)
    target = jnp.where(used, key * cap + rank, -1.0)
    hot = jnp.where(row_at.astype(jnp.float32) == target, 1.0, 0.0)
    tags = jnp.sum(hot * (inside + 1.0), axis=1, keepdims=True)
    hot = hot.astype(jnp.bfloat16)
    cells_z = lines_ref.shape[2]
    rows = mm(hot[:, :hold], lines_ref[0])
    for shot in range(1, shots):
        rows = rows + mm(hot[:, shot * hold : (shot + 1) * hold], lines_ref[shot])
    out_ref[:, :cells_z] = rows.astype(jnp.bfloat16)
    out_ref[:, cells_z:] = jnp.broadcast_to(tags, (total, LANES)).astype(jnp.bfloat16)


def unpack_lines_kernel(cap, shots, per_owner, got_ref, out_ref):
    total = got_ref.shape[0]
    cells_z = out_ref.shape[1]
    tags = got_ref[:, cells_z : cells_z + LANES].astype(jnp.float32)[:, 0:1]
    row_at = lax.broadcasted_iota(jnp.int32, (total, 1), 0).astype(jnp.float32)
    block = jnp.floor((row_at + 0.5) * (1.0 / cap))
    shot_of = block - shots * jnp.floor((block + 0.5) * (1.0 / shots))
    target = jnp.where(tags > 0.5, tags - 1.0 + shot_of * per_owner, -1.0)
    line_at = lax.broadcasted_iota(jnp.int32, (total, shots * per_owner), 1).astype(jnp.float32)
    hot = jnp.where(line_at == target, 1.0, 0.0).astype(jnp.bfloat16)
    out_ref[...] = mm(hot, got_ref[:, :cells_z], ((0,), (0,)))


def pack_lines(strip_lines, strip_ids, per_owner, cap, after):
    shots, hold, cells_z = strip_lines.shape
    vmem = pl.BlockSpec(memory_space=VMEM)
    return pl.pallas_call(
        functools.partial(pack_lines_kernel, cap, per_owner),
        in_specs=[vmem, vmem, pl.BlockSpec(memory_space=pl.ANY)],
        out_specs=vmem,
        out_shape=jax.ShapeDtypeStruct((shots * hold, cells_z + LANES), jnp.bfloat16),
        compiler_params=params(),
        cost_estimate=cost(),
        name="pack_lines",
    )(strip_ids, strip_lines, after)


def deliver(message, cap, shots, per_owner):
    total, wide = message.shape
    message = message.reshape(lax.axis_size("space"), shots * cap, wide)
    got = lax.all_to_all(message, "space", 0, 0, tiled=False)
    return pl.pallas_call(
        functools.partial(unpack_lines_kernel, cap, shots, per_owner),
        out_shape=jax.ShapeDtypeStruct((shots * per_owner, wide - LANES), jnp.float32),
        compiler_params=params(),
        cost_estimate=cost(),
        name="unpack_lines",
    )(got.reshape(total, wide))


def split3(value):
    parts = []
    for _ in range(3):
        part = value.astype(jnp.bfloat16)
        parts.append(part)
        value = value - part.astype(jnp.float32)
    return parts


def take_lines(new_ref, saved_ref, shot, step, layer):
    _, layers, rows_y, _ = new_ref.shape
    base = ((shot * STEPS + step) * layers + layer) * EDGE
    new_ref[0, layer, 0:2, :] = saved_ref[base : base + 2, :]
    new_ref[0, layer, rows_y - 2 :, :] = saved_ref[base + 2 : base + 4, :]


def finish_kernel(shot, new_from, saved_ref, new_ref, send0_ref, send1_ref):
    del new_from
    for layer in range(new_ref.shape[1]):
        take_lines(new_ref, saved_ref, shot, 0, layer)
    write_sends(new_ref, BOTH, (send0_ref, send1_ref))


def finish_first(shot, new, saved):
    comps, _, rows_y, cells_z = new.shape
    half = jax.ShapeDtypeStruct((comps, 2, rows_y, cells_z), jnp.bfloat16)
    vmem = pl.BlockSpec(memory_space=VMEM)
    return pl.pallas_call(
        functools.partial(finish_kernel, shot),
        in_specs=[vmem, vmem],
        out_specs=[vmem] * 3,
        out_shape=[jax.ShapeDtypeStruct(new.shape, new.dtype), half, half],
        input_output_aliases={0: 0},
        compiler_params=params(),
        cost_estimate=cost(),
        name="finish_first_%d" % shot,
    )(new, saved)


def step_kernel(shot, step, comps, got_groups, send_groups, create, framed, lines, waits, keeps, *refs):
    refs = list(refs)

    def take(count):
        taken, refs[:] = refs[:count], refs[count:]
        return taken

    first, last = step == 0, step == STEPS - 1
    with_image = 1 in comps
    now_ref, later_ref = take(2)
    got_of = {}
    for group in got_groups:
        got0_ref, got1_ref = take(2)
        for place, comp in enumerate(group):
            got_of[comp] = (got0_ref, got1_ref, place)
    [saved_ref] = take(1) if lines else [None]
    pos_ref, traces_ref = take(2) if with_image else (None, None)
    framing = last and with_image
    [offsets_ref] = take(1) if first or framing else [None]
    [speed_from] = take(1)
    [contrib_from] = take(1) if with_image and not first else [None]
    [frame_from] = take(1) if framing and framed else [None]
    keep_refs = take(len(keeps))
    held = last and comps == (1,)
    [field_from] = take(1) if last and comps == (0,) else [None]
    take(waits)
    if held:
        [field_ref] = take(1)
    elif last:
        take(0 if create else 1)
        [out_ref] = take(1)
    else:
        [new_ref] = take(1)
        send_refs = take(2 * len(send_groups))
    [contrib_ref] = take(1) if with_image else [None]
    [speed_out] = take(1) if first else [None]
    if last and not held:
        new_ref, out_sems = take(2)
    loads = []
    if first:
        state_ref, load_sems = take(2)
        loads = [pltpu.make_async_copy(now_ref.at[shot], state_ref, load_sems.at[0])]
        now_ref, later_ref = state_ref.at[0], state_ref.at[1]
    elif step == 1:
        state_ref, load_sems = take(2)
        loads = [pltpu.make_async_copy(later_ref.at[shot, 0], state_ref, load_sems.at[0])]
        later_ref = state_ref
    for load in loads:
        load.start()
    layers, rows_y, cells_z = (field_ref if held else new_ref).shape[-3:]
    stores = []

    def store(source_ref, target_ref):
        stores.append(pltpu.make_async_copy(source_ref, target_ref, out_sems.at[len(stores)]))
        stores[-1].start()

    for keep, keep_ref in zip(keeps, keep_refs):
        store(keep_ref, out_ref.at[keep, 1])
    if field_from is not None:
        store(field_from, out_ref.at[shot, 0, 1])
    odd = is_odd()
    across_z = band(cells_z, -90.0)
    across_y = band(rows_y, 0.0)
    if with_image:
        trace_row = traces_ref[shot, step : step + 1, :]
        lane_of = lax.broadcasted_iota(jnp.int32, (LANES, trace_row.shape[1]), 0)
        trace_parts = [
            jnp.where(lane_of == RDEPTH, part.astype(jnp.float32), 0.0).astype(jnp.bfloat16)
            for part in split3(trace_row)
        ]
        spots = pos_ref[shot : shot + 1, :]
        cell_of = lax.broadcasted_iota(jnp.int32, (rows_y, trace_row.shape[1]), 0)
    for load in loads:
        load.wait()

    for comp in comps:
        got0_ref, got1_ref, place = got_of[comp]

        def layer_of(at):
            if at < 0:
                both = (got1_ref[place, 2 + at], got0_ref[place, 2 + at])
            elif at >= layers:
                both = (got0_ref[place, at - layers], got1_ref[place, at - layers])
            else:
                return now_ref[comp, at]
            even_one, odd_one = (part.astype(jnp.float32) for part in both)
            return jnp.where(odd, odd_one, even_one)

        for layer in range(layers):
            if first and comp == comps[0]:
                start_y, gap = window_at(offsets_ref[shot], speed_from.shape[1], rows_y)
                speed = speed_from[layer, pl.ds(start_y, rows_y + 8), :]
                speed = pltpu.roll(speed, lax.rem(rows_y + 8 - gap, rows_y + 8), 0)[:rows_y]
                speed_out[layer] = speed
            else:
                speed = (speed_out if first else speed_from)[layer]
            here = layer_of(layer)
            high = here.astype(jnp.bfloat16)
            low = (here - high.astype(jnp.float32)).astype(jnp.bfloat16)
            growth = mm(high, across_z) + mm(low, across_z)
            growth = growth + (mm(across_y, high) + mm(across_y, low))
            growth = growth + 16.0 * (layer_of(layer - 1) + layer_of(layer + 1))
            growth = growth - (layer_of(layer - 2) + layer_of(layer + 2))
            growth = growth * (1.0 / 12.0)
            if comp == 1:
                hot = jnp.where(spots == cell_of + layer * rows_y, 1.0, 0.0).astype(jnp.bfloat16)
                plane = mm(hot, trace_parts[0], ((1,), (1,)))
                plane = plane + mm(hot, trace_parts[1], ((1,), (1,)))
                plane = plane + mm(hot, trace_parts[2], ((1,), (1,)))
                growth = jnp.concatenate(
                    [growth[:, :LANES] + plane, growth[:, LANES:]], axis=1
                )
            change = speed * growth
            moved = 2.0 * here - later_ref[comp, layer] + change
            if held:
                field_ref[layer] = moved
            else:
                new_ref[comp, layer] = moved
            if comp == 1:
                term = now_ref[0, layer] * change
                if not first:
                    term = contrib_from[layer] + term
                if framing:
                    if not framed:
                        contrib_ref[layer] = jnp.zeros_like(contrib_ref[layer])
                    else:
                        contrib_ref[layer] = frame_from[layer]
                    add_window(contrib_ref, (layer,), term, offsets_ref[shot])
                else:
                    contrib_ref[layer] = term
            elif lines:
                take_lines(new_ref, saved_ref, shot, step, layer)
            if last and not held:
                store(new_ref.at[comp, layer], out_ref.at[shot, 0, comp, layer])
    for started in stores:
        started.wait()
    if not last:
        write_sends(new_ref, send_groups, send_refs)


def one_step(
    shot, step, comps, got_groups, send_groups,
    wavefields, offsets, now, later, got, saved, pos, traces, speed, contrib, frame, out, after, heavy, model_y, keeps=(), field=None,
):
    first, last = step == 0, step == STEPS - 1
    with_image = 1 in comps
    shots = wavefields.shape[0]
    both, layers, rows_y, cells_z = wavefields.shape[2:]
    vmem, hbm = pl.BlockSpec(memory_space=VMEM), pl.BlockSpec(memory_space=HBM)
    state = jax.ShapeDtypeStruct((both, layers, rows_y, cells_z), jnp.float32)
    image = jax.ShapeDtypeStruct((layers, rows_y, cells_z), jnp.float32)
    aliases = {}
    scratch = []
    args = [
        pltpu.with_memory_space_constraint(field, HBM) if field is wavefields else field
        for field in (now, later)
    ]
    specs = [hbm if first else vmem, hbm if step < 2 else vmem]
    args += [value for pair in got for value in pair]
    specs += [vmem] * (2 * len(got))
    lines = saved is not None and 0 in comps
    if lines:
        args.append(saved)
        specs.append(vmem)
    if with_image:
        args += [pos, traces]
        specs += [vmem, vmem]
    framing = last and with_image
    if first or framing:
        args.append(offsets)
        specs.append(pl.BlockSpec(memory_space=SMEM))
    args.append(speed)
    specs.append(vmem)
    if with_image and not first:
        args.append(contrib)
        specs.append(vmem)
    if framing and frame is not None:
        args.append(frame)
        specs.append(vmem)
    args += [value for _, value in keeps]
    specs += [vmem] * len(keeps)
    held = last and comps == (1,)
    if last and comps == (0,):
        args.append(field)
        specs.append(vmem)
    args += after
    specs += [pl.BlockSpec(memory_space=pl.ANY)] * len(after)
    if held:
        outs = [image]
        out_specs = [vmem]
    elif last:
        if out is not None:
            aliases[len(args)] = 0
            args.append(out)
            specs.append(hbm)
        outs = [jax.ShapeDtypeStruct((shots, 2) + state.shape, jnp.float32)]
        out_specs = [hbm]
        scratch = [
            pltpu.VMEM(state.shape, jnp.float32),
            pltpu.SemaphoreType.DMA((1 + len(keeps) + both * layers,)),
        ]
    else:
        outs = [state]
        for group in send_groups:
            half = jax.ShapeDtypeStruct((len(group), 2, rows_y, cells_z), jnp.bfloat16)
            outs += [half, half]
        out_specs = [vmem] * len(outs)
    if framing:
        outs.append(jax.ShapeDtypeStruct((layers, model_y, cells_z), jnp.float32))
        out_specs.append(vmem)
    elif with_image:
        outs.append(image)
        out_specs.append(vmem)
    if first:
        outs.append(image)
        out_specs.append(vmem)
    if step < 2:
        lead = (2,) if first else ()
        scratch = [pltpu.VMEM(lead + state.shape, jnp.float32), pltpu.SemaphoreType.DMA((1,))]
    return pl.pallas_call(
        functools.partial(
            step_kernel, shot, step, comps, got_groups, send_groups, out is None, frame is not None,
            lines, len(after), tuple(keep for keep, _ in keeps),
        ),
        in_specs=specs,
        out_specs=out_specs,
        out_shape=outs,
        scratch_shapes=scratch,
        input_output_aliases=aliases,
        compiler_params=params(),
        cost_estimate=cost(HEAVY if heavy else 0),
        name="step_%d_shot_%d" % (step, shot),
    )(*args)


def sum_kernel(scale, own_ref, other_ref, *refs):
    refs[-1][...] = (own_ref[...] + other_ref[...]) * scale


def sum_frames(own, other, scale, after):
    layers, model_y, cells_z = own.shape
    block = pl.BlockSpec((1, model_y, cells_z), lambda i: (i, 0, 0))
    return pl.pallas_call(
        functools.partial(sum_kernel, scale),
        grid=(layers,),
        in_specs=[block, block, pl.BlockSpec(memory_space=HBM)],
        out_specs=block,
        out_shape=jax.ShapeDtypeStruct(own.shape, jnp.float32),
        compiler_params=params(),
        cost_estimate=cost(),
        name="sum_frames",
    )(own, other, pltpu.with_memory_space_constraint(after, HBM))


def body(wavefields, courant, offsets, strip_lines, strip_ids, receiver_pos, traces):
    shots = wavefields.shape[0]
    layers = wavefields.shape[3]
    cells_z = wavefields.shape[5]
    model_y = courant.shape[1]
    per_owner = STEPS * EDGE * layers
    shot_devices = lax.axis_size("shot")
    scale = 1.0 / (shots * shot_devices)
    cap = strip_lines.shape[1] // lax.axis_size("space")

    def exchange(sends):
        return [
            (swap_pairs(sends[at], 0), swap_pairs(sends[at + 1], 1)) for at in range(0, len(sends), 2)
        ]

    sends = pack_halo(wavefields, 0, [])
    got = [exchange(sends)]
    message = pack_lines(strip_lines, strip_ids, per_owner, cap, sends[0])
    saved = deliver(message, cap, shots, per_owner)
    for shot in range(1, shots):
        got.append(exchange(pack_halo(wavefields, shot, [message])))
    groups = [BOTH] * shots
    now = [wavefields] * shots
    later = [wavefields] * shots
    contrib = [None] * shots
    speed = [courant] * shots
    out = None
    frame = None
    after = []
    for step in range(STEPS):
        for shot in range(shots):
            split = shot == shots - 1
            send_groups = SPLIT if split and step == STEPS - 2 else BOTH
            common = (wavefields, offsets, now[shot], later[shot])
            fixed = (receiver_pos, traces, speed[shot])
            if step < STEPS - 1:
                early = step == 0 and shot == 0
                made = one_step(
                    shot, step, BOTH[0], groups[shot], () if early else send_groups, *common,
                    got[shot], None if early else saved, *fixed, contrib[shot], None, None, after, early,
                    model_y,
                )
                later[shot], now[shot] = now[shot], made[0]
                if early:
                    made = [*finish_first(shot, made[0], saved), *made[1:]]
                    now[shot] = made[0]
                ends = 1 + 2 * len(send_groups)
                got[shot] = exchange(made[1:ends])
                groups[shot] = send_groups
                contrib[shot] = made[ends]
                if step == 0:
                    speed[shot] = made[ends + 1]
                after = [made[1]]
                continue
            keeps = [] if split and shots > 1 else [(shot, now[shot])]
            if shot == 0 and shots > 1:
                keeps.append((shots - 1, now[shots - 1]))
            field = None
            for group in groups[shot]:
                made = one_step(
                    shot, step, group, (group,), (), *common, got[shot][:1], saved, *fixed,
                    contrib[shot], frame, out, after, group == (0,), model_y,
                    () if group == (1,) else keeps, field,
                )
                got[shot] = got[shot][1:]
                if group == (1,):
                    field = made[0]
                else:
                    out = made[0]
                if 1 in group:
                    frame = made[1]
                    after = [frame]
    if shot_devices == 2:
        other = lax.ppermute(frame, "shot", [(0, 1), (1, 0)])
        image = sum_frames(frame, other, scale, out)
    else:
        image = lax.psum(frame, "shot") * scale
    return (out, image)


def solution(mesh):
    placed = (
        P("shot", None, None, "space", None, None),
        P("space", None, None),
        P("shot"),
        P("shot", "space", None),
        P("shot", "space"),
        P("shot", "space"),
        P("shot", None, "space"),
    )
    return jax.shard_map(
        body,
        mesh=mesh,
        in_specs=placed,
        out_specs=(P("shot", None, None, "space", None, None), P("space", None, None)),
        check_vma=False,
    )
```

```python
import functools

import jax
import jax.numpy as jnp
from jax import lax
from jax.experimental import pallas as pl
from jax.experimental.pallas import tpu as pltpu
from jax.sharding import PartitionSpec as P

STEPS = 4
RDEPTH = 4
EDGE = 4
LANES = 128
VMEM_LIMIT = 24 * 1024 * 1024
VMEM = pltpu.VMEM
SMEM = pltpu.SMEM
HBM = pltpu.HBM
BOTH = ((0, 1),)
SPLIT = ((1,), (0,))
HEAVY = 10**13


def params():
    return pltpu.CompilerParams(vmem_limit_bytes=VMEM_LIMIT)


def cost(weight=0):
    return pl.CostEstimate(flops=1 + weight, bytes_accessed=1, transcendentals=0)


def swap_pairs(value, first):
    count = lax.axis_size("space")
    routes = []
    for at in range(first, count - 1, 2):
        routes += [(at, at + 1), (at + 1, at)]
    return lax.ppermute(value, "space", routes)


def band(rows, centre):
    gap = jnp.abs(
        lax.broadcasted_iota(jnp.int32, (rows, rows), 0)
        - lax.broadcasted_iota(jnp.int32, (rows, rows), 1)
    )
    weights = jnp.where(gap == 0, centre, jnp.where(gap == 1, 16.0, jnp.where(gap == 2, -1.0, 0.0)))
    return weights.astype(jnp.bfloat16)


def mm(left, right, dims=((1,), (0,))):
    return lax.dot_general(left, right, (dims, ((), ())), preferred_element_type=jnp.float32)


def window_at(offset, model_y, rows_y):
    start = jnp.minimum(lax.div(offset, 8), (model_y - rows_y - 8) // 8) * 8
    return pl.multiple_of(start, 8), offset - start


def add_window(target_ref, lead, part, offset):
    rows_y = part.shape[0]
    start, gap = window_at(offset, target_ref.shape[-2], rows_y)
    moved = jnp.concatenate([part, jnp.zeros((8, part.shape[1]), part.dtype)], axis=0)
    at = lead + (pl.ds(start, rows_y + 8), slice(None))
    target_ref[at] = target_ref[at] + pltpu.roll(moved, gap, 0)


def is_odd():
    return lax.rem(lax.axis_index("space"), 2) == 1


def write_sends(field_ref, groups, send_refs):
    odd = is_odd()
    for at_group, group in enumerate(groups):
        send0_ref, send1_ref = send_refs[2 * at_group : 2 * at_group + 2]
        for place, comp in enumerate(group):
            for at in range(2):
                low = field_ref[comp, at]
                high = field_ref[comp, at + field_ref.shape[-3] - 2]
                send0_ref[place, at] = jnp.where(odd, low, high).astype(jnp.bfloat16)
                send1_ref[place, at] = jnp.where(odd, high, low).astype(jnp.bfloat16)


def pack_kernel(shot, field_ref, *refs):
    send0_ref, send1_ref, own_ref, sems = refs[-4:]
    comps = own_ref.shape[0]
    loads = [
        pltpu.make_async_copy(field_ref.at[shot, 0, comp], own_ref.at[comp], sems.at[comp])
        for comp in range(comps)
    ]
    for load in loads:
        load.start()
    for comp, load in enumerate(loads):
        load.wait()
        write_sends(own_ref, ((comp,),), (send0_ref.at[comp : comp + 1], send1_ref.at[comp : comp + 1]))


def pack_halo(wavefields, shot, after):
    _, _, comps, layers, rows_y, cells_z = wavefields.shape
    half = jax.ShapeDtypeStruct((comps, 2, rows_y, cells_z), jnp.bfloat16)
    return pl.pallas_call(
        functools.partial(pack_kernel, shot),
        in_specs=[pl.BlockSpec(memory_space=HBM)] + [pl.BlockSpec(memory_space=pl.ANY)] * len(after),
        out_specs=[pl.BlockSpec(memory_space=VMEM)] * 2,
        out_shape=[half, half],
        scratch_shapes=[
            pltpu.VMEM((comps, layers, rows_y, cells_z), jnp.float32),
            pltpu.SemaphoreType.DMA((comps,)),
        ],
        compiler_params=params(),
        cost_estimate=cost(),
        name="pack_halo",
    )(pltpu.with_memory_space_constraint(wavefields, HBM), *after)


def pack_lines_kernel(cap, per_owner, ids_ref, lines_ref, after_ref, out_ref):
    shots, hold = ids_ref.shape
    total = shots * hold
    ids = jnp.concatenate([ids_ref[shot : shot + 1] for shot in range(shots)], axis=1)
    ids = ids.astype(jnp.float32)
    row_at = lax.broadcasted_iota(jnp.int32, (total, total), 0)
    col_at = lax.broadcasted_iota(jnp.int32, (total, total), 1)
    slot_at = lax.broadcasted_iota(jnp.int32, (1, total), 1)
    shot_of = jnp.zeros((1, total), jnp.float32)
    for shot in range(1, shots):
        shot_of = shot_of + (slot_at >= shot * hold).astype(jnp.float32)
    owner = jnp.floor((ids + 0.5) * (1.0 / per_owner))
    inside = ids - owner * per_owner
    used = ids >= 0.0
    key = jnp.where(used, owner * shots + shot_of, -1.0)
    wide_key = jnp.broadcast_to(key, (total, total))
    same = jnp.where(row_at == col_at, wide_key, 0.0)
    tall_key = jnp.sum(same, axis=1, keepdims=True)
    earlier_one = (tall_key == wide_key) & (row_at < col_at)
    rank = jnp.sum(earlier_one.astype(jnp.float32), axis=0, keepdims=True)
    target = jnp.where(used, key * cap + rank, -1.0)
    hot = jnp.where(row_at.astype(jnp.float32) == target, 1.0, 0.0)
    tags = jnp.sum(hot * (inside + 1.0), axis=1, keepdims=True)
    hot = hot.astype(jnp.bfloat16)
    cells_z = lines_ref.shape[2]
    rows = mm(hot[:, :hold], lines_ref[0])
    for shot in range(1, shots):
        rows = rows + mm(hot[:, shot * hold : (shot + 1) * hold], lines_ref[shot])
    out_ref[:, :cells_z] = rows.astype(jnp.bfloat16)
    out_ref[:, cells_z:] = jnp.broadcast_to(tags, (total, LANES)).astype(jnp.bfloat16)


def unpack_lines_kernel(cap, shots, per_owner, got_ref, out_ref):
    total = got_ref.shape[0]
    cells_z = out_ref.shape[1]
    tags = got_ref[:, cells_z : cells_z + LANES].astype(jnp.float32)[:, 0:1]
    row_at = lax.broadcasted_iota(jnp.int32, (total, 1), 0).astype(jnp.float32)
    block = jnp.floor((row_at + 0.5) * (1.0 / cap))
    shot_of = block - shots * jnp.floor((block + 0.5) * (1.0 / shots))
    target = jnp.where(tags > 0.5, tags - 1.0 + shot_of * per_owner, -1.0)
    line_at = lax.broadcasted_iota(jnp.int32, (total, shots * per_owner), 1).astype(jnp.float32)
    hot = jnp.where(line_at == target, 1.0, 0.0).astype(jnp.bfloat16)
    out_ref[...] = mm(hot, got_ref[:, :cells_z], ((0,), (0,)))


def pack_lines(strip_lines, strip_ids, per_owner, cap, after):
    shots, hold, cells_z = strip_lines.shape
    vmem = pl.BlockSpec(memory_space=VMEM)
    return pl.pallas_call(
        functools.partial(pack_lines_kernel, cap, per_owner),
        in_specs=[vmem, vmem, pl.BlockSpec(memory_space=pl.ANY)],
        out_specs=vmem,
        out_shape=jax.ShapeDtypeStruct((shots * hold, cells_z + LANES), jnp.bfloat16),
        compiler_params=params(),
        cost_estimate=cost(),
        name="pack_lines",
    )(strip_ids, strip_lines, after)


def deliver(message, cap, shots, per_owner):
    total, wide = message.shape
    message = message.reshape(lax.axis_size("space"), shots * cap, wide)
    got = lax.all_to_all(message, "space", 0, 0, tiled=False)
    return pl.pallas_call(
        functools.partial(unpack_lines_kernel, cap, shots, per_owner),
        out_shape=jax.ShapeDtypeStruct((shots * per_owner, wide - LANES), jnp.float32),
        compiler_params=params(),
        cost_estimate=cost(),
        name="unpack_lines",
    )(got.reshape(total, wide))


def split3(value):
    parts = []
    for _ in range(3):
        part = value.astype(jnp.bfloat16)
        parts.append(part)
        value = value - part.astype(jnp.float32)
    return parts


def take_lines(new_ref, saved_ref, shot, step, layer):
    _, layers, rows_y, _ = new_ref.shape
    base = ((shot * STEPS + step) * layers + layer) * EDGE
    new_ref[0, layer, 0:2, :] = saved_ref[base : base + 2, :]
    new_ref[0, layer, rows_y - 2 :, :] = saved_ref[base + 2 : base + 4, :]


def finish_kernel(shot, new_from, saved_ref, new_ref, send0_ref, send1_ref):
    del new_from
    for layer in range(new_ref.shape[1]):
        take_lines(new_ref, saved_ref, shot, 0, layer)
    write_sends(new_ref, BOTH, (send0_ref, send1_ref))


def finish_first(shot, new, saved):
    comps, _, rows_y, cells_z = new.shape
    half = jax.ShapeDtypeStruct((comps, 2, rows_y, cells_z), jnp.bfloat16)
    vmem = pl.BlockSpec(memory_space=VMEM)
    return pl.pallas_call(
        functools.partial(finish_kernel, shot),
        in_specs=[vmem, vmem],
        out_specs=[vmem] * 3,
        out_shape=[jax.ShapeDtypeStruct(new.shape, new.dtype), half, half],
        input_output_aliases={0: 0},
        compiler_params=params(),
        cost_estimate=cost(),
        name="finish_first_%d" % shot,
    )(new, saved)


def step_kernel(shot, step, comps, got_groups, send_groups, create, framed, lines, waits, keeps, *refs):
    refs = list(refs)

    def take(count):
        taken, refs[:] = refs[:count], refs[count:]
        return taken

    first, last = step == 0, step == STEPS - 1
    with_image = 1 in comps
    now_ref, later_ref = take(2)
    got_of = {}
    for group in got_groups:
        got0_ref, got1_ref = take(2)
        for place, comp in enumerate(group):
            got_of[comp] = (got0_ref, got1_ref, place)
    [saved_ref] = take(1) if lines else [None]
    pos_ref, traces_ref = take(2) if with_image else (None, None)
    framing = last and with_image
    [offsets_ref] = take(1) if first or framing else [None]
    [speed_from] = take(1)
    [contrib_from] = take(1) if with_image and not first else [None]
    [frame_from] = take(1) if framing and framed else [None]
    keep_refs = take(len(keeps))
    held = last and comps == (1,)
    [field_from] = take(1) if last and comps == (0,) else [None]
    take(waits)
    if held:
        [field_ref] = take(1)
    elif last:
        take(0 if create else 1)
        [out_ref] = take(1)
    else:
        [new_ref] = take(1)
        send_refs = take(2 * len(send_groups))
    [contrib_ref] = take(1) if with_image else [None]
    [speed_out] = take(1) if first else [None]
    if last and not held:
        new_ref, out_sems = take(2)
    loads = []
    if first:
        state_ref, load_sems = take(2)
        loads = [pltpu.make_async_copy(now_ref.at[shot], state_ref, load_sems.at[0])]
        now_ref, later_ref = state_ref.at[0], state_ref.at[1]
    elif step == 1:
        state_ref, load_sems = take(2)
        loads = [pltpu.make_async_copy(later_ref.at[shot, 0], state_ref, load_sems.at[0])]
        later_ref = state_ref
    for load in loads:
        load.start()
    layers, rows_y, cells_z = (field_ref if held else new_ref).shape[-3:]
    stores = []

    def store(source_ref, target_ref):
        stores.append(pltpu.make_async_copy(source_ref, target_ref, out_sems.at[len(stores)]))
        stores[-1].start()

    for keep, keep_ref in zip(keeps, keep_refs):
        store(keep_ref, out_ref.at[keep, 1])
    if field_from is not None:
        store(field_from, out_ref.at[shot, 0, 1])
    odd = is_odd()
    across_z = band(cells_z, -90.0)
    across_y = band(rows_y, 0.0)
    if with_image:
        trace_row = traces_ref[shot, step : step + 1, :]
        lane_of = lax.broadcasted_iota(jnp.int32, (LANES, trace_row.shape[1]), 0)
        trace_parts = [
            jnp.where(lane_of == RDEPTH, part.astype(jnp.float32), 0.0).astype(jnp.bfloat16)
            for part in split3(trace_row)
        ]
        spots = pos_ref[shot : shot + 1, :]
        cell_of = lax.broadcasted_iota(jnp.int32, (rows_y, trace_row.shape[1]), 0)
    for load in loads:
        load.wait()

    for comp in comps:
        got0_ref, got1_ref, place = got_of[comp]

        def layer_of(at):
            if at < 0:
                both = (got1_ref[place, 2 + at], got0_ref[place, 2 + at])
            elif at >= layers:
                both = (got0_ref[place, at - layers], got1_ref[place, at - layers])
            else:
                return now_ref[comp, at]
            even_one, odd_one = (part.astype(jnp.float32) for part in both)
            return jnp.where(odd, odd_one, even_one)

        for layer in range(layers):
            if first and comp == comps[0]:
                start_y, gap = window_at(offsets_ref[shot], speed_from.shape[1], rows_y)
                speed = speed_from[layer, pl.ds(start_y, rows_y + 8), :]
                speed = pltpu.roll(speed, lax.rem(rows_y + 8 - gap, rows_y + 8), 0)[:rows_y]
                speed_out[layer] = speed
            else:
                speed = (speed_out if first else speed_from)[layer]
            here = layer_of(layer)
            high = here.astype(jnp.bfloat16)
            low = (here - high.astype(jnp.float32)).astype(jnp.bfloat16)
            growth = mm(high, across_z) + mm(low, across_z)
            growth = growth + (mm(across_y, high) + mm(across_y, low))
            growth = growth + 16.0 * (layer_of(layer - 1) + layer_of(layer + 1))
            growth = growth - (layer_of(layer - 2) + layer_of(layer + 2))
            growth = growth * (1.0 / 12.0)
            if comp == 1:
                hot = jnp.where(spots == cell_of + layer * rows_y, 1.0, 0.0).astype(jnp.bfloat16)
                plane = mm(hot, trace_parts[0], ((1,), (1,)))
                plane = plane + mm(hot, trace_parts[1], ((1,), (1,)))
                plane = plane + mm(hot, trace_parts[2], ((1,), (1,)))
                growth = jnp.concatenate(
                    [growth[:, :LANES] + plane, growth[:, LANES:]], axis=1
                )
            change = speed * growth
            moved = 2.0 * here - later_ref[comp, layer] + change
            if held:
                field_ref[layer] = moved
            else:
                new_ref[comp, layer] = moved
            if comp == 1:
                term = now_ref[0, layer] * change
                if not first:
                    term = contrib_from[layer] + term
                if framing:
                    if not framed:
                        contrib_ref[layer] = jnp.zeros_like(contrib_ref[layer])
                    else:
                        contrib_ref[layer] = frame_from[layer]
                    add_window(contrib_ref, (layer,), term, offsets_ref[shot])
                else:
                    contrib_ref[layer] = term
            elif lines:
                take_lines(new_ref, saved_ref, shot, step, layer)
            if last and not held:
                store(new_ref.at[comp, layer], out_ref.at[shot, 0, comp, layer])
    for started in stores:
        started.wait()
    if not last:
        write_sends(new_ref, send_groups, send_refs)


def one_step(
    shot, step, comps, got_groups, send_groups,
    wavefields, offsets, now, later, got, saved, pos, traces, speed, contrib, frame, out, after, heavy, model_y, keeps=(), field=None,
):
    first, last = step == 0, step == STEPS - 1
    with_image = 1 in comps
    shots = wavefields.shape[0]
    both, layers, rows_y, cells_z = wavefields.shape[2:]
    vmem, hbm = pl.BlockSpec(memory_space=VMEM), pl.BlockSpec(memory_space=HBM)
    state = jax.ShapeDtypeStruct((both, layers, rows_y, cells_z), jnp.float32)
    image = jax.ShapeDtypeStruct((layers, rows_y, cells_z), jnp.float32)
    aliases = {}
    scratch = []
    args = [
        pltpu.with_memory_space_constraint(field, HBM) if field is wavefields else field
        for field in (now, later)
    ]
    specs = [hbm if first else vmem, hbm if step < 2 else vmem]
    args += [value for pair in got for value in pair]
    specs += [vmem] * (2 * len(got))
    lines = saved is not None and 0 in comps
    if lines:
        args.append(saved)
        specs.append(vmem)
    if with_image:
        args += [pos, traces]
        specs += [vmem, vmem]
    framing = last and with_image
    if first or framing:
        args.append(offsets)
        specs.append(pl.BlockSpec(memory_space=SMEM))
    args.append(speed)
    specs.append(vmem)
    if with_image and not first:
        args.append(contrib)
        specs.append(vmem)
    if framing and frame is not None:
        args.append(frame)
        specs.append(vmem)
    args += [value for _, value in keeps]
    specs += [vmem] * len(keeps)
    held = last and comps == (1,)
    if last and comps == (0,):
        args.append(field)
        specs.append(vmem)
    args += after
    specs += [pl.BlockSpec(memory_space=pl.ANY)] * len(after)
    if held:
        outs = [image]
        out_specs = [vmem]
    elif last:
        if out is not None:
            aliases[len(args)] = 0
            args.append(out)
            specs.append(hbm)
        outs = [jax.ShapeDtypeStruct((shots, 2) + state.shape, jnp.float32)]
        out_specs = [hbm]
        scratch = [
            pltpu.VMEM(state.shape, jnp.float32),
            pltpu.SemaphoreType.DMA((1 + len(keeps) + both * layers,)),
        ]
    else:
        outs = [state]
        for group in send_groups:
            half = jax.ShapeDtypeStruct((len(group), 2, rows_y, cells_z), jnp.bfloat16)
            outs += [half, half]
        out_specs = [vmem] * len(outs)
    if framing:
        outs.append(jax.ShapeDtypeStruct((layers, model_y, cells_z), jnp.float32))
        out_specs.append(vmem)
    elif with_image:
        outs.append(image)
        out_specs.append(vmem)
    if first:
        outs.append(image)
        out_specs.append(vmem)
    if step < 2:
        lead = (2,) if first else ()
        scratch = [pltpu.VMEM(lead + state.shape, jnp.float32), pltpu.SemaphoreType.DMA((1,))]
    return pl.pallas_call(
        functools.partial(
            step_kernel, shot, step, comps, got_groups, send_groups, out is None, frame is not None,
            lines, len(after), tuple(keep for keep, _ in keeps),
        ),
        in_specs=specs,
        out_specs=out_specs,
        out_shape=outs,
        scratch_shapes=scratch,
        input_output_aliases=aliases,
        compiler_params=params(),
        cost_estimate=cost(HEAVY if heavy else 0),
        name="step_%d_shot_%d" % (step, shot),
    )(*args)


def sum_kernel(scale, own_ref, other_ref, after_ref, image_ref, sum_ref, sems):
    del after_ref
    stores = []
    for layer in range(sum_ref.shape[0]):
        sum_ref[layer] = (own_ref[layer] + other_ref[layer]) * scale
        stores.append(
            pltpu.make_async_copy(sum_ref.at[layer], image_ref.at[layer], sems.at[layer])
        )
        stores[-1].start()
    for started in stores:
        started.wait()


def sum_frames(own, other, scale, after):
    vmem, hbm = pl.BlockSpec(memory_space=VMEM), pl.BlockSpec(memory_space=HBM)
    return pl.pallas_call(
        functools.partial(sum_kernel, scale),
        in_specs=[vmem, vmem, hbm],
        out_specs=hbm,
        out_shape=jax.ShapeDtypeStruct(own.shape, jnp.float32),
        scratch_shapes=[
            pltpu.VMEM(own.shape, jnp.float32),
            pltpu.SemaphoreType.DMA((own.shape[0],)),
        ],
        compiler_params=params(),
        cost_estimate=cost(),
        name="sum_frames",
    )(own, other, pltpu.with_memory_space_constraint(after, HBM))


def body(wavefields, courant, offsets, strip_lines, strip_ids, receiver_pos, traces):
    shots = wavefields.shape[0]
    layers = wavefields.shape[3]
    cells_z = wavefields.shape[5]
    model_y = courant.shape[1]
    per_owner = STEPS * EDGE * layers
    shot_devices = lax.axis_size("shot")
    scale = 1.0 / (shots * shot_devices)
    cap = strip_lines.shape[1] // lax.axis_size("space")

    def exchange(sends):
        return [
            (swap_pairs(sends[at], 0), swap_pairs(sends[at + 1], 1)) for at in range(0, len(sends), 2)
        ]

    sends = pack_halo(wavefields, 0, [])
    got = [exchange(sends)]
    for shot in range(1, shots):
        sends = pack_halo(wavefields, shot, [sends[0]])
        got.append(exchange(sends))
    message = pack_lines(strip_lines, strip_ids, per_owner, cap, sends[0])
    saved = deliver(message, cap, shots, per_owner)
    groups = [BOTH] * shots
    now = [wavefields] * shots
    later = [wavefields] * shots
    contrib = [None] * shots
    speed = [courant] * shots
    out = None
    frame = None
    after = []
    for step in range(STEPS):
        for shot in range(shots):
            split = shot == shots - 1
            send_groups = SPLIT if split and step == STEPS - 2 else BOTH
            common = (wavefields, offsets, now[shot], later[shot])
            fixed = (receiver_pos, traces, speed[shot])
            if step < STEPS - 1:
                early = step == 0 and shot == 0
                made = one_step(
                    shot, step, BOTH[0], groups[shot], () if early else send_groups, *common,
                    got[shot], None if early else saved, *fixed, contrib[shot], None, None, after, early,
                    model_y,
                )
                later[shot], now[shot] = now[shot], made[0]
                if early:
                    made = [*finish_first(shot, made[0], saved), *made[1:]]
                    now[shot] = made[0]
                ends = 1 + 2 * len(send_groups)
                got[shot] = exchange(made[1:ends])
                groups[shot] = send_groups
                contrib[shot] = made[ends]
                if step == 0:
                    speed[shot] = made[ends + 1]
                after = [made[1]]
                continue
            keeps = [] if split and shots > 1 else [(shot, now[shot])]
            if shot == 0 and shots > 1:
                keeps.append((shots - 1, now[shots - 1]))
            field = None
            for group in groups[shot]:
                made = one_step(
                    shot, step, group, (group,), (), *common, got[shot][:1], saved, *fixed,
                    contrib[shot], frame, out, after, group == (0,), model_y,
                    () if group == (1,) else keeps, field,
                )
                got[shot] = got[shot][1:]
                if group == (1,):
                    field = made[0]
                else:
                    out = made[0]
                if 1 in group:
                    frame = made[1]
                    after = [frame]
    if shot_devices == 2:
        other = lax.ppermute(frame, "shot", [(0, 1), (1, 0)])
        image = sum_frames(frame, other, scale, out)
    else:
        image = lax.psum(frame, "shot") * scale
    return (out, image)


def solution(mesh):
    placed = (
        P("shot", None, None, "space", None, None),
        P("space", None, None),
        P("shot"),
        P("shot", "space", None),
        P("shot", "space"),
        P("shot", "space"),
        P("shot", None, "space"),
    )
    return jax.shard_map(
        body,
        mesh=mesh,
        in_specs=placed,
        out_specs=(P("shot", None, None, "space", None, None), P("space", None, None)),
        check_vma=False,
    )
```

```python
import functools

import jax
import jax.numpy as jnp
from jax import lax
from jax.experimental import pallas as pl
from jax.experimental.pallas import tpu as pltpu
from jax.sharding import PartitionSpec as P

STEPS = 4
RDEPTH = 4
EDGE = 4
LANES = 128
VMEM_LIMIT = 24 * 1024 * 1024
VMEM = pltpu.VMEM
SMEM = pltpu.SMEM
HBM = pltpu.HBM
BOTH = ((0, 1),)
SPLIT = ((1,), (0,))
HEAVY = 10**13


def params():
    return pltpu.CompilerParams(vmem_limit_bytes=VMEM_LIMIT)


def cost(weight=0):
    return pl.CostEstimate(flops=1 + weight, bytes_accessed=1, transcendentals=0)


def swap_pairs(value, first):
    count = lax.axis_size("space")
    routes = []
    for at in range(first, count - 1, 2):
        routes += [(at, at + 1), (at + 1, at)]
    return lax.ppermute(value, "space", routes)


def band(rows, centre):
    gap = jnp.abs(
        lax.broadcasted_iota(jnp.int32, (rows, rows), 0)
        - lax.broadcasted_iota(jnp.int32, (rows, rows), 1)
    )
    weights = jnp.where(gap == 0, centre, jnp.where(gap == 1, 16.0, jnp.where(gap == 2, -1.0, 0.0)))
    return weights.astype(jnp.bfloat16)


def mm(left, right, dims=((1,), (0,))):
    return lax.dot_general(left, right, (dims, ((), ())), preferred_element_type=jnp.float32)


def window_at(offset, model_y, rows_y):
    start = jnp.minimum(lax.div(offset, 8), (model_y - rows_y - 8) // 8) * 8
    return pl.multiple_of(start, 8), offset - start


def add_window(target_ref, layer, part, offset):
    rows_y, cells_z = part.shape
    groups = rows_y // 8
    start = pl.multiple_of(lax.div(offset, 8) * 8, 8)
    gap = lax.rem(offset, 8)
    turned = pltpu.roll(part.reshape(groups, 8, cells_z), gap, 1)
    before = lax.broadcasted_iota(jnp.int32, (8, cells_z), 0) < gap
    body = [jnp.where(before, 0.0, turned[0])]
    body += [jnp.where(before, turned[at - 1], turned[at]) for at in range(1, groups)]
    at = pl.ds(start, rows_y)
    target_ref[layer, at, :] = target_ref[layer, at, :] + jnp.concatenate(body, axis=0)

    @pl.when(gap > 0)
    def _():
        rest = pl.ds(pl.multiple_of(start + rows_y, 8), 8)
        target_ref[layer, rest, :] = target_ref[layer, rest, :] + jnp.where(before, turned[-1], 0.0)


def is_odd():
    return lax.rem(lax.axis_index("space"), 2) == 1


def write_sends(field_ref, groups, send_refs):
    odd = is_odd()
    for at_group, group in enumerate(groups):
        send0_ref, send1_ref = send_refs[2 * at_group : 2 * at_group + 2]
        for place, comp in enumerate(group):
            for at in range(2):
                low = field_ref[comp, at]
                high = field_ref[comp, at + field_ref.shape[-3] - 2]
                send0_ref[place, at] = jnp.where(odd, low, high).astype(jnp.bfloat16)
                send1_ref[place, at] = jnp.where(odd, high, low).astype(jnp.bfloat16)


def pack_kernel(shot, field_ref, *refs):
    send0_ref, send1_ref, own_ref, sems = refs[-4:]
    comps = own_ref.shape[0]
    loads = [
        pltpu.make_async_copy(field_ref.at[shot, 0, comp], own_ref.at[comp], sems.at[comp])
        for comp in range(comps)
    ]
    for load in loads:
        load.start()
    for comp, load in enumerate(loads):
        load.wait()
        write_sends(own_ref, ((comp,),), (send0_ref.at[comp : comp + 1], send1_ref.at[comp : comp + 1]))


def pack_halo(wavefields, shot, after):
    _, _, comps, layers, rows_y, cells_z = wavefields.shape
    half = jax.ShapeDtypeStruct((comps, 2, rows_y, cells_z), jnp.bfloat16)
    return pl.pallas_call(
        functools.partial(pack_kernel, shot),
        in_specs=[pl.BlockSpec(memory_space=HBM)] + [pl.BlockSpec(memory_space=pl.ANY)] * len(after),
        out_specs=[pl.BlockSpec(memory_space=VMEM)] * 2,
        out_shape=[half, half],
        scratch_shapes=[
            pltpu.VMEM((comps, layers, rows_y, cells_z), jnp.float32),
            pltpu.SemaphoreType.DMA((comps,)),
        ],
        compiler_params=params(),
        cost_estimate=cost(),
        name="pack_halo",
    )(pltpu.with_memory_space_constraint(wavefields, HBM), *after)


def pack_lines_kernel(cap, per_owner, ids_ref, lines_ref, after_ref, out_ref):
    shots, hold = ids_ref.shape
    total = shots * hold
    ids = jnp.concatenate([ids_ref[shot : shot + 1] for shot in range(shots)], axis=1)
    ids = ids.astype(jnp.float32)
    row_at = lax.broadcasted_iota(jnp.int32, (total, total), 0)
    col_at = lax.broadcasted_iota(jnp.int32, (total, total), 1)
    slot_at = lax.broadcasted_iota(jnp.int32, (1, total), 1)
    shot_of = jnp.zeros((1, total), jnp.float32)
    for shot in range(1, shots):
        shot_of = shot_of + (slot_at >= shot * hold).astype(jnp.float32)
    owner = jnp.floor((ids + 0.5) * (1.0 / per_owner))
    inside = ids - owner * per_owner
    used = ids >= 0.0
    key = jnp.where(used, owner * shots + shot_of, -1.0)
    wide_key = jnp.broadcast_to(key, (total, total))
    same = jnp.where(row_at == col_at, wide_key, 0.0)
    tall_key = jnp.sum(same, axis=1, keepdims=True)
    earlier_one = (tall_key == wide_key) & (row_at < col_at)
    rank = jnp.sum(earlier_one.astype(jnp.float32), axis=0, keepdims=True)
    target = jnp.where(used, key * cap + rank, -1.0)
    hot = jnp.where(row_at.astype(jnp.float32) == target, 1.0, 0.0)
    tags = jnp.sum(hot * (inside + 1.0), axis=1, keepdims=True)
    hot = hot.astype(jnp.bfloat16)
    cells_z = lines_ref.shape[2]
    rows = mm(hot[:, :hold], lines_ref[0])
    for shot in range(1, shots):
        rows = rows + mm(hot[:, shot * hold : (shot + 1) * hold], lines_ref[shot])
    out_ref[:, :cells_z] = rows.astype(jnp.bfloat16)
    out_ref[:, cells_z:] = jnp.broadcast_to(tags, (total, LANES)).astype(jnp.bfloat16)


def unpack_lines_kernel(cap, shots, per_owner, got_ref, out_ref):
    total = got_ref.shape[0]
    cells_z = out_ref.shape[1]
    tags = got_ref[:, cells_z : cells_z + LANES].astype(jnp.float32)[:, 0:1]
    row_at = lax.broadcasted_iota(jnp.int32, (total, 1), 0).astype(jnp.float32)
    block = jnp.floor((row_at + 0.5) * (1.0 / cap))
    shot_of = block - shots * jnp.floor((block + 0.5) * (1.0 / shots))
    target = jnp.where(tags > 0.5, tags - 1.0 + shot_of * per_owner, -1.0)
    line_at = lax.broadcasted_iota(jnp.int32, (total, shots * per_owner), 1).astype(jnp.float32)
    hot = jnp.where(line_at == target, 1.0, 0.0).astype(jnp.bfloat16)
    out_ref[...] = mm(hot, got_ref[:, :cells_z], ((0,), (0,)))


def pack_lines(strip_lines, strip_ids, per_owner, cap, after):
    shots, hold, cells_z = strip_lines.shape
    vmem = pl.BlockSpec(memory_space=VMEM)
    return pl.pallas_call(
        functools.partial(pack_lines_kernel, cap, per_owner),
        in_specs=[vmem, vmem, pl.BlockSpec(memory_space=pl.ANY)],
        out_specs=vmem,
        out_shape=jax.ShapeDtypeStruct((shots * hold, cells_z + LANES), jnp.bfloat16),
        compiler_params=params(),
        cost_estimate=cost(),
        name="pack_lines",
    )(strip_ids, strip_lines, after)


def deliver(message, cap, shots, per_owner):
    total, wide = message.shape
    message = message.reshape(lax.axis_size("space"), shots * cap, wide)
    got = lax.all_to_all(message, "space", 0, 0, tiled=False)
    return pl.pallas_call(
        functools.partial(unpack_lines_kernel, cap, shots, per_owner),
        out_shape=jax.ShapeDtypeStruct((shots * per_owner, wide - LANES), jnp.float32),
        compiler_params=params(),
        cost_estimate=cost(),
        name="unpack_lines",
    )(got.reshape(total, wide))


def split3(value):
    parts = []
    for _ in range(3):
        part = value.astype(jnp.bfloat16)
        parts.append(part)
        value = value - part.astype(jnp.float32)
    return parts


def take_lines(new_ref, saved_ref, shot, step, layer):
    _, layers, rows_y, _ = new_ref.shape
    base = ((shot * STEPS + step) * layers + layer) * EDGE
    new_ref[0, layer, 0:2, :] = saved_ref[base : base + 2, :]
    new_ref[0, layer, rows_y - 2 :, :] = saved_ref[base + 2 : base + 4, :]


def finish_kernel(shot, new_from, saved_ref, new_ref, send0_ref, send1_ref):
    del new_from
    for layer in range(new_ref.shape[1]):
        take_lines(new_ref, saved_ref, shot, 0, layer)
    write_sends(new_ref, BOTH, (send0_ref, send1_ref))


def finish_first(shot, new, saved):
    comps, _, rows_y, cells_z = new.shape
    half = jax.ShapeDtypeStruct((comps, 2, rows_y, cells_z), jnp.bfloat16)
    vmem = pl.BlockSpec(memory_space=VMEM)
    return pl.pallas_call(
        functools.partial(finish_kernel, shot),
        in_specs=[vmem, vmem],
        out_specs=[vmem] * 3,
        out_shape=[jax.ShapeDtypeStruct(new.shape, new.dtype), half, half],
        input_output_aliases={0: 0},
        compiler_params=params(),
        cost_estimate=cost(),
        name="finish_first_%d" % shot,
    )(new, saved)


def step_kernel(shot, step, comps, got_groups, send_groups, create, framed, lines, waits, keeps, *refs):
    refs = list(refs)

    def take(count):
        taken, refs[:] = refs[:count], refs[count:]
        return taken

    first, last = step == 0, step == STEPS - 1
    with_image = 1 in comps
    now_ref, later_ref = take(2)
    got_of = {}
    for group in got_groups:
        got0_ref, got1_ref = take(2)
        for place, comp in enumerate(group):
            got_of[comp] = (got0_ref, got1_ref, place)
    [saved_ref] = take(1) if lines else [None]
    pos_ref, traces_ref = take(2) if with_image else (None, None)
    framing = last and with_image
    [offsets_ref] = take(1) if first or framing else [None]
    [speed_from] = take(1)
    [contrib_from] = take(1) if with_image and not first else [None]
    [frame_from] = take(1) if framing and framed else [None]
    keep_refs = take(len(keeps))
    held = last and comps == (1,)
    [field_from] = take(1) if last and comps == (0,) else [None]
    take(waits)
    if held:
        [field_ref] = take(1)
    elif last:
        take(0 if create else 1)
        [out_ref] = take(1)
    else:
        [new_ref] = take(1)
        send_refs = take(2 * len(send_groups))
    [contrib_ref] = take(1) if with_image else [None]
    [speed_out] = take(1) if first else [None]
    if last and not held:
        new_ref, out_sems = take(2)
    loads = []
    if first:
        state_ref, load_sems = take(2)
        loads = [pltpu.make_async_copy(now_ref.at[shot], state_ref, load_sems.at[0])]
        now_ref, later_ref = state_ref.at[0], state_ref.at[1]
    elif step == 1:
        state_ref, load_sems = take(2)
        loads = [pltpu.make_async_copy(later_ref.at[shot, 0], state_ref, load_sems.at[0])]
        later_ref = state_ref
    for load in loads:
        load.start()
    layers, rows_y, cells_z = (field_ref if held else new_ref).shape[-3:]
    stores = []

    def store(source_ref, target_ref):
        stores.append(pltpu.make_async_copy(source_ref, target_ref, out_sems.at[len(stores)]))
        stores[-1].start()

    for keep, keep_ref in zip(keeps, keep_refs):
        store(keep_ref, out_ref.at[keep, 1])
    if field_from is not None:
        store(field_from, out_ref.at[shot, 0, 1])
    odd = is_odd()
    across_z = band(cells_z, -90.0)
    across_y = band(rows_y, 0.0)
    if with_image:
        trace_row = traces_ref[shot, step : step + 1, :]
        lane_of = lax.broadcasted_iota(jnp.int32, (LANES, trace_row.shape[1]), 0)
        trace_parts = [
            jnp.where(lane_of == RDEPTH, part.astype(jnp.float32), 0.0).astype(jnp.bfloat16)
            for part in split3(trace_row)
        ]
        spots = pos_ref[shot : shot + 1, :]
        cell_of = lax.broadcasted_iota(jnp.int32, (rows_y, trace_row.shape[1]), 0)
    for load in loads:
        load.wait()

    for comp in comps:
        got0_ref, got1_ref, place = got_of[comp]

        def layer_of(at):
            if at < 0:
                both = (got1_ref[place, 2 + at], got0_ref[place, 2 + at])
            elif at >= layers:
                both = (got0_ref[place, at - layers], got1_ref[place, at - layers])
            else:
                return now_ref[comp, at]
            even_one, odd_one = (part.astype(jnp.float32) for part in both)
            return jnp.where(odd, odd_one, even_one)

        for layer in range(layers):
            if first and comp == comps[0]:
                start_y, gap = window_at(offsets_ref[shot], speed_from.shape[1], rows_y)
                speed = speed_from[layer, pl.ds(start_y, rows_y + 8), :]
                speed = pltpu.roll(speed, lax.rem(rows_y + 8 - gap, rows_y + 8), 0)[:rows_y]
                speed_out[layer] = speed
            else:
                speed = (speed_out if first else speed_from)[layer]
            here = layer_of(layer)
            high = here.astype(jnp.bfloat16)
            low = (here - high.astype(jnp.float32)).astype(jnp.bfloat16)
            growth = mm(high, across_z) + mm(low, across_z)
            growth = growth + (mm(across_y, high) + mm(across_y, low))
            growth = growth + 16.0 * (layer_of(layer - 1) + layer_of(layer + 1))
            growth = growth - (layer_of(layer - 2) + layer_of(layer + 2))
            growth = growth * (1.0 / 12.0)
            if comp == 1:
                hot = jnp.where(spots == cell_of + layer * rows_y, 1.0, 0.0).astype(jnp.bfloat16)
                plane = mm(hot, trace_parts[0], ((1,), (1,)))
                plane = plane + mm(hot, trace_parts[1], ((1,), (1,)))
                plane = plane + mm(hot, trace_parts[2], ((1,), (1,)))
                growth = jnp.concatenate(
                    [growth[:, :LANES] + plane, growth[:, LANES:]], axis=1
                )
            change = speed * growth
            moved = 2.0 * here - later_ref[comp, layer] + change
            if held:
                field_ref[layer] = moved
            else:
                new_ref[comp, layer] = moved
            if comp == 1:
                term = now_ref[0, layer] * change
                if not first:
                    term = contrib_from[layer] + term
                if framing:
                    if not framed:
                        contrib_ref[layer] = jnp.zeros_like(contrib_ref[layer])
                    else:
                        contrib_ref[layer] = frame_from[layer]
                    add_window(contrib_ref, layer, term, offsets_ref[shot])
                else:
                    contrib_ref[layer] = term
            elif lines:
                take_lines(new_ref, saved_ref, shot, step, layer)
            if last and not held:
                store(new_ref.at[comp, layer], out_ref.at[shot, 0, comp, layer])
    for started in stores:
        started.wait()
    if not last:
        write_sends(new_ref, send_groups, send_refs)


def one_step(
    shot, step, comps, got_groups, send_groups,
    wavefields, offsets, now, later, got, saved, pos, traces, speed, contrib, frame, out, after, heavy, model_y, keeps=(), field=None,
):
    first, last = step == 0, step == STEPS - 1
    with_image = 1 in comps
    shots = wavefields.shape[0]
    both, layers, rows_y, cells_z = wavefields.shape[2:]
    vmem, hbm = pl.BlockSpec(memory_space=VMEM), pl.BlockSpec(memory_space=HBM)
    state = jax.ShapeDtypeStruct((both, layers, rows_y, cells_z), jnp.float32)
    image = jax.ShapeDtypeStruct((layers, rows_y, cells_z), jnp.float32)
    aliases = {}
    scratch = []
    args = [
        pltpu.with_memory_space_constraint(field, HBM) if field is wavefields else field
        for field in (now, later)
    ]
    specs = [hbm if first else vmem, hbm if step < 2 else vmem]
    args += [value for pair in got for value in pair]
    specs += [vmem] * (2 * len(got))
    lines = saved is not None and 0 in comps
    if lines:
        args.append(saved)
        specs.append(vmem)
    if with_image:
        args += [pos, traces]
        specs += [vmem, vmem]
    framing = last and with_image
    if first or framing:
        args.append(offsets)
        specs.append(pl.BlockSpec(memory_space=SMEM))
    args.append(speed)
    specs.append(vmem)
    if with_image and not first:
        args.append(contrib)
        specs.append(vmem)
    if framing and frame is not None:
        args.append(frame)
        specs.append(vmem)
    args += [value for _, value in keeps]
    specs += [vmem] * len(keeps)
    held = last and comps == (1,)
    if last and comps == (0,):
        args.append(field)
        specs.append(vmem)
    args += after
    specs += [pl.BlockSpec(memory_space=pl.ANY)] * len(after)
    if held:
        outs = [image]
        out_specs = [vmem]
    elif last:
        if out is not None:
            aliases[len(args)] = 0
            args.append(out)
            specs.append(hbm)
        outs = [jax.ShapeDtypeStruct((shots, 2) + state.shape, jnp.float32)]
        out_specs = [hbm]
        scratch = [
            pltpu.VMEM(state.shape, jnp.float32),
            pltpu.SemaphoreType.DMA((1 + len(keeps) + both * layers,)),
        ]
    else:
        outs = [state]
        for group in send_groups:
            half = jax.ShapeDtypeStruct((len(group), 2, rows_y, cells_z), jnp.bfloat16)
            outs += [half, half]
        out_specs = [vmem] * len(outs)
    if framing:
        outs.append(jax.ShapeDtypeStruct((layers, model_y, cells_z), jnp.float32))
        out_specs.append(vmem)
    elif with_image:
        outs.append(image)
        out_specs.append(vmem)
    if first:
        outs.append(image)
        out_specs.append(vmem)
    if step < 2:
        lead = (2,) if first else ()
        scratch = [pltpu.VMEM(lead + state.shape, jnp.float32), pltpu.SemaphoreType.DMA((1,))]
    return pl.pallas_call(
        functools.partial(
            step_kernel, shot, step, comps, got_groups, send_groups, out is None, frame is not None,
            lines, len(after), tuple(keep for keep, _ in keeps),
        ),
        in_specs=specs,
        out_specs=out_specs,
        out_shape=outs,
        scratch_shapes=scratch,
        input_output_aliases=aliases,
        compiler_params=params(),
        cost_estimate=cost(HEAVY if heavy else 0),
        name="step_%d_shot_%d" % (step, shot),
    )(*args)


def sum_kernel(scale, own_ref, other_ref, after_ref, image_ref, sum_ref, sems):
    del after_ref
    stores = []
    for layer in range(sum_ref.shape[0]):
        sum_ref[layer] = (own_ref[layer] + other_ref[layer]) * scale
        stores.append(
            pltpu.make_async_copy(sum_ref.at[layer], image_ref.at[layer], sems.at[layer])
        )
        stores[-1].start()
    for started in stores:
        started.wait()


def sum_frames(own, other, scale, after):
    vmem, hbm = pl.BlockSpec(memory_space=VMEM), pl.BlockSpec(memory_space=HBM)
    return pl.pallas_call(
        functools.partial(sum_kernel, scale),
        in_specs=[vmem, vmem, hbm],
        out_specs=hbm,
        out_shape=jax.ShapeDtypeStruct(own.shape, jnp.float32),
        scratch_shapes=[
            pltpu.VMEM(own.shape, jnp.float32),
            pltpu.SemaphoreType.DMA((own.shape[0],)),
        ],
        compiler_params=params(),
        cost_estimate=cost(),
        name="sum_frames",
    )(own, other, pltpu.with_memory_space_constraint(after, HBM))


def body(wavefields, courant, offsets, strip_lines, strip_ids, receiver_pos, traces):
    shots = wavefields.shape[0]
    layers = wavefields.shape[3]
    cells_z = wavefields.shape[5]
    model_y = courant.shape[1]
    per_owner = STEPS * EDGE * layers
    shot_devices = lax.axis_size("shot")
    scale = 1.0 / (shots * shot_devices)
    cap = strip_lines.shape[1] // lax.axis_size("space")

    def exchange(sends):
        return [
            (swap_pairs(sends[at], 0), swap_pairs(sends[at + 1], 1)) for at in range(0, len(sends), 2)
        ]

    sends = pack_halo(wavefields, 0, [])
    got = [exchange(sends)]
    message = pack_lines(strip_lines, strip_ids, per_owner, cap, sends[0])
    saved = deliver(message, cap, shots, per_owner)
    for shot in range(1, shots):
        got.append(exchange(pack_halo(wavefields, shot, [message])))
    groups = [BOTH] * shots
    now = [wavefields] * shots
    later = [wavefields] * shots
    contrib = [None] * shots
    speed = [courant] * shots
    out = None
    frame = None
    after = []
    for step in range(STEPS):
        for shot in range(shots):
            split = shot == shots - 1
            send_groups = SPLIT if split and step == STEPS - 2 else BOTH
            common = (wavefields, offsets, now[shot], later[shot])
            fixed = (receiver_pos, traces, speed[shot])
            if step < STEPS - 1:
                early = step == 0 and shot == 0
                made = one_step(
                    shot, step, BOTH[0], groups[shot], () if early else send_groups, *common,
                    got[shot], None if early else saved, *fixed, contrib[shot], None, None, after, early,
                    model_y,
                )
                later[shot], now[shot] = now[shot], made[0]
                if early:
                    made = [*finish_first(shot, made[0], saved), *made[1:]]
                    now[shot] = made[0]
                ends = 1 + 2 * len(send_groups)
                got[shot] = exchange(made[1:ends])
                groups[shot] = send_groups
                contrib[shot] = made[ends]
                if step == 0:
                    speed[shot] = made[ends + 1]
                after = [made[1]]
                continue
            keeps = [] if split and shots > 1 else [(shot, now[shot])]
            if shot == 0 and shots > 1:
                keeps.append((shots - 1, now[shots - 1]))
            field = None
            for group in groups[shot]:
                made = one_step(
                    shot, step, group, (group,), (), *common, got[shot][:1], saved, *fixed,
                    contrib[shot], frame, out, after, group == (0,), model_y,
                    () if group == (1,) else keeps, field,
                )
                got[shot] = got[shot][1:]
                if group == (1,):
                    field = made[0]
                else:
                    out = made[0]
                if 1 in group:
                    frame = made[1]
                    after = [frame]
    if shot_devices == 2:
        other = lax.ppermute(frame, "shot", [(0, 1), (1, 0)])
        image = sum_frames(frame, other, scale, out)
    else:
        image = lax.psum(frame, "shot") * scale
    return (out, image)


def solution(mesh):
    placed = (
        P("shot", None, None, "space", None, None),
        P("space", None, None),
        P("shot"),
        P("shot", "space", None),
        P("shot", "space"),
        P("shot", "space"),
        P("shot", None, "space"),
    )
    return jax.shard_map(
        body,
        mesh=mesh,
        in_specs=placed,
        out_specs=(P("shot", None, None, "space", None, None), P("space", None, None)),
        check_vma=False,
    )
```

```python
import functools

import jax
import jax.numpy as jnp
from jax import lax
from jax.experimental import pallas as pl
from jax.experimental.pallas import tpu as pltpu
from jax.sharding import PartitionSpec as P

STEPS = 4
RDEPTH = 4
EDGE = 4
LANES = 128
VMEM_LIMIT = 24 * 1024 * 1024
VMEM = pltpu.VMEM
SMEM = pltpu.SMEM
HBM = pltpu.HBM
BOTH = ((0, 1),)
SPLIT = ((1,), (0,))
HEAVY = 10**13


def params():
    return pltpu.CompilerParams(vmem_limit_bytes=VMEM_LIMIT)


def cost(weight=0):
    return pl.CostEstimate(flops=1 + weight, bytes_accessed=1, transcendentals=0)


def swap_pairs(value, first):
    count = lax.axis_size("space")
    routes = []
    for at in range(first, count - 1, 2):
        routes += [(at, at + 1), (at + 1, at)]
    return lax.ppermute(value, "space", routes)


def band(rows, centre):
    gap = jnp.abs(
        lax.broadcasted_iota(jnp.int32, (rows, rows), 0)
        - lax.broadcasted_iota(jnp.int32, (rows, rows), 1)
    )
    weights = jnp.where(gap == 0, centre, jnp.where(gap == 1, 16.0, jnp.where(gap == 2, -1.0, 0.0)))
    return weights.astype(jnp.bfloat16)


def mm(left, right, dims=((1,), (0,))):
    return lax.dot_general(left, right, (dims, ((), ())), preferred_element_type=jnp.float32)


def window_at(offset, model_y, rows_y):
    start = jnp.minimum(lax.div(offset, 8), (model_y - rows_y - 8) // 8) * 8
    return pl.multiple_of(start, 8), offset - start


def put_window(target_ref, layer, part, offset):
    rows_y, cells_z = part.shape
    groups = rows_y // 8
    start = pl.multiple_of(lax.div(offset, 8) * 8, 8)
    gap = lax.rem(offset, 8)
    turned = pltpu.roll(part.reshape(groups, 8, cells_z), gap, 1)
    before = lax.broadcasted_iota(jnp.int32, (8, cells_z), 0) < gap
    body = [jnp.where(before, 0.0, turned[0])]
    body += [jnp.where(before, turned[at - 1], turned[at]) for at in range(1, groups)]
    body.append(jnp.where(before, turned[-1], 0.0))
    target_ref[layer, pl.ds(start, rows_y + 8), :] = jnp.concatenate(body, axis=0)


def is_odd():
    return lax.rem(lax.axis_index("space"), 2) == 1


def write_sends(field_ref, groups, send_refs):
    odd = is_odd()
    for at_group, group in enumerate(groups):
        send0_ref, send1_ref = send_refs[2 * at_group : 2 * at_group + 2]
        for place, comp in enumerate(group):
            for at in range(2):
                low = field_ref[comp, at]
                high = field_ref[comp, at + field_ref.shape[-3] - 2]
                send0_ref[place, at] = jnp.where(odd, low, high).astype(jnp.bfloat16)
                send1_ref[place, at] = jnp.where(odd, high, low).astype(jnp.bfloat16)


def pack_kernel(shot, field_ref, *refs):
    send0_ref, send1_ref, own_ref, sems = refs[-4:]
    comps = own_ref.shape[0]
    loads = [
        pltpu.make_async_copy(field_ref.at[shot, 0, comp], own_ref.at[comp], sems.at[comp])
        for comp in range(comps)
    ]
    for load in loads:
        load.start()
    for comp, load in enumerate(loads):
        load.wait()
        write_sends(own_ref, ((comp,),), (send0_ref.at[comp : comp + 1], send1_ref.at[comp : comp + 1]))


def pack_halo(wavefields, shot, after):
    _, _, comps, layers, rows_y, cells_z = wavefields.shape
    half = jax.ShapeDtypeStruct((comps, 2, rows_y, cells_z), jnp.bfloat16)
    return pl.pallas_call(
        functools.partial(pack_kernel, shot),
        in_specs=[pl.BlockSpec(memory_space=HBM)] + [pl.BlockSpec(memory_space=pl.ANY)] * len(after),
        out_specs=[pl.BlockSpec(memory_space=VMEM)] * 2,
        out_shape=[half, half],
        scratch_shapes=[
            pltpu.VMEM((comps, layers, rows_y, cells_z), jnp.float32),
            pltpu.SemaphoreType.DMA((comps,)),
        ],
        compiler_params=params(),
        cost_estimate=cost(),
        name="pack_halo",
    )(pltpu.with_memory_space_constraint(wavefields, HBM), *after)


def pack_lines_kernel(cap, per_owner, ids_ref, lines_ref, after_ref, out_ref):
    shots, hold = ids_ref.shape
    total = shots * hold
    ids = jnp.concatenate([ids_ref[shot : shot + 1] for shot in range(shots)], axis=1)
    ids = ids.astype(jnp.float32)
    row_at = lax.broadcasted_iota(jnp.int32, (total, total), 0)
    col_at = lax.broadcasted_iota(jnp.int32, (total, total), 1)
    slot_at = lax.broadcasted_iota(jnp.int32, (1, total), 1)
    shot_of = jnp.zeros((1, total), jnp.float32)
    for shot in range(1, shots):
        shot_of = shot_of + (slot_at >= shot * hold).astype(jnp.float32)
    owner = jnp.floor((ids + 0.5) * (1.0 / per_owner))
    inside = ids - owner * per_owner
    used = ids >= 0.0
    key = jnp.where(used, owner * shots + shot_of, -1.0)
    wide_key = jnp.broadcast_to(key, (total, total))
    same = jnp.where(row_at == col_at, wide_key, 0.0)
    tall_key = jnp.sum(same, axis=1, keepdims=True)
    earlier_one = (tall_key == wide_key) & (row_at < col_at)
    rank = jnp.sum(earlier_one.astype(jnp.float32), axis=0, keepdims=True)
    target = jnp.where(used, key * cap + rank, -1.0)
    hot = jnp.where(row_at.astype(jnp.float32) == target, 1.0, 0.0)
    tags = jnp.sum(hot * (inside + 1.0), axis=1, keepdims=True)
    hot = hot.astype(jnp.bfloat16)
    cells_z = lines_ref.shape[2]
    rows = mm(hot[:, :hold], lines_ref[0])
    for shot in range(1, shots):
        rows = rows + mm(hot[:, shot * hold : (shot + 1) * hold], lines_ref[shot])
    out_ref[:, :cells_z] = rows.astype(jnp.bfloat16)
    out_ref[:, cells_z:] = jnp.broadcast_to(tags, (total, LANES)).astype(jnp.bfloat16)


def unpack_lines_kernel(cap, shots, per_owner, got_ref, out_ref):
    total = got_ref.shape[0]
    cells_z = out_ref.shape[1]
    tags = got_ref[:, cells_z : cells_z + LANES].astype(jnp.float32)[:, 0:1]
    row_at = lax.broadcasted_iota(jnp.int32, (total, 1), 0).astype(jnp.float32)
    block = jnp.floor((row_at + 0.5) * (1.0 / cap))
    shot_of = block - shots * jnp.floor((block + 0.5) * (1.0 / shots))
    target = jnp.where(tags > 0.5, tags - 1.0 + shot_of * per_owner, -1.0)
    line_at = lax.broadcasted_iota(jnp.int32, (total, shots * per_owner), 1).astype(jnp.float32)
    hot = jnp.where(line_at == target, 1.0, 0.0).astype(jnp.bfloat16)
    out_ref[...] = mm(hot, got_ref[:, :cells_z], ((0,), (0,)))


def pack_lines(strip_lines, strip_ids, per_owner, cap, after):
    shots, hold, cells_z = strip_lines.shape
    vmem = pl.BlockSpec(memory_space=VMEM)
    return pl.pallas_call(
        functools.partial(pack_lines_kernel, cap, per_owner),
        in_specs=[vmem, vmem, pl.BlockSpec(memory_space=pl.ANY)],
        out_specs=vmem,
        out_shape=jax.ShapeDtypeStruct((shots * hold, cells_z + LANES), jnp.bfloat16),
        compiler_params=params(),
        cost_estimate=cost(),
        name="pack_lines",
    )(strip_ids, strip_lines, after)


def deliver(message, cap, shots, per_owner):
    total, wide = message.shape
    message = message.reshape(lax.axis_size("space"), shots * cap, wide)
    got = lax.all_to_all(message, "space", 0, 0, tiled=False)
    return pl.pallas_call(
        functools.partial(unpack_lines_kernel, cap, shots, per_owner),
        out_shape=jax.ShapeDtypeStruct((shots * per_owner, wide - LANES), jnp.float32),
        compiler_params=params(),
        cost_estimate=cost(),
        name="unpack_lines",
    )(got.reshape(total, wide))


def split3(value):
    parts = []
    for _ in range(3):
        part = value.astype(jnp.bfloat16)
        parts.append(part)
        value = value - part.astype(jnp.float32)
    return parts


def take_lines(new_ref, saved_ref, shot, step, layer):
    _, layers, rows_y, _ = new_ref.shape
    base = ((shot * STEPS + step) * layers + layer) * EDGE
    new_ref[0, layer, 0:2, :] = saved_ref[base : base + 2, :]
    new_ref[0, layer, rows_y - 2 :, :] = saved_ref[base + 2 : base + 4, :]


def finish_kernel(shot, new_from, saved_ref, new_ref, send0_ref, send1_ref):
    del new_from
    for layer in range(new_ref.shape[1]):
        take_lines(new_ref, saved_ref, shot, 0, layer)
    write_sends(new_ref, BOTH, (send0_ref, send1_ref))


def finish_first(shot, new, saved):
    comps, _, rows_y, cells_z = new.shape
    half = jax.ShapeDtypeStruct((comps, 2, rows_y, cells_z), jnp.bfloat16)
    vmem = pl.BlockSpec(memory_space=VMEM)
    return pl.pallas_call(
        functools.partial(finish_kernel, shot),
        in_specs=[vmem, vmem],
        out_specs=[vmem] * 3,
        out_shape=[jax.ShapeDtypeStruct(new.shape, new.dtype), half, half],
        input_output_aliases={0: 0},
        compiler_params=params(),
        cost_estimate=cost(),
        name="finish_first_%d" % shot,
    )(new, saved)


def step_kernel(shot, step, comps, got_groups, send_groups, create, lines, waits, keeps, *refs):
    refs = list(refs)

    def take(count):
        taken, refs[:] = refs[:count], refs[count:]
        return taken

    first, last = step == 0, step == STEPS - 1
    with_image = 1 in comps
    now_ref, later_ref = take(2)
    got_of = {}
    for group in got_groups:
        got0_ref, got1_ref = take(2)
        for place, comp in enumerate(group):
            got_of[comp] = (got0_ref, got1_ref, place)
    [saved_ref] = take(1) if lines else [None]
    pos_ref, traces_ref = take(2) if with_image else (None, None)
    framing = last and with_image
    [offsets_ref] = take(1) if first or framing else [None]
    [speed_from] = take(1)
    [contrib_from] = take(1) if with_image and not first else [None]
    keep_refs = take(len(keeps))
    held = last and comps == (1,)
    [field_from] = take(1) if last and comps == (0,) else [None]
    take(waits)
    if held:
        [field_ref] = take(1)
    elif last:
        take(0 if create else 1)
        [out_ref] = take(1)
    else:
        [new_ref] = take(1)
        send_refs = take(2 * len(send_groups))
    [contrib_ref] = take(1) if with_image else [None]
    [speed_out] = take(1) if first else [None]
    if last and not held:
        new_ref, out_sems = take(2)
    [terms_ref] = take(1) if framing else [None]
    loads = []
    if first:
        state_ref, load_sems = take(2)
        loads = [pltpu.make_async_copy(now_ref.at[shot], state_ref, load_sems.at[0])]
        now_ref, later_ref = state_ref.at[0], state_ref.at[1]
    elif step == 1:
        state_ref, load_sems = take(2)
        loads = [pltpu.make_async_copy(later_ref.at[shot, 0], state_ref, load_sems.at[0])]
        later_ref = state_ref
    for load in loads:
        load.start()
    layers, rows_y, cells_z = (field_ref if held else new_ref).shape[-3:]
    stores = []

    def store(source_ref, target_ref):
        stores.append(pltpu.make_async_copy(source_ref, target_ref, out_sems.at[len(stores)]))
        stores[-1].start()

    for keep, keep_ref in zip(keeps, keep_refs):
        store(keep_ref, out_ref.at[keep, 1])
    if field_from is not None:
        store(field_from, out_ref.at[shot, 0, 1])
    odd = is_odd()
    across_z = band(cells_z, -90.0)
    across_y = band(rows_y, 0.0)
    if with_image:
        trace_row = traces_ref[shot, step : step + 1, :]
        lane_of = lax.broadcasted_iota(jnp.int32, (LANES, trace_row.shape[1]), 0)
        trace_parts = [
            jnp.where(lane_of == RDEPTH, part.astype(jnp.float32), 0.0).astype(jnp.bfloat16)
            for part in split3(trace_row)
        ]
        spots = pos_ref[shot : shot + 1, :]
        cell_of = lax.broadcasted_iota(jnp.int32, (rows_y, trace_row.shape[1]), 0)
    for load in loads:
        load.wait()

    for comp in comps:
        got0_ref, got1_ref, place = got_of[comp]

        def layer_of(at):
            if at < 0:
                both = (got1_ref[place, 2 + at], got0_ref[place, 2 + at])
            elif at >= layers:
                both = (got0_ref[place, at - layers], got1_ref[place, at - layers])
            else:
                return now_ref[comp, at]
            even_one, odd_one = (part.astype(jnp.float32) for part in both)
            return jnp.where(odd, odd_one, even_one)

        for layer in range(layers):
            if first and comp == comps[0]:
                start_y, gap = window_at(offsets_ref[shot], speed_from.shape[1], rows_y)
                speed = speed_from[layer, pl.ds(start_y, rows_y + 8), :]
                speed = pltpu.roll(speed, lax.rem(rows_y + 8 - gap, rows_y + 8), 0)[:rows_y]
                speed_out[layer] = speed
            else:
                speed = (speed_out if first else speed_from)[layer]
            here = layer_of(layer)
            high = here.astype(jnp.bfloat16)
            low = (here - high.astype(jnp.float32)).astype(jnp.bfloat16)
            growth = mm(high, across_z) + mm(low, across_z)
            growth = growth + (mm(across_y, high) + mm(across_y, low))
            growth = growth + 16.0 * (layer_of(layer - 1) + layer_of(layer + 1))
            growth = growth - (layer_of(layer - 2) + layer_of(layer + 2))
            growth = growth * (1.0 / 12.0)
            if comp == 1:
                hot = jnp.where(spots == cell_of + layer * rows_y, 1.0, 0.0).astype(jnp.bfloat16)
                plane = mm(hot, trace_parts[0], ((1,), (1,)))
                plane = plane + mm(hot, trace_parts[1], ((1,), (1,)))
                plane = plane + mm(hot, trace_parts[2], ((1,), (1,)))
                growth = jnp.concatenate(
                    [growth[:, :LANES] + plane, growth[:, LANES:]], axis=1
                )
            change = speed * growth
            moved = 2.0 * here - later_ref[comp, layer] + change
            if held:
                field_ref[layer] = moved
            else:
                new_ref[comp, layer] = moved
            if comp == 1:
                term = now_ref[0, layer] * change
                if not first:
                    term = contrib_from[layer] + term
                if framing:
                    terms_ref[layer] = term
                else:
                    contrib_ref[layer] = term
            elif lines:
                take_lines(new_ref, saved_ref, shot, step, layer)
            if last and not held:
                store(new_ref.at[comp, layer], out_ref.at[shot, 0, comp, layer])
    if framing:
        contrib_ref[...] = jnp.zeros_like(contrib_ref)
        for layer in range(layers):
            put_window(contrib_ref, layer, terms_ref[layer], offsets_ref[shot])
    for started in stores:
        started.wait()
    if not last:
        write_sends(new_ref, send_groups, send_refs)


def one_step(
    shot, step, comps, got_groups, send_groups,
    wavefields, offsets, now, later, got, saved, pos, traces, speed, contrib, out, after, heavy, model_y, keeps=(), field=None,
):
    first, last = step == 0, step == STEPS - 1
    with_image = 1 in comps
    shots = wavefields.shape[0]
    both, layers, rows_y, cells_z = wavefields.shape[2:]
    vmem, hbm = pl.BlockSpec(memory_space=VMEM), pl.BlockSpec(memory_space=HBM)
    state = jax.ShapeDtypeStruct((both, layers, rows_y, cells_z), jnp.float32)
    image = jax.ShapeDtypeStruct((layers, rows_y, cells_z), jnp.float32)
    aliases = {}
    scratch = []
    args = [
        pltpu.with_memory_space_constraint(field, HBM) if field is wavefields else field
        for field in (now, later)
    ]
    specs = [hbm if first else vmem, hbm if step < 2 else vmem]
    args += [value for pair in got for value in pair]
    specs += [vmem] * (2 * len(got))
    lines = saved is not None and 0 in comps
    if lines:
        args.append(saved)
        specs.append(vmem)
    if with_image:
        args += [pos, traces]
        specs += [vmem, vmem]
    framing = last and with_image
    if first or framing:
        args.append(offsets)
        specs.append(pl.BlockSpec(memory_space=SMEM))
    args.append(speed)
    specs.append(vmem)
    if with_image and not first:
        args.append(contrib)
        specs.append(vmem)
    args += [value for _, value in keeps]
    specs += [vmem] * len(keeps)
    held = last and comps == (1,)
    if last and comps == (0,):
        args.append(field)
        specs.append(vmem)
    args += after
    specs += [pl.BlockSpec(memory_space=pl.ANY)] * len(after)
    if held:
        outs = [image]
        out_specs = [vmem]
    elif last:
        if out is not None:
            aliases[len(args)] = 0
            args.append(out)
            specs.append(hbm)
        outs = [jax.ShapeDtypeStruct((shots, 2) + state.shape, jnp.float32)]
        out_specs = [hbm]
        scratch = [
            pltpu.VMEM(state.shape, jnp.float32),
            pltpu.SemaphoreType.DMA((1 + len(keeps) + both * layers,)),
        ]
    else:
        outs = [state]
        for group in send_groups:
            half = jax.ShapeDtypeStruct((len(group), 2, rows_y, cells_z), jnp.bfloat16)
            outs += [half, half]
        out_specs = [vmem] * len(outs)
    if framing:
        outs.append(jax.ShapeDtypeStruct((layers, model_y + 8, cells_z), jnp.float32))
        out_specs.append(vmem)
    elif with_image:
        outs.append(image)
        out_specs.append(vmem)
    if first:
        outs.append(image)
        out_specs.append(vmem)
    if framing:
        scratch.append(pltpu.VMEM(image.shape, jnp.float32))
    if step < 2:
        lead = (2,) if first else ()
        scratch = [pltpu.VMEM(lead + state.shape, jnp.float32), pltpu.SemaphoreType.DMA((1,))]
    return pl.pallas_call(
        functools.partial(
            step_kernel, shot, step, comps, got_groups, send_groups, out is None, lines,
            len(after), tuple(keep for keep, _ in keeps),
        ),
        in_specs=specs,
        out_specs=out_specs,
        out_shape=outs,
        scratch_shapes=scratch,
        input_output_aliases=aliases,
        compiler_params=params(),
        cost_estimate=cost(HEAVY if heavy else 0),
        name="step_%d_shot_%d" % (step, shot),
    )(*args)


def sum_kernel(scale, *refs):
    image_ref, sum_ref, sems = refs[-3:]
    frame_refs = refs[:-4]
    layers, model_y, _ = sum_ref.shape
    stores = []
    for layer in range(layers):
        total = None
        for at in range(0, len(frame_refs), 2):
            own_ref, other_ref = frame_refs[at : at + 2]
            pair = own_ref[layer, :model_y] + other_ref[layer, :model_y]
            total = pair if total is None else total + pair
        sum_ref[layer] = total * scale
        stores.append(
            pltpu.make_async_copy(sum_ref.at[layer], image_ref.at[layer], sems.at[layer])
        )
        stores[-1].start()
    for started in stores:
        started.wait()


def sum_frames(frames, others, scale, model_y, after):
    layers, _, cells_z = frames[0].shape
    vmem, hbm = pl.BlockSpec(memory_space=VMEM), pl.BlockSpec(memory_space=HBM)
    args = [value for pair in zip(frames, others) for value in pair]
    shape_out = jax.ShapeDtypeStruct((layers, model_y, cells_z), jnp.float32)
    return pl.pallas_call(
        functools.partial(sum_kernel, scale),
        in_specs=[vmem] * len(args) + [hbm],
        out_specs=hbm,
        out_shape=shape_out,
        scratch_shapes=[
            pltpu.VMEM(shape_out.shape, jnp.float32),
            pltpu.SemaphoreType.DMA((layers,)),
        ],
        compiler_params=params(),
        cost_estimate=cost(),
        name="sum_frames",
    )(*args, pltpu.with_memory_space_constraint(after, HBM))


def body(wavefields, courant, offsets, strip_lines, strip_ids, receiver_pos, traces):
    shots = wavefields.shape[0]
    layers = wavefields.shape[3]
    cells_z = wavefields.shape[5]
    model_y = courant.shape[1]
    per_owner = STEPS * EDGE * layers
    shot_devices = lax.axis_size("shot")
    scale = 1.0 / (shots * shot_devices)
    cap = strip_lines.shape[1] // lax.axis_size("space")

    def exchange(sends):
        return [
            (swap_pairs(sends[at], 0), swap_pairs(sends[at + 1], 1)) for at in range(0, len(sends), 2)
        ]

    sends = pack_halo(wavefields, 0, [])
    got = [exchange(sends)]
    message = pack_lines(strip_lines, strip_ids, per_owner, cap, sends[0])
    saved = deliver(message, cap, shots, per_owner)
    for shot in range(1, shots):
        got.append(exchange(pack_halo(wavefields, shot, [message])))
    groups = [BOTH] * shots
    now = [wavefields] * shots
    later = [wavefields] * shots
    contrib = [None] * shots
    speed = [courant] * shots
    out = None
    frames = []
    after = []
    for step in range(STEPS):
        for shot in range(shots):
            split = shot == shots - 1
            send_groups = SPLIT if split and step == STEPS - 2 else BOTH
            common = (wavefields, offsets, now[shot], later[shot])
            fixed = (receiver_pos, traces, speed[shot])
            if step < STEPS - 1:
                early = step == 0 and shot == 0
                made = one_step(
                    shot, step, BOTH[0], groups[shot], () if early else send_groups, *common,
                    got[shot], None if early else saved, *fixed, contrib[shot], None, after, early,
                    model_y,
                )
                later[shot], now[shot] = now[shot], made[0]
                if early:
                    made = [*finish_first(shot, made[0], saved), *made[1:]]
                    now[shot] = made[0]
                ends = 1 + 2 * len(send_groups)
                got[shot] = exchange(made[1:ends])
                groups[shot] = send_groups
                contrib[shot] = made[ends]
                if step == 0:
                    speed[shot] = made[ends + 1]
                after = [made[1]]
                continue
            keeps = [] if split and shots > 1 else [(shot, now[shot])]
            if shot == 0 and shots > 1:
                keeps.append((shots - 1, now[shots - 1]))
            field = None
            for group in groups[shot]:
                made = one_step(
                    shot, step, group, (group,), (), *common, got[shot][:1], saved, *fixed,
                    contrib[shot], out, after, group == (0,), model_y,
                    () if group == (1,) else keeps, field,
                )
                got[shot] = got[shot][1:]
                if group == (1,):
                    field = made[0]
                else:
                    out = made[0]
                if 1 in group:
                    frames.append(made[1])
                    after = [made[1]]
    if shot_devices == 2:
        others = [lax.ppermute(frame, "shot", [(0, 1), (1, 0)]) for frame in frames]
        image = sum_frames(frames, others, scale, model_y, out)
    else:
        frame = sum(frames)[:, :model_y]
        image = lax.psum(frame, "shot") * scale
    return (out, image)


def solution(mesh):
    placed = (
        P("shot", None, None, "space", None, None),
        P("space", None, None),
        P("shot"),
        P("shot", "space", None),
        P("shot", "space"),
        P("shot", "space"),
        P("shot", None, "space"),
    )
    return jax.shard_map(
        body,
        mesh=mesh,
        in_specs=placed,
        out_specs=(P("shot", None, None, "space", None, None), P("space", None, None)),
        check_vma=False,
    )
```

```python
import functools

import jax
import jax.numpy as jnp
from jax import lax
from jax.experimental import pallas as pl
from jax.experimental.pallas import tpu as pltpu
from jax.sharding import PartitionSpec as P

STEPS = 4
RDEPTH = 4
EDGE = 4
LANES = 128
VMEM_LIMIT = 24 * 1024 * 1024
VMEM = pltpu.VMEM
SMEM = pltpu.SMEM
HBM = pltpu.HBM
BOTH = ((0, 1),)
SPLIT = ((1,), (0,))
HEAVY = 10**13


def params():
    return pltpu.CompilerParams(vmem_limit_bytes=VMEM_LIMIT)


def cost(weight=0):
    return pl.CostEstimate(flops=1 + weight, bytes_accessed=1, transcendentals=0)


def swap_pairs(value, first):
    count = lax.axis_size("space")
    routes = []
    for at in range(first, count - 1, 2):
        routes += [(at, at + 1), (at + 1, at)]
    return lax.ppermute(value, "space", routes)


def band(rows, centre):
    gap = jnp.abs(
        lax.broadcasted_iota(jnp.int32, (rows, rows), 0)
        - lax.broadcasted_iota(jnp.int32, (rows, rows), 1)
    )
    weights = jnp.where(gap == 0, centre, jnp.where(gap == 1, 16.0, jnp.where(gap == 2, -1.0, 0.0)))
    return weights.astype(jnp.bfloat16)


def mm(left, right, dims=((1,), (0,))):
    return lax.dot_general(left, right, (dims, ((), ())), preferred_element_type=jnp.float32)


def window_at(offset, model_y, rows_y):
    start = jnp.minimum(lax.div(offset, 8), (model_y - rows_y - 8) // 8) * 8
    return pl.multiple_of(start, 8), offset - start


def put_window(target_ref, layer, part_ref, offset):
    _, rows_y, cells_z = part_ref.shape
    start = pl.multiple_of(lax.div(offset, 8) * 8, 8)
    gap = lax.rem(offset, 8)
    before = lax.broadcasted_iota(jnp.int32, (8, cells_z), 0) < gap
    last = jnp.zeros((8, cells_z), jnp.float32)
    for at in range(0, rows_y + 8, 8):
        turned = jnp.zeros((8, cells_z), jnp.float32)
        if at < rows_y:
            turned = pltpu.roll(part_ref[layer, at : at + 8], gap, 0)
        here = pl.ds(pl.multiple_of(start + at, 8), 8)
        target_ref[layer, here, :] = jnp.where(before, last, turned)
        last = turned


def is_odd():
    return lax.rem(lax.axis_index("space"), 2) == 1


def write_sends(field_ref, groups, send_refs):
    odd = is_odd()
    for at_group, group in enumerate(groups):
        send0_ref, send1_ref = send_refs[2 * at_group : 2 * at_group + 2]
        for place, comp in enumerate(group):
            for at in range(2):
                low = field_ref[comp, at]
                high = field_ref[comp, at + field_ref.shape[-3] - 2]
                send0_ref[place, at] = jnp.where(odd, low, high).astype(jnp.bfloat16)
                send1_ref[place, at] = jnp.where(odd, high, low).astype(jnp.bfloat16)


def pack_kernel(shot, field_ref, *refs):
    send0_ref, send1_ref, own_ref, sems = refs[-4:]
    comps = own_ref.shape[0]
    loads = [
        pltpu.make_async_copy(field_ref.at[shot, 0, comp], own_ref.at[comp], sems.at[comp])
        for comp in range(comps)
    ]
    for load in loads:
        load.start()
    for comp, load in enumerate(loads):
        load.wait()
        write_sends(own_ref, ((comp,),), (send0_ref.at[comp : comp + 1], send1_ref.at[comp : comp + 1]))


def pack_halo(wavefields, shot, after):
    _, _, comps, layers, rows_y, cells_z = wavefields.shape
    half = jax.ShapeDtypeStruct((comps, 2, rows_y, cells_z), jnp.bfloat16)
    return pl.pallas_call(
        functools.partial(pack_kernel, shot),
        in_specs=[pl.BlockSpec(memory_space=HBM)] + [pl.BlockSpec(memory_space=pl.ANY)] * len(after),
        out_specs=[pl.BlockSpec(memory_space=VMEM)] * 2,
        out_shape=[half, half],
        scratch_shapes=[
            pltpu.VMEM((comps, layers, rows_y, cells_z), jnp.float32),
            pltpu.SemaphoreType.DMA((comps,)),
        ],
        compiler_params=params(),
        cost_estimate=cost(),
        name="pack_halo",
    )(pltpu.with_memory_space_constraint(wavefields, HBM), *after)


def pack_lines_kernel(cap, per_owner, ids_ref, lines_ref, after_ref, out_ref):
    shots, hold = ids_ref.shape
    total = shots * hold
    ids = jnp.concatenate([ids_ref[shot : shot + 1] for shot in range(shots)], axis=1)
    ids = ids.astype(jnp.float32)
    row_at = lax.broadcasted_iota(jnp.int32, (total, total), 0)
    col_at = lax.broadcasted_iota(jnp.int32, (total, total), 1)
    slot_at = lax.broadcasted_iota(jnp.int32, (1, total), 1)
    shot_of = jnp.zeros((1, total), jnp.float32)
    for shot in range(1, shots):
        shot_of = shot_of + (slot_at >= shot * hold).astype(jnp.float32)
    owner = jnp.floor((ids + 0.5) * (1.0 / per_owner))
    inside = ids - owner * per_owner
    used = ids >= 0.0
    key = jnp.where(used, owner * shots + shot_of, -1.0)
    wide_key = jnp.broadcast_to(key, (total, total))
    same = jnp.where(row_at == col_at, wide_key, 0.0)
    tall_key = jnp.sum(same, axis=1, keepdims=True)
    earlier_one = (tall_key == wide_key) & (row_at < col_at)
    rank = jnp.sum(earlier_one.astype(jnp.float32), axis=0, keepdims=True)
    target = jnp.where(used, key * cap + rank, -1.0)
    hot = jnp.where(row_at.astype(jnp.float32) == target, 1.0, 0.0)
    tags = jnp.sum(hot * (inside + 1.0), axis=1, keepdims=True)
    hot = hot.astype(jnp.bfloat16)
    cells_z = lines_ref.shape[2]
    rows = mm(hot[:, :hold], lines_ref[0])
    for shot in range(1, shots):
        rows = rows + mm(hot[:, shot * hold : (shot + 1) * hold], lines_ref[shot])
    out_ref[:, :cells_z] = rows.astype(jnp.bfloat16)
    out_ref[:, cells_z:] = jnp.broadcast_to(tags, (total, LANES)).astype(jnp.bfloat16)


def unpack_lines_kernel(cap, shots, per_owner, got_ref, out_ref):
    total = got_ref.shape[0]
    cells_z = out_ref.shape[1]
    tags = got_ref[:, cells_z : cells_z + LANES].astype(jnp.float32)[:, 0:1]
    row_at = lax.broadcasted_iota(jnp.int32, (total, 1), 0).astype(jnp.float32)
    block = jnp.floor((row_at + 0.5) * (1.0 / cap))
    shot_of = block - shots * jnp.floor((block + 0.5) * (1.0 / shots))
    target = jnp.where(tags > 0.5, tags - 1.0 + shot_of * per_owner, -1.0)
    line_at = lax.broadcasted_iota(jnp.int32, (total, shots * per_owner), 1).astype(jnp.float32)
    hot = jnp.where(line_at == target, 1.0, 0.0).astype(jnp.bfloat16)
    out_ref[...] = mm(hot, got_ref[:, :cells_z], ((0,), (0,)))


def pack_lines(strip_lines, strip_ids, per_owner, cap, after):
    shots, hold, cells_z = strip_lines.shape
    vmem = pl.BlockSpec(memory_space=VMEM)
    return pl.pallas_call(
        functools.partial(pack_lines_kernel, cap, per_owner),
        in_specs=[vmem, vmem, pl.BlockSpec(memory_space=pl.ANY)],
        out_specs=vmem,
        out_shape=jax.ShapeDtypeStruct((shots * hold, cells_z + LANES), jnp.bfloat16),
        compiler_params=params(),
        cost_estimate=cost(),
        name="pack_lines",
    )(strip_ids, strip_lines, after)


def deliver(message, cap, shots, per_owner):
    total, wide = message.shape
    message = message.reshape(lax.axis_size("space"), shots * cap, wide)
    got = lax.all_to_all(message, "space", 0, 0, tiled=False)
    return pl.pallas_call(
        functools.partial(unpack_lines_kernel, cap, shots, per_owner),
        out_shape=jax.ShapeDtypeStruct((shots * per_owner, wide - LANES), jnp.float32),
        compiler_params=params(),
        cost_estimate=cost(),
        name="unpack_lines",
    )(got.reshape(total, wide))


def split3(value):
    parts = []
    for _ in range(3):
        part = value.astype(jnp.bfloat16)
        parts.append(part)
        value = value - part.astype(jnp.float32)
    return parts


def take_lines(new_ref, saved_ref, shot, step, layer):
    _, layers, rows_y, _ = new_ref.shape
    base = ((shot * STEPS + step) * layers + layer) * EDGE
    new_ref[0, layer, 0:2, :] = saved_ref[base : base + 2, :]
    new_ref[0, layer, rows_y - 2 :, :] = saved_ref[base + 2 : base + 4, :]


def finish_kernel(shot, new_from, saved_ref, new_ref, send0_ref, send1_ref):
    del new_from
    for layer in range(new_ref.shape[1]):
        take_lines(new_ref, saved_ref, shot, 0, layer)
    write_sends(new_ref, BOTH, (send0_ref, send1_ref))


def finish_first(shot, new, saved):
    comps, _, rows_y, cells_z = new.shape
    half = jax.ShapeDtypeStruct((comps, 2, rows_y, cells_z), jnp.bfloat16)
    vmem = pl.BlockSpec(memory_space=VMEM)
    return pl.pallas_call(
        functools.partial(finish_kernel, shot),
        in_specs=[vmem, vmem],
        out_specs=[vmem] * 3,
        out_shape=[jax.ShapeDtypeStruct(new.shape, new.dtype), half, half],
        input_output_aliases={0: 0},
        compiler_params=params(),
        cost_estimate=cost(),
        name="finish_first_%d" % shot,
    )(new, saved)


def step_kernel(shot, step, comps, got_groups, send_groups, create, lines, waits, keeps, *refs):
    refs = list(refs)

    def take(count):
        taken, refs[:] = refs[:count], refs[count:]
        return taken

    first, last = step == 0, step == STEPS - 1
    with_image = 1 in comps
    now_ref, later_ref = take(2)
    got_of = {}
    for group in got_groups:
        got0_ref, got1_ref = take(2)
        for place, comp in enumerate(group):
            got_of[comp] = (got0_ref, got1_ref, place)
    [saved_ref] = take(1) if lines else [None]
    pos_ref, traces_ref = take(2) if with_image else (None, None)
    framing = last and with_image
    [offsets_ref] = take(1) if first or framing else [None]
    [speed_from] = take(1)
    [contrib_from] = take(1) if with_image and not first else [None]
    keep_refs = take(len(keeps))
    held = last and comps == (1,)
    [field_from] = take(1) if last and comps == (0,) else [None]
    take(waits)
    if held:
        [field_ref] = take(1)
    elif last:
        take(0 if create else 1)
        [out_ref] = take(1)
    else:
        [new_ref] = take(1)
        send_refs = take(2 * len(send_groups))
    [contrib_ref] = take(1) if with_image else [None]
    [speed_out] = take(1) if first else [None]
    if last and not held:
        new_ref, out_sems = take(2)
    [terms_ref] = take(1) if framing else [None]
    loads = []
    if first:
        state_ref, load_sems = take(2)
        loads = [pltpu.make_async_copy(now_ref.at[shot], state_ref, load_sems.at[0])]
        now_ref, later_ref = state_ref.at[0], state_ref.at[1]
    elif step == 1:
        state_ref, load_sems = take(2)
        loads = [pltpu.make_async_copy(later_ref.at[shot, 0], state_ref, load_sems.at[0])]
        later_ref = state_ref
    for load in loads:
        load.start()
    layers, rows_y, cells_z = (field_ref if held else new_ref).shape[-3:]
    stores = []

    def store(source_ref, target_ref):
        stores.append(pltpu.make_async_copy(source_ref, target_ref, out_sems.at[len(stores)]))
        stores[-1].start()

    for keep, keep_ref in zip(keeps, keep_refs):
        store(keep_ref, out_ref.at[keep, 1])
    if field_from is not None:
        store(field_from, out_ref.at[shot, 0, 1])
    odd = is_odd()
    across_z = band(cells_z, -90.0)
    across_y = band(rows_y, 0.0)
    if with_image:
        trace_row = traces_ref[shot, step : step + 1, :]
        lane_of = lax.broadcasted_iota(jnp.int32, (LANES, trace_row.shape[1]), 0)
        trace_parts = [
            jnp.where(lane_of == RDEPTH, part.astype(jnp.float32), 0.0).astype(jnp.bfloat16)
            for part in split3(trace_row)
        ]
        spots = pos_ref[shot : shot + 1, :]
        cell_of = lax.broadcasted_iota(jnp.int32, (rows_y, trace_row.shape[1]), 0)
    for load in loads:
        load.wait()

    for comp in comps:
        got0_ref, got1_ref, place = got_of[comp]

        def layer_of(at):
            if at < 0:
                both = (got1_ref[place, 2 + at], got0_ref[place, 2 + at])
            elif at >= layers:
                both = (got0_ref[place, at - layers], got1_ref[place, at - layers])
            else:
                return now_ref[comp, at]
            even_one, odd_one = (part.astype(jnp.float32) for part in both)
            return jnp.where(odd, odd_one, even_one)

        for layer in range(layers):
            if first and comp == comps[0]:
                start_y, gap = window_at(offsets_ref[shot], speed_from.shape[1], rows_y)
                speed = speed_from[layer, pl.ds(start_y, rows_y + 8), :]
                speed = pltpu.roll(speed, lax.rem(rows_y + 8 - gap, rows_y + 8), 0)[:rows_y]
                speed_out[layer] = speed
            else:
                speed = (speed_out if first else speed_from)[layer]
            here = layer_of(layer)
            high = here.astype(jnp.bfloat16)
            low = (here - high.astype(jnp.float32)).astype(jnp.bfloat16)
            growth = mm(high, across_z) + mm(low, across_z)
            growth = growth + (mm(across_y, high) + mm(across_y, low))
            growth = growth + 16.0 * (layer_of(layer - 1) + layer_of(layer + 1))
            growth = growth - (layer_of(layer - 2) + layer_of(layer + 2))
            growth = growth * (1.0 / 12.0)
            if comp == 1:
                hot = jnp.where(spots == cell_of + layer * rows_y, 1.0, 0.0).astype(jnp.bfloat16)
                plane = mm(hot, trace_parts[0], ((1,), (1,)))
                plane = plane + mm(hot, trace_parts[1], ((1,), (1,)))
                plane = plane + mm(hot, trace_parts[2], ((1,), (1,)))
                growth = jnp.concatenate(
                    [growth[:, :LANES] + plane, growth[:, LANES:]], axis=1
                )
            change = speed * growth
            moved = 2.0 * here - later_ref[comp, layer] + change
            if held:
                field_ref[layer] = moved
            else:
                new_ref[comp, layer] = moved
            if comp == 1:
                term = now_ref[0, layer] * change
                if not first:
                    term = contrib_from[layer] + term
                if framing:
                    terms_ref[layer] = term
                else:
                    contrib_ref[layer] = term
            elif lines:
                take_lines(new_ref, saved_ref, shot, step, layer)
            if last and not held:
                store(new_ref.at[comp, layer], out_ref.at[shot, 0, comp, layer])
    if framing:
        contrib_ref[...] = jnp.zeros_like(contrib_ref)
        for layer in range(layers):
            put_window(contrib_ref, layer, terms_ref, offsets_ref[shot])
    for started in stores:
        started.wait()
    if not last:
        write_sends(new_ref, send_groups, send_refs)


def one_step(
    shot, step, comps, got_groups, send_groups,
    wavefields, offsets, now, later, got, saved, pos, traces, speed, contrib, out, after, heavy, model_y, keeps=(), field=None,
):
    first, last = step == 0, step == STEPS - 1
    with_image = 1 in comps
    shots = wavefields.shape[0]
    both, layers, rows_y, cells_z = wavefields.shape[2:]
    vmem, hbm = pl.BlockSpec(memory_space=VMEM), pl.BlockSpec(memory_space=HBM)
    state = jax.ShapeDtypeStruct((both, layers, rows_y, cells_z), jnp.float32)
    image = jax.ShapeDtypeStruct((layers, rows_y, cells_z), jnp.float32)
    aliases = {}
    scratch = []
    args = [
        pltpu.with_memory_space_constraint(field, HBM) if field is wavefields else field
        for field in (now, later)
    ]
    specs = [hbm if first else vmem, hbm if step < 2 else vmem]
    args += [value for pair in got for value in pair]
    specs += [vmem] * (2 * len(got))
    lines = saved is not None and 0 in comps
    if lines:
        args.append(saved)
        specs.append(vmem)
    if with_image:
        args += [pos, traces]
        specs += [vmem, vmem]
    framing = last and with_image
    if first or framing:
        args.append(offsets)
        specs.append(pl.BlockSpec(memory_space=SMEM))
    args.append(speed)
    specs.append(vmem)
    if with_image and not first:
        args.append(contrib)
        specs.append(vmem)
    args += [value for _, value in keeps]
    specs += [vmem] * len(keeps)
    held = last and comps == (1,)
    if last and comps == (0,):
        args.append(field)
        specs.append(vmem)
    args += after
    specs += [pl.BlockSpec(memory_space=pl.ANY)] * len(after)
    if held:
        outs = [image]
        out_specs = [vmem]
    elif last:
        if out is not None:
            aliases[len(args)] = 0
            args.append(out)
            specs.append(hbm)
        outs = [jax.ShapeDtypeStruct((shots, 2) + state.shape, jnp.float32)]
        out_specs = [hbm]
        scratch = [
            pltpu.VMEM(state.shape, jnp.float32),
            pltpu.SemaphoreType.DMA((1 + len(keeps) + both * layers,)),
        ]
    else:
        outs = [state]
        for group in send_groups:
            half = jax.ShapeDtypeStruct((len(group), 2, rows_y, cells_z), jnp.bfloat16)
            outs += [half, half]
        out_specs = [vmem] * len(outs)
    if framing:
        outs.append(jax.ShapeDtypeStruct((layers, model_y + 8, cells_z), jnp.float32))
        out_specs.append(vmem)
    elif with_image:
        outs.append(image)
        out_specs.append(vmem)
    if first:
        outs.append(image)
        out_specs.append(vmem)
    if framing:
        scratch.append(pltpu.VMEM(image.shape, jnp.float32))
    if step < 2:
        lead = (2,) if first else ()
        scratch = [pltpu.VMEM(lead + state.shape, jnp.float32), pltpu.SemaphoreType.DMA((1,))]
    return pl.pallas_call(
        functools.partial(
            step_kernel, shot, step, comps, got_groups, send_groups, out is None, lines,
            len(after), tuple(keep for keep, _ in keeps),
        ),
        in_specs=specs,
        out_specs=out_specs,
        out_shape=outs,
        scratch_shapes=scratch,
        input_output_aliases=aliases,
        compiler_params=params(),
        cost_estimate=cost(HEAVY if heavy else 0),
        name="step_%d_shot_%d" % (step, shot),
    )(*args)


def sum_kernel(scale, *refs):
    image_ref, sum_ref, sems = refs[-3:]
    frame_refs = refs[:-4]
    layers, model_y, _ = sum_ref.shape
    stores = []
    for layer in range(layers):
        for row in range(0, model_y, 16):
            rows = slice(row, row + 16)
            total = None
            for at in range(0, len(frame_refs), 2):
                pair = frame_refs[at][layer, rows] + frame_refs[at + 1][layer, rows]
                total = pair if total is None else total + pair
            sum_ref[layer, rows] = total * scale
        stores.append(
            pltpu.make_async_copy(sum_ref.at[layer], image_ref.at[layer], sems.at[layer])
        )
        stores[-1].start()
    for started in stores:
        started.wait()


def sum_frames(frames, others, scale, model_y, after):
    layers, _, cells_z = frames[0].shape
    vmem, hbm = pl.BlockSpec(memory_space=VMEM), pl.BlockSpec(memory_space=HBM)
    args = [value for pair in zip(frames, others) for value in pair]
    shape_out = jax.ShapeDtypeStruct((layers, model_y, cells_z), jnp.float32)
    return pl.pallas_call(
        functools.partial(sum_kernel, scale),
        in_specs=[vmem] * len(args) + [hbm],
        out_specs=hbm,
        out_shape=shape_out,
        scratch_shapes=[
            pltpu.VMEM(shape_out.shape, jnp.float32),
            pltpu.SemaphoreType.DMA((layers,)),
        ],
        compiler_params=params(),
        cost_estimate=cost(),
        name="sum_frames",
    )(*args, pltpu.with_memory_space_constraint(after, HBM))


def body(wavefields, courant, offsets, strip_lines, strip_ids, receiver_pos, traces):
    shots = wavefields.shape[0]
    layers = wavefields.shape[3]
    cells_z = wavefields.shape[5]
    model_y = courant.shape[1]
    per_owner = STEPS * EDGE * layers
    shot_devices = lax.axis_size("shot")
    scale = 1.0 / (shots * shot_devices)
    cap = strip_lines.shape[1] // lax.axis_size("space")

    def exchange(sends):
        return [
            (swap_pairs(sends[at], 0), swap_pairs(sends[at + 1], 1)) for at in range(0, len(sends), 2)
        ]

    sends = pack_halo(wavefields, 0, [])
    got = [exchange(sends)]
    message = pack_lines(strip_lines, strip_ids, per_owner, cap, sends[0])
    saved = deliver(message, cap, shots, per_owner)
    for shot in range(1, shots):
        got.append(exchange(pack_halo(wavefields, shot, [message])))
    groups = [BOTH] * shots
    now = [wavefields] * shots
    later = [wavefields] * shots
    contrib = [None] * shots
    speed = [courant] * shots
    out = None
    frames = []
    after = []
    for step in range(STEPS):
        for shot in range(shots):
            split = shot == shots - 1
            send_groups = SPLIT if split and step == STEPS - 2 else BOTH
            common = (wavefields, offsets, now[shot], later[shot])
            fixed = (receiver_pos, traces, speed[shot])
            if step < STEPS - 1:
                early = step == 0 and shot == 0
                made = one_step(
                    shot, step, BOTH[0], groups[shot], () if early else send_groups, *common,
                    got[shot], None if early else saved, *fixed, contrib[shot], None, after, early,
                    model_y,
                )
                later[shot], now[shot] = now[shot], made[0]
                if early:
                    made = [*finish_first(shot, made[0], saved), *made[1:]]
                    now[shot] = made[0]
                ends = 1 + 2 * len(send_groups)
                got[shot] = exchange(made[1:ends])
                groups[shot] = send_groups
                contrib[shot] = made[ends]
                if step == 0:
                    speed[shot] = made[ends + 1]
                after = [made[1]]
                continue
            keeps = [] if split and shots > 1 else [(shot, now[shot])]
            if shot == 0 and shots > 1:
                keeps.append((shots - 1, now[shots - 1]))
            field = None
            for group in groups[shot]:
                made = one_step(
                    shot, step, group, (group,), (), *common, got[shot][:1], saved, *fixed,
                    contrib[shot], out, after, group == (0,), model_y,
                    () if group == (1,) else keeps, field,
                )
                got[shot] = got[shot][1:]
                if group == (1,):
                    field = made[0]
                else:
                    out = made[0]
                if 1 in group:
                    frames.append(made[1])
                    after = [made[1]]
    if shot_devices == 2:
        others = [lax.ppermute(frame, "shot", [(0, 1), (1, 0)]) for frame in frames]
        image = sum_frames(frames, others, scale, model_y, out)
    else:
        frame = sum(frames)[:, :model_y]
        image = lax.psum(frame, "shot") * scale
    return (out, image)


def solution(mesh):
    placed = (
        P("shot", None, None, "space", None, None),
        P("space", None, None),
        P("shot"),
        P("shot", "space", None),
        P("shot", "space"),
        P("shot", "space"),
        P("shot", None, "space"),
    )
    return jax.shard_map(
        body,
        mesh=mesh,
        in_specs=placed,
        out_specs=(P("shot", None, None, "space", None, None), P("space", None, None)),
        check_vma=False,
    )
```

```python
import functools

import jax
import jax.numpy as jnp
from jax import lax
from jax.experimental import pallas as pl
from jax.experimental.pallas import tpu as pltpu
from jax.sharding import PartitionSpec as P

STEPS = 4
RDEPTH = 4
EDGE = 4
LANES = 128
VMEM_LIMIT = 24 * 1024 * 1024
VMEM = pltpu.VMEM
SMEM = pltpu.SMEM
HBM = pltpu.HBM
BOTH = ((0, 1),)
SPLIT = ((1,), (0,))
HEAVY = 10**13


def params():
    return pltpu.CompilerParams(vmem_limit_bytes=VMEM_LIMIT)


def cost(weight=0):
    return pl.CostEstimate(flops=1 + weight, bytes_accessed=1, transcendentals=0)


def swap_pairs(value, first):
    count = lax.axis_size("space")
    routes = []
    for at in range(first, count - 1, 2):
        routes += [(at, at + 1), (at + 1, at)]
    return lax.ppermute(value, "space", routes)


def band(rows, centre):
    gap = jnp.abs(
        lax.broadcasted_iota(jnp.int32, (rows, rows), 0)
        - lax.broadcasted_iota(jnp.int32, (rows, rows), 1)
    )
    weights = jnp.where(gap == 0, centre, jnp.where(gap == 1, 16.0, jnp.where(gap == 2, -1.0, 0.0)))
    return weights.astype(jnp.bfloat16)


def mm(left, right, dims=((1,), (0,))):
    return lax.dot_general(left, right, (dims, ((), ())), preferred_element_type=jnp.float32)


def window_at(offset, model_y, rows_y):
    start = jnp.minimum(lax.div(offset, 8), (model_y - rows_y - 8) // 8) * 8
    return pl.multiple_of(start, 8), offset - start


def put_window(target_ref, layer, part_ref, offset):
    _, rows_y, cells_z = part_ref.shape
    start = pl.multiple_of(lax.div(offset, 8) * 8, 8)
    gap = lax.rem(offset, 8)
    before = lax.broadcasted_iota(jnp.int32, (8, cells_z), 0) < gap
    last = jnp.zeros((8, cells_z), jnp.float32)
    for at in range(0, rows_y + 8, 8):
        turned = jnp.zeros((8, cells_z), jnp.float32)
        if at < rows_y:
            turned = pltpu.roll(part_ref[layer, at : at + 8], gap, 0)
        here = pl.ds(pl.multiple_of(start + at, 8), 8)
        target_ref[layer, here, :] = jnp.where(before, last, turned)
        last = turned


def is_odd():
    return lax.rem(lax.axis_index("space"), 2) == 1


def halo_shape(group, rows_y, cells_z):
    rows = sum(2 * (rows_y if comp == 1 else rows_y - EDGE) for comp in group)
    return jax.ShapeDtypeStruct((rows, cells_z), jnp.bfloat16)


def halo_layer(halo, group, rows_y, comp, at):
    if comp == 1:
        return halo[at * rows_y : (at + 1) * rows_y]
    kept = rows_y - EDGE
    base = (2 * rows_y if 1 in group else 0) + at * kept
    edge = jnp.zeros((EDGE // 2, halo.shape[1]), halo.dtype)
    return jnp.concatenate([edge, halo[base : base + kept], edge], axis=0)


def write_sends(field_ref, groups, send_refs):
    odd = is_odd()
    _, layers, rows_y, _ = field_ref.shape

    def pieces(group, first):
        made = []
        for comp in sorted(group, reverse=True):
            for at in (first, first + 1):
                layer = field_ref[comp, at]
                made.append(layer if comp == 1 else layer[EDGE // 2 : rows_y - EDGE // 2])
        return jnp.concatenate(made, axis=0)

    for at_group, group in enumerate(groups):
        low, high = pieces(group, 0), pieces(group, layers - 2)
        send_refs[2 * at_group][...] = jnp.where(odd, low, high).astype(jnp.bfloat16)
        send_refs[2 * at_group + 1][...] = jnp.where(odd, high, low).astype(jnp.bfloat16)


def pack_kernel(shot, field_ref, *refs):
    send0_ref, send1_ref, own_ref, sems = refs[-4:]
    comps = own_ref.shape[0]
    loads = [
        pltpu.make_async_copy(field_ref.at[shot, 0, comp], own_ref.at[comp], sems.at[comp])
        for comp in range(comps)
    ]
    for load in loads:
        load.start()
    for load in loads:
        load.wait()
    write_sends(own_ref, BOTH, (send0_ref, send1_ref))


def pack_halo(wavefields, shot, after):
    _, _, comps, layers, rows_y, cells_z = wavefields.shape
    half = halo_shape(BOTH[0], rows_y, cells_z)
    return pl.pallas_call(
        functools.partial(pack_kernel, shot),
        in_specs=[pl.BlockSpec(memory_space=HBM)] + [pl.BlockSpec(memory_space=pl.ANY)] * len(after),
        out_specs=[pl.BlockSpec(memory_space=VMEM)] * 2,
        out_shape=[half, half],
        scratch_shapes=[
            pltpu.VMEM((comps, layers, rows_y, cells_z), jnp.float32),
            pltpu.SemaphoreType.DMA((comps,)),
        ],
        compiler_params=params(),
        cost_estimate=cost(),
        name="pack_halo",
    )(pltpu.with_memory_space_constraint(wavefields, HBM), *after)


def pack_lines_kernel(cap, per_owner, ids_ref, lines_ref, after_ref, out_ref):
    shots, hold = ids_ref.shape
    total = shots * hold
    ids = jnp.concatenate([ids_ref[shot : shot + 1] for shot in range(shots)], axis=1)
    ids = ids.astype(jnp.float32)
    row_at = lax.broadcasted_iota(jnp.int32, (total, total), 0)
    col_at = lax.broadcasted_iota(jnp.int32, (total, total), 1)
    slot_at = lax.broadcasted_iota(jnp.int32, (1, total), 1)
    shot_of = jnp.zeros((1, total), jnp.float32)
    for shot in range(1, shots):
        shot_of = shot_of + (slot_at >= shot * hold).astype(jnp.float32)
    owner = jnp.floor((ids + 0.5) * (1.0 / per_owner))
    inside = ids - owner * per_owner
    used = ids >= 0.0
    key = jnp.where(used, owner * shots + shot_of, -1.0)
    wide_key = jnp.broadcast_to(key, (total, total))
    same = jnp.where(row_at == col_at, wide_key, 0.0)
    tall_key = jnp.sum(same, axis=1, keepdims=True)
    earlier_one = (tall_key == wide_key) & (row_at < col_at)
    rank = jnp.sum(earlier_one.astype(jnp.float32), axis=0, keepdims=True)
    target = jnp.where(used, key * cap + rank, -1.0)
    hot = jnp.where(row_at.astype(jnp.float32) == target, 1.0, 0.0)
    tags = jnp.sum(hot * (inside + 1.0), axis=1, keepdims=True)
    hot = hot.astype(jnp.bfloat16)
    cells_z = lines_ref.shape[2]
    rows = mm(hot[:, :hold], lines_ref[0])
    for shot in range(1, shots):
        rows = rows + mm(hot[:, shot * hold : (shot + 1) * hold], lines_ref[shot])
    out_ref[:, :cells_z] = rows.astype(jnp.bfloat16)
    out_ref[:, cells_z:] = jnp.broadcast_to(tags, (total, LANES)).astype(jnp.bfloat16)


def unpack_lines_kernel(cap, shots, per_owner, got_ref, out_ref):
    total = got_ref.shape[0]
    cells_z = out_ref.shape[1]
    tags = got_ref[:, cells_z : cells_z + LANES].astype(jnp.float32)[:, 0:1]
    row_at = lax.broadcasted_iota(jnp.int32, (total, 1), 0).astype(jnp.float32)
    block = jnp.floor((row_at + 0.5) * (1.0 / cap))
    shot_of = block - shots * jnp.floor((block + 0.5) * (1.0 / shots))
    target = jnp.where(tags > 0.5, tags - 1.0 + shot_of * per_owner, -1.0)
    line_at = lax.broadcasted_iota(jnp.int32, (total, shots * per_owner), 1).astype(jnp.float32)
    hot = jnp.where(line_at == target, 1.0, 0.0).astype(jnp.bfloat16)
    out_ref[...] = mm(hot, got_ref[:, :cells_z], ((0,), (0,)))


def pack_lines(strip_lines, strip_ids, per_owner, cap, after):
    shots, hold, cells_z = strip_lines.shape
    vmem = pl.BlockSpec(memory_space=VMEM)
    return pl.pallas_call(
        functools.partial(pack_lines_kernel, cap, per_owner),
        in_specs=[vmem, vmem, pl.BlockSpec(memory_space=pl.ANY)],
        out_specs=vmem,
        out_shape=jax.ShapeDtypeStruct((shots * hold, cells_z + LANES), jnp.bfloat16),
        compiler_params=params(),
        cost_estimate=cost(),
        name="pack_lines",
    )(strip_ids, strip_lines, after)


def deliver(message, cap, shots, per_owner):
    total, wide = message.shape
    message = message.reshape(lax.axis_size("space"), shots * cap, wide)
    got = lax.all_to_all(message, "space", 0, 0, tiled=False)
    return pl.pallas_call(
        functools.partial(unpack_lines_kernel, cap, shots, per_owner),
        out_shape=jax.ShapeDtypeStruct((shots * per_owner, wide - LANES), jnp.float32),
        compiler_params=params(),
        cost_estimate=cost(),
        name="unpack_lines",
    )(got.reshape(total, wide))


def split3(value):
    parts = []
    for _ in range(3):
        part = value.astype(jnp.bfloat16)
        parts.append(part)
        value = value - part.astype(jnp.float32)
    return parts


def take_lines(new_ref, saved_ref, shot, step, layer):
    _, layers, rows_y, _ = new_ref.shape
    base = ((shot * STEPS + step) * layers + layer) * EDGE
    new_ref[0, layer, 0:2, :] = saved_ref[base : base + 2, :]
    new_ref[0, layer, rows_y - 2 :, :] = saved_ref[base + 2 : base + 4, :]


def finish_kernel(shot, new_from, saved_ref, new_ref, send0_ref, send1_ref):
    del new_from
    for layer in range(new_ref.shape[1]):
        take_lines(new_ref, saved_ref, shot, 0, layer)
    write_sends(new_ref, BOTH, (send0_ref, send1_ref))


def finish_first(shot, new, saved):
    comps, _, rows_y, cells_z = new.shape
    half = halo_shape(BOTH[0], rows_y, cells_z)
    vmem = pl.BlockSpec(memory_space=VMEM)
    return pl.pallas_call(
        functools.partial(finish_kernel, shot),
        in_specs=[vmem, vmem],
        out_specs=[vmem] * 3,
        out_shape=[jax.ShapeDtypeStruct(new.shape, new.dtype), half, half],
        input_output_aliases={0: 0},
        compiler_params=params(),
        cost_estimate=cost(),
        name="finish_first_%d" % shot,
    )(new, saved)


def step_kernel(shot, step, comps, got_groups, send_groups, create, lines, waits, keeps, *refs):
    refs = list(refs)

    def take(count):
        taken, refs[:] = refs[:count], refs[count:]
        return taken

    first, last = step == 0, step == STEPS - 1
    with_image = 1 in comps
    now_ref, later_ref = take(2)
    got_of = {}
    for group in got_groups:
        got0_ref, got1_ref = take(2)
        for comp in group:
            got_of[comp] = (got0_ref, got1_ref, group)
    [saved_ref] = take(1) if lines else [None]
    pos_ref, traces_ref = take(2) if with_image else (None, None)
    framing = last and with_image
    [offsets_ref] = take(1) if first or framing else [None]
    [speed_from] = take(1)
    [contrib_from] = take(1) if with_image and not first else [None]
    keep_refs = take(len(keeps))
    held = last and comps == (1,)
    [field_from] = take(1) if last and comps == (0,) else [None]
    take(waits)
    if held:
        [field_ref] = take(1)
    elif last:
        take(0 if create else 1)
        [out_ref] = take(1)
    else:
        [new_ref] = take(1)
        send_refs = take(2 * len(send_groups))
    [contrib_ref] = take(1) if with_image else [None]
    [speed_out] = take(1) if first else [None]
    if last and not held:
        new_ref, out_sems = take(2)
    [terms_ref] = take(1) if framing else [None]
    loads = []
    if first:
        state_ref, load_sems = take(2)
        loads = [pltpu.make_async_copy(now_ref.at[shot], state_ref, load_sems.at[0])]
        now_ref, later_ref = state_ref.at[0], state_ref.at[1]
    elif step == 1:
        state_ref, load_sems = take(2)
        loads = [pltpu.make_async_copy(later_ref.at[shot, 0], state_ref, load_sems.at[0])]
        later_ref = state_ref
    for load in loads:
        load.start()
    layers, rows_y, cells_z = (field_ref if held else new_ref).shape[-3:]
    stores = []

    def store(source_ref, target_ref):
        stores.append(pltpu.make_async_copy(source_ref, target_ref, out_sems.at[len(stores)]))
        stores[-1].start()

    for keep, keep_ref in zip(keeps, keep_refs):
        store(keep_ref, out_ref.at[keep, 1])
    if field_from is not None:
        store(field_from, out_ref.at[shot, 0, 1])
    odd = is_odd()
    across_z = band(cells_z, -90.0)
    across_y = band(rows_y, 0.0)
    if with_image:
        trace_row = traces_ref[shot, step : step + 1, :]
        lane_of = lax.broadcasted_iota(jnp.int32, (LANES, trace_row.shape[1]), 0)
        trace_parts = [
            jnp.where(lane_of == RDEPTH, part.astype(jnp.float32), 0.0).astype(jnp.bfloat16)
            for part in split3(trace_row)
        ]
        spots = pos_ref[shot : shot + 1, :]
        cell_of = lax.broadcasted_iota(jnp.int32, (rows_y, trace_row.shape[1]), 0)
    for load in loads:
        load.wait()

    for comp in comps:
        got0_ref, got1_ref, group = got_of[comp]
        got0, got1 = got0_ref[...].astype(jnp.float32), got1_ref[...].astype(jnp.float32)
        below, above = jnp.where(odd, got0, got1), jnp.where(odd, got1, got0)

        def layer_of(at):
            if at < 0:
                return halo_layer(below, group, rows_y, comp, 2 + at)
            if at >= layers:
                return halo_layer(above, group, rows_y, comp, at - layers)
            return now_ref[comp, at]

        for layer in range(layers):
            if first and comp == comps[0]:
                start_y, gap = window_at(offsets_ref[shot], speed_from.shape[1], rows_y)
                speed = speed_from[layer, pl.ds(start_y, rows_y + 8), :]
                speed = pltpu.roll(speed, lax.rem(rows_y + 8 - gap, rows_y + 8), 0)[:rows_y]
                speed_out[layer] = speed
            else:
                speed = (speed_out if first else speed_from)[layer]
            here = layer_of(layer)
            high = here.astype(jnp.bfloat16)
            low = (here - high.astype(jnp.float32)).astype(jnp.bfloat16)
            growth = mm(high, across_z) + mm(low, across_z)
            growth = growth + (mm(across_y, high) + mm(across_y, low))
            growth = growth + 16.0 * (layer_of(layer - 1) + layer_of(layer + 1))
            growth = growth - (layer_of(layer - 2) + layer_of(layer + 2))
            growth = growth * (1.0 / 12.0)
            if comp == 1:
                hot = jnp.where(spots == cell_of + layer * rows_y, 1.0, 0.0).astype(jnp.bfloat16)
                plane = mm(hot, trace_parts[0], ((1,), (1,)))
                plane = plane + mm(hot, trace_parts[1], ((1,), (1,)))
                plane = plane + mm(hot, trace_parts[2], ((1,), (1,)))
                growth = jnp.concatenate(
                    [growth[:, :LANES] + plane, growth[:, LANES:]], axis=1
                )
            change = speed * growth
            moved = 2.0 * here - later_ref[comp, layer] + change
            if held:
                field_ref[layer] = moved
            else:
                new_ref[comp, layer] = moved
            if comp == 1:
                term = now_ref[0, layer] * change
                if not first:
                    term = contrib_from[layer] + term
                if framing:
                    terms_ref[layer] = term
                else:
                    contrib_ref[layer] = term
            elif lines:
                take_lines(new_ref, saved_ref, shot, step, layer)
            if last and not held:
                store(new_ref.at[comp, layer], out_ref.at[shot, 0, comp, layer])
    if framing:
        contrib_ref[...] = jnp.zeros_like(contrib_ref)
        for layer in range(layers):
            put_window(contrib_ref, layer, terms_ref, offsets_ref[shot])
    for started in stores:
        started.wait()
    if not last:
        write_sends(new_ref, send_groups, send_refs)


def one_step(
    shot, step, comps, got_groups, send_groups,
    wavefields, offsets, now, later, got, saved, pos, traces, speed, contrib, out, after, heavy, model_y, keeps=(), field=None,
):
    first, last = step == 0, step == STEPS - 1
    with_image = 1 in comps
    shots = wavefields.shape[0]
    both, layers, rows_y, cells_z = wavefields.shape[2:]
    vmem, hbm = pl.BlockSpec(memory_space=VMEM), pl.BlockSpec(memory_space=HBM)
    state = jax.ShapeDtypeStruct((both, layers, rows_y, cells_z), jnp.float32)
    image = jax.ShapeDtypeStruct((layers, rows_y, cells_z), jnp.float32)
    aliases = {}
    scratch = []
    args = [
        pltpu.with_memory_space_constraint(field, HBM) if field is wavefields else field
        for field in (now, later)
    ]
    specs = [hbm if first else vmem, hbm if step < 2 else vmem]
    args += [value for pair in got for value in pair]
    specs += [vmem] * (2 * len(got))
    lines = saved is not None and 0 in comps
    if lines:
        args.append(saved)
        specs.append(vmem)
    if with_image:
        args += [pos, traces]
        specs += [vmem, vmem]
    framing = last and with_image
    if first or framing:
        args.append(offsets)
        specs.append(pl.BlockSpec(memory_space=SMEM))
    args.append(speed)
    specs.append(vmem)
    if with_image and not first:
        args.append(contrib)
        specs.append(vmem)
    args += [value for _, value in keeps]
    specs += [vmem] * len(keeps)
    held = last and comps == (1,)
    if last and comps == (0,):
        args.append(field)
        specs.append(vmem)
    args += after
    specs += [pl.BlockSpec(memory_space=pl.ANY)] * len(after)
    if held:
        outs = [image]
        out_specs = [vmem]
    elif last:
        if out is not None:
            aliases[len(args)] = 0
            args.append(out)
            specs.append(hbm)
        outs = [jax.ShapeDtypeStruct((shots, 2) + state.shape, jnp.float32)]
        out_specs = [hbm]
        scratch = [
            pltpu.VMEM(state.shape, jnp.float32),
            pltpu.SemaphoreType.DMA((1 + len(keeps) + both * layers,)),
        ]
    else:
        outs = [state]
        for group in send_groups:
            half = halo_shape(group, rows_y, cells_z)
            outs += [half, half]
        out_specs = [vmem] * len(outs)
    if framing:
        outs.append(jax.ShapeDtypeStruct((layers, model_y + 8, cells_z), jnp.float32))
        out_specs.append(vmem)
    elif with_image:
        outs.append(image)
        out_specs.append(vmem)
    if first:
        outs.append(image)
        out_specs.append(vmem)
    if framing:
        scratch.append(pltpu.VMEM(image.shape, jnp.float32))
    if step < 2:
        lead = (2,) if first else ()
        scratch = [pltpu.VMEM(lead + state.shape, jnp.float32), pltpu.SemaphoreType.DMA((1,))]
    return pl.pallas_call(
        functools.partial(
            step_kernel, shot, step, comps, got_groups, send_groups, out is None, lines,
            len(after), tuple(keep for keep, _ in keeps),
        ),
        in_specs=specs,
        out_specs=out_specs,
        out_shape=outs,
        scratch_shapes=scratch,
        input_output_aliases=aliases,
        compiler_params=params(),
        cost_estimate=cost(HEAVY if heavy else 0),
        name="step_%d_shot_%d" % (step, shot),
    )(*args)


def sum_kernel(scale, *refs):
    image_ref, sum_ref, sems = refs[-3:]
    frame_refs = refs[:-4]
    layers, model_y, _ = sum_ref.shape
    stores = []
    for layer in range(layers):
        for row in range(0, model_y, 16):
            rows = slice(row, row + 16)
            total = None
            for at in range(0, len(frame_refs), 2):
                pair = frame_refs[at][layer, rows] + frame_refs[at + 1][layer, rows]
                total = pair if total is None else total + pair
            sum_ref[layer, rows] = total * scale
        stores.append(
            pltpu.make_async_copy(sum_ref.at[layer], image_ref.at[layer], sems.at[layer])
        )
        stores[-1].start()
    for started in stores:
        started.wait()


def sum_frames(frames, others, scale, model_y, after):
    layers, _, cells_z = frames[0].shape
    vmem, hbm = pl.BlockSpec(memory_space=VMEM), pl.BlockSpec(memory_space=HBM)
    args = [value for pair in zip(frames, others) for value in pair]
    shape_out = jax.ShapeDtypeStruct((layers, model_y, cells_z), jnp.float32)
    return pl.pallas_call(
        functools.partial(sum_kernel, scale),
        in_specs=[vmem] * len(args) + [hbm],
        out_specs=hbm,
        out_shape=shape_out,
        scratch_shapes=[
            pltpu.VMEM(shape_out.shape, jnp.float32),
            pltpu.SemaphoreType.DMA((layers,)),
        ],
        compiler_params=params(),
        cost_estimate=cost(),
        name="sum_frames",
    )(*args, pltpu.with_memory_space_constraint(after, HBM))


def body(wavefields, courant, offsets, strip_lines, strip_ids, receiver_pos, traces):
    shots = wavefields.shape[0]
    layers = wavefields.shape[3]
    cells_z = wavefields.shape[5]
    model_y = courant.shape[1]
    per_owner = STEPS * EDGE * layers
    shot_devices = lax.axis_size("shot")
    scale = 1.0 / (shots * shot_devices)
    cap = strip_lines.shape[1] // lax.axis_size("space")

    def exchange(sends):
        return [
            (swap_pairs(sends[at], 0), swap_pairs(sends[at + 1], 1)) for at in range(0, len(sends), 2)
        ]

    sends = pack_halo(wavefields, 0, [])
    got = [exchange(sends)]
    message = pack_lines(strip_lines, strip_ids, per_owner, cap, sends[0])
    saved = deliver(message, cap, shots, per_owner)
    for shot in range(1, shots):
        got.append(exchange(pack_halo(wavefields, shot, [message])))
    groups = [BOTH] * shots
    now = [wavefields] * shots
    later = [wavefields] * shots
    contrib = [None] * shots
    speed = [courant] * shots
    out = None
    frames = []
    after = []
    for step in range(STEPS):
        for shot in range(shots):
            split = shot == shots - 1
            send_groups = SPLIT if split and step == STEPS - 2 else BOTH
            common = (wavefields, offsets, now[shot], later[shot])
            fixed = (receiver_pos, traces, speed[shot])
            if step < STEPS - 1:
                early = step == 0 and shot == 0
                made = one_step(
                    shot, step, BOTH[0], groups[shot], () if early else send_groups, *common,
                    got[shot], None if early else saved, *fixed, contrib[shot], None, after, early,
                    model_y,
                )
                later[shot], now[shot] = now[shot], made[0]
                if early:
                    made = [*finish_first(shot, made[0], saved), *made[1:]]
                    now[shot] = made[0]
                ends = 1 + 2 * len(send_groups)
                got[shot] = exchange(made[1:ends])
                groups[shot] = send_groups
                contrib[shot] = made[ends]
                if step == 0:
                    speed[shot] = made[ends + 1]
                after = [made[1]]
                continue
            keeps = [] if split and shots > 1 else [(shot, now[shot])]
            if shot == 0 and shots > 1:
                keeps.append((shots - 1, now[shots - 1]))
            field = None
            for group in groups[shot]:
                made = one_step(
                    shot, step, group, (group,), (), *common, got[shot][:1], saved, *fixed,
                    contrib[shot], out, after, group == (0,), model_y,
                    () if group == (1,) else keeps, field,
                )
                got[shot] = got[shot][1:]
                if group == (1,):
                    field = made[0]
                else:
                    out = made[0]
                if 1 in group:
                    frames.append(made[1])
                    after = [made[1]]
    if shot_devices == 2:
        others = [lax.ppermute(frame, "shot", [(0, 1), (1, 0)]) for frame in frames]
        image = sum_frames(frames, others, scale, model_y, out)
    else:
        frame = sum(frames)[:, :model_y]
        image = lax.psum(frame, "shot") * scale
    return (out, image)


def solution(mesh):
    placed = (
        P("shot", None, None, "space", None, None),
        P("space", None, None),
        P("shot"),
        P("shot", "space", None),
        P("shot", "space"),
        P("shot", "space"),
        P("shot", None, "space"),
    )
    return jax.shard_map(
        body,
        mesh=mesh,
        in_specs=placed,
        out_specs=(P("shot", None, None, "space", None, None), P("space", None, None)),
        check_vma=False,
    )
```

```python
import functools

import jax
import jax.numpy as jnp
from jax import lax
from jax.experimental import pallas as pl
from jax.experimental.pallas import tpu as pltpu
from jax.sharding import PartitionSpec as P

STEPS = 4
RDEPTH = 4
EDGE = 4
LANES = 128
VMEM_LIMIT = 24 * 1024 * 1024
VMEM = pltpu.VMEM
SMEM = pltpu.SMEM
HBM = pltpu.HBM
BOTH = ((0, 1),)
SPLIT = ((1,), (0,))
HEAVY = 10**13


def params():
    return pltpu.CompilerParams(vmem_limit_bytes=VMEM_LIMIT)


def cost(weight=0):
    return pl.CostEstimate(flops=1 + weight, bytes_accessed=1, transcendentals=0)


def swap_pairs(value, first):
    count = lax.axis_size("space")
    routes = []
    for at in range(first, count - 1, 2):
        routes += [(at, at + 1), (at + 1, at)]
    return lax.ppermute(value, "space", routes)


def band(rows, centre):
    gap = jnp.abs(
        lax.broadcasted_iota(jnp.int32, (rows, rows), 0)
        - lax.broadcasted_iota(jnp.int32, (rows, rows), 1)
    )
    weights = jnp.where(gap == 0, centre, jnp.where(gap == 1, 16.0, jnp.where(gap == 2, -1.0, 0.0)))
    return weights.astype(jnp.bfloat16)


def mm(left, right, dims=((1,), (0,))):
    return lax.dot_general(left, right, (dims, ((), ())), preferred_element_type=jnp.float32)


def window_at(offset, model_y, rows_y):
    start = jnp.minimum(lax.div(offset, 8), (model_y - rows_y - 8) // 8) * 8
    return pl.multiple_of(start, 8), offset - start


def put_window(target_ref, layer, part_ref, offset, base_ref):
    _, rows_y, cells_z = part_ref.shape
    start = pl.multiple_of(lax.div(offset, 8) * 8, 8)
    gap = lax.rem(offset, 8)
    before = lax.broadcasted_iota(jnp.int32, (8, cells_z), 0) < gap
    last = jnp.zeros((8, cells_z), jnp.float32)
    for at in range(0, rows_y + 8, 8):
        turned = jnp.zeros((8, cells_z), jnp.float32)
        if at < rows_y:
            turned = pltpu.roll(part_ref[layer, at : at + 8], gap, 0)
        here = pl.ds(pl.multiple_of(start + at, 8), 8)
        placed = jnp.where(before, last, turned)
        if base_ref is not None:
            placed = base_ref[layer, here, :] + placed
        target_ref[layer, here, :] = placed
        last = turned


def is_odd():
    return lax.rem(lax.axis_index("space"), 2) == 1


def halo_shape(group, rows_y, cells_z):
    rows = sum(2 * (rows_y if comp == 1 else rows_y - EDGE) for comp in group)
    return jax.ShapeDtypeStruct((rows, cells_z), jnp.bfloat16)


def halo_layer(halo, group, rows_y, comp, at):
    if comp == 1:
        return halo[at * rows_y : (at + 1) * rows_y]
    kept = rows_y - EDGE
    base = (2 * rows_y if 1 in group else 0) + at * kept
    edge = jnp.zeros((EDGE // 2, halo.shape[1]), halo.dtype)
    return jnp.concatenate([edge, halo[base : base + kept], edge], axis=0)


def write_sends(field_ref, groups, send_refs):
    odd = is_odd()
    _, layers, rows_y, _ = field_ref.shape

    def pieces(group, first):
        made = []
        for comp in sorted(group, reverse=True):
            for at in (first, first + 1):
                layer = field_ref[comp, at]
                made.append(layer if comp == 1 else layer[EDGE // 2 : rows_y - EDGE // 2])
        return jnp.concatenate(made, axis=0)

    for at_group, group in enumerate(groups):
        low, high = pieces(group, 0), pieces(group, layers - 2)
        send_refs[2 * at_group][...] = jnp.where(odd, low, high).astype(jnp.bfloat16)
        send_refs[2 * at_group + 1][...] = jnp.where(odd, high, low).astype(jnp.bfloat16)


def pack_kernel(shot, field_ref, *refs):
    send0_ref, send1_ref, own_ref, sems = refs[-4:]
    comps = own_ref.shape[0]
    loads = [
        pltpu.make_async_copy(field_ref.at[shot, 0, comp], own_ref.at[comp], sems.at[comp])
        for comp in range(comps)
    ]
    for load in loads:
        load.start()
    for load in loads:
        load.wait()
    write_sends(own_ref, BOTH, (send0_ref, send1_ref))


def pack_halo(wavefields, shot, after):
    _, _, comps, layers, rows_y, cells_z = wavefields.shape
    half = halo_shape(BOTH[0], rows_y, cells_z)
    return pl.pallas_call(
        functools.partial(pack_kernel, shot),
        in_specs=[pl.BlockSpec(memory_space=HBM)] + [pl.BlockSpec(memory_space=pl.ANY)] * len(after),
        out_specs=[pl.BlockSpec(memory_space=VMEM)] * 2,
        out_shape=[half, half],
        scratch_shapes=[
            pltpu.VMEM((comps, layers, rows_y, cells_z), jnp.float32),
            pltpu.SemaphoreType.DMA((comps,)),
        ],
        compiler_params=params(),
        cost_estimate=cost(),
        name="pack_halo",
    )(pltpu.with_memory_space_constraint(wavefields, HBM), *after)


def pack_lines_kernel(cap, per_owner, ids_ref, lines_ref, after_ref, out_ref):
    shots, hold = ids_ref.shape
    total = shots * hold
    ids = jnp.concatenate([ids_ref[shot : shot + 1] for shot in range(shots)], axis=1)
    ids = ids.astype(jnp.float32)
    row_at = lax.broadcasted_iota(jnp.int32, (total, total), 0)
    col_at = lax.broadcasted_iota(jnp.int32, (total, total), 1)
    slot_at = lax.broadcasted_iota(jnp.int32, (1, total), 1)
    shot_of = jnp.zeros((1, total), jnp.float32)
    for shot in range(1, shots):
        shot_of = shot_of + (slot_at >= shot * hold).astype(jnp.float32)
    owner = jnp.floor((ids + 0.5) * (1.0 / per_owner))
    inside = ids - owner * per_owner
    used = ids >= 0.0
    key = jnp.where(used, owner * shots + shot_of, -1.0)
    wide_key = jnp.broadcast_to(key, (total, total))
    same = jnp.where(row_at == col_at, wide_key, 0.0)
    tall_key = jnp.sum(same, axis=1, keepdims=True)
    earlier_one = (tall_key == wide_key) & (row_at < col_at)
    rank = jnp.sum(earlier_one.astype(jnp.float32), axis=0, keepdims=True)
    target = jnp.where(used, key * cap + rank, -1.0)
    hot = jnp.where(row_at.astype(jnp.float32) == target, 1.0, 0.0)
    tags = jnp.sum(hot * (inside + 1.0), axis=1, keepdims=True)
    hot = hot.astype(jnp.bfloat16)
    cells_z = lines_ref.shape[2]
    rows = mm(hot[:, :hold], lines_ref[0])
    for shot in range(1, shots):
        rows = rows + mm(hot[:, shot * hold : (shot + 1) * hold], lines_ref[shot])
    out_ref[:, :cells_z] = rows.astype(jnp.bfloat16)
    out_ref[:, cells_z:] = jnp.broadcast_to(tags, (total, LANES)).astype(jnp.bfloat16)


def unpack_lines_kernel(cap, shots, per_owner, got_ref, out_ref):
    total = got_ref.shape[0]
    cells_z = out_ref.shape[1]
    tags = got_ref[:, cells_z : cells_z + LANES].astype(jnp.float32)[:, 0:1]
    row_at = lax.broadcasted_iota(jnp.int32, (total, 1), 0).astype(jnp.float32)
    block = jnp.floor((row_at + 0.5) * (1.0 / cap))
    shot_of = block - shots * jnp.floor((block + 0.5) * (1.0 / shots))
    target = jnp.where(tags > 0.5, tags - 1.0 + shot_of * per_owner, -1.0)
    line_at = lax.broadcasted_iota(jnp.int32, (total, shots * per_owner), 1).astype(jnp.float32)
    hot = jnp.where(line_at == target, 1.0, 0.0).astype(jnp.bfloat16)
    out_ref[...] = mm(hot, got_ref[:, :cells_z], ((0,), (0,)))


def pack_lines(strip_lines, strip_ids, per_owner, cap, after):
    shots, hold, cells_z = strip_lines.shape
    vmem = pl.BlockSpec(memory_space=VMEM)
    return pl.pallas_call(
        functools.partial(pack_lines_kernel, cap, per_owner),
        in_specs=[vmem, vmem, pl.BlockSpec(memory_space=pl.ANY)],
        out_specs=vmem,
        out_shape=jax.ShapeDtypeStruct((shots * hold, cells_z + LANES), jnp.bfloat16),
        compiler_params=params(),
        cost_estimate=cost(),
        name="pack_lines",
    )(strip_ids, strip_lines, after)


def deliver(message, cap, shots, per_owner):
    total, wide = message.shape
    message = message.reshape(lax.axis_size("space"), shots * cap, wide)
    got = lax.all_to_all(message, "space", 0, 0, tiled=False)
    return pl.pallas_call(
        functools.partial(unpack_lines_kernel, cap, shots, per_owner),
        out_shape=jax.ShapeDtypeStruct((shots * per_owner, wide - LANES), jnp.float32),
        compiler_params=params(),
        cost_estimate=cost(),
        name="unpack_lines",
    )(got.reshape(total, wide))


def split3(value):
    parts = []
    for _ in range(3):
        part = value.astype(jnp.bfloat16)
        parts.append(part)
        value = value - part.astype(jnp.float32)
    return parts


def take_lines(new_ref, saved_ref, shot, step, layer):
    _, layers, rows_y, _ = new_ref.shape
    base = ((shot * STEPS + step) * layers + layer) * EDGE
    new_ref[0, layer, 0:2, :] = saved_ref[base : base + 2, :]
    new_ref[0, layer, rows_y - 2 :, :] = saved_ref[base + 2 : base + 4, :]


def finish_kernel(shot, new_from, saved_ref, new_ref, send0_ref, send1_ref):
    del new_from
    for layer in range(new_ref.shape[1]):
        take_lines(new_ref, saved_ref, shot, 0, layer)
    write_sends(new_ref, BOTH, (send0_ref, send1_ref))


def finish_first(shot, new, saved):
    comps, _, rows_y, cells_z = new.shape
    half = halo_shape(BOTH[0], rows_y, cells_z)
    vmem = pl.BlockSpec(memory_space=VMEM)
    return pl.pallas_call(
        functools.partial(finish_kernel, shot),
        in_specs=[vmem, vmem],
        out_specs=[vmem] * 3,
        out_shape=[jax.ShapeDtypeStruct(new.shape, new.dtype), half, half],
        input_output_aliases={0: 0},
        compiler_params=params(),
        cost_estimate=cost(),
        name="finish_first_%d" % shot,
    )(new, saved)


def step_kernel(shot, step, comps, got_groups, send_groups, create, framed, lines, waits, keeps, *refs):
    refs = list(refs)

    def take(count):
        taken, refs[:] = refs[:count], refs[count:]
        return taken

    first, last = step == 0, step == STEPS - 1
    with_image = 1 in comps
    now_ref, later_ref = take(2)
    got_of = {}
    for group in got_groups:
        got0_ref, got1_ref = take(2)
        for comp in group:
            got_of[comp] = (got0_ref, got1_ref, group)
    [saved_ref] = take(1) if lines else [None]
    pos_ref, traces_ref = take(2) if with_image else (None, None)
    framing = last and with_image
    [offsets_ref] = take(1) if first or framing else [None]
    [speed_from] = take(1)
    [contrib_from] = take(1) if with_image and not first else [None]
    [frame_from] = take(1) if framed else [None]
    keep_refs = take(len(keeps))
    held = last and comps == (1,)
    [field_from] = take(1) if last and comps == (0,) else [None]
    take(waits)
    if held:
        [field_ref] = take(1)
    elif last:
        take(0 if create else 1)
        [out_ref] = take(1)
    else:
        [new_ref] = take(1)
        send_refs = take(2 * len(send_groups))
    [contrib_ref] = take(1) if with_image else [None]
    [speed_out] = take(1) if first else [None]
    if last and not held:
        new_ref, out_sems = take(2)
    [terms_ref] = take(1) if framing else [None]
    loads = []
    if first:
        state_ref, load_sems = take(2)
        loads = [pltpu.make_async_copy(now_ref.at[shot], state_ref, load_sems.at[0])]
        now_ref, later_ref = state_ref.at[0], state_ref.at[1]
    elif step == 1:
        state_ref, load_sems = take(2)
        loads = [pltpu.make_async_copy(later_ref.at[shot, 0], state_ref, load_sems.at[0])]
        later_ref = state_ref
    for load in loads:
        load.start()
    layers, rows_y, cells_z = (field_ref if held else new_ref).shape[-3:]
    stores = []

    def store(source_ref, target_ref):
        stores.append(pltpu.make_async_copy(source_ref, target_ref, out_sems.at[len(stores)]))
        stores[-1].start()

    for keep, keep_ref in zip(keeps, keep_refs):
        store(keep_ref, out_ref.at[keep, 1])
    if field_from is not None:
        store(field_from, out_ref.at[shot, 0, 1])
    odd = is_odd()
    across_z = band(cells_z, -90.0)
    across_y = band(rows_y, 0.0)
    if with_image:
        trace_row = traces_ref[shot, step : step + 1, :]
        lane_of = lax.broadcasted_iota(jnp.int32, (LANES, trace_row.shape[1]), 0)
        trace_parts = [
            jnp.where(lane_of == RDEPTH, part.astype(jnp.float32), 0.0).astype(jnp.bfloat16)
            for part in split3(trace_row)
        ]
        spots = pos_ref[shot : shot + 1, :]
        cell_of = lax.broadcasted_iota(jnp.int32, (rows_y, trace_row.shape[1]), 0)
    for load in loads:
        load.wait()

    for comp in comps:
        got0_ref, got1_ref, group = got_of[comp]
        got0, got1 = got0_ref[...].astype(jnp.float32), got1_ref[...].astype(jnp.float32)
        below, above = jnp.where(odd, got0, got1), jnp.where(odd, got1, got0)

        def layer_of(at):
            if at < 0:
                return halo_layer(below, group, rows_y, comp, 2 + at)
            if at >= layers:
                return halo_layer(above, group, rows_y, comp, at - layers)
            return now_ref[comp, at]

        for layer in range(layers):
            if first and comp == comps[0]:
                start_y, gap = window_at(offsets_ref[shot], speed_from.shape[1], rows_y)
                speed = speed_from[layer, pl.ds(start_y, rows_y + 8), :]
                speed = pltpu.roll(speed, lax.rem(rows_y + 8 - gap, rows_y + 8), 0)[:rows_y]
                speed_out[layer] = speed
            else:
                speed = (speed_out if first else speed_from)[layer]
            here = layer_of(layer)
            high = here.astype(jnp.bfloat16)
            low = (here - high.astype(jnp.float32)).astype(jnp.bfloat16)
            growth = mm(high, across_z) + mm(low, across_z)
            growth = growth + (mm(across_y, high) + mm(across_y, low))
            growth = growth + 16.0 * (layer_of(layer - 1) + layer_of(layer + 1))
            growth = growth - (layer_of(layer - 2) + layer_of(layer + 2))
            growth = growth * (1.0 / 12.0)
            if comp == 1:
                hot = jnp.where(spots == cell_of + layer * rows_y, 1.0, 0.0).astype(jnp.bfloat16)
                plane = mm(hot, trace_parts[0], ((1,), (1,)))
                plane = plane + mm(hot, trace_parts[1], ((1,), (1,)))
                plane = plane + mm(hot, trace_parts[2], ((1,), (1,)))
                growth = jnp.concatenate(
                    [growth[:, :LANES] + plane, growth[:, LANES:]], axis=1
                )
            change = speed * growth
            moved = 2.0 * here - later_ref[comp, layer] + change
            if held:
                field_ref[layer] = moved
            else:
                new_ref[comp, layer] = moved
            if comp == 1:
                term = now_ref[0, layer] * change
                if not first:
                    term = contrib_from[layer] + term
                if framing:
                    terms_ref[layer] = term
                else:
                    contrib_ref[layer] = term
            elif lines:
                take_lines(new_ref, saved_ref, shot, step, layer)
            if last and not held:
                store(new_ref.at[comp, layer], out_ref.at[shot, 0, comp, layer])
    if framing:
        for layer in range(layers):
            empty = jnp.zeros_like(contrib_ref[layer])
            contrib_ref[layer] = empty if frame_from is None else frame_from[layer]
        for layer in range(layers):
            put_window(contrib_ref, layer, terms_ref, offsets_ref[shot], frame_from)
    for started in stores:
        started.wait()
    if not last:
        write_sends(new_ref, send_groups, send_refs)


def one_step(
    shot, step, comps, got_groups, send_groups,
    wavefields, offsets, now, later, got, saved, pos, traces, speed, contrib, frame, out, after, heavy, model_y, keeps=(), field=None,
):
    first, last = step == 0, step == STEPS - 1
    with_image = 1 in comps
    shots = wavefields.shape[0]
    both, layers, rows_y, cells_z = wavefields.shape[2:]
    vmem, hbm = pl.BlockSpec(memory_space=VMEM), pl.BlockSpec(memory_space=HBM)
    state = jax.ShapeDtypeStruct((both, layers, rows_y, cells_z), jnp.float32)
    image = jax.ShapeDtypeStruct((layers, rows_y, cells_z), jnp.float32)
    aliases = {}
    scratch = []
    args = [
        pltpu.with_memory_space_constraint(field, HBM) if field is wavefields else field
        for field in (now, later)
    ]
    specs = [hbm if first else vmem, hbm if step < 2 else vmem]
    args += [value for pair in got for value in pair]
    specs += [vmem] * (2 * len(got))
    lines = saved is not None and 0 in comps
    if lines:
        args.append(saved)
        specs.append(vmem)
    if with_image:
        args += [pos, traces]
        specs += [vmem, vmem]
    framing = last and with_image
    if first or framing:
        args.append(offsets)
        specs.append(pl.BlockSpec(memory_space=SMEM))
    args.append(speed)
    specs.append(vmem)
    if with_image and not first:
        args.append(contrib)
        specs.append(vmem)
    if frame is not None:
        args.append(frame)
        specs.append(vmem)
    args += [value for _, value in keeps]
    specs += [vmem] * len(keeps)
    held = last and comps == (1,)
    if last and comps == (0,):
        args.append(field)
        specs.append(vmem)
    args += after
    specs += [pl.BlockSpec(memory_space=pl.ANY)] * len(after)
    if held:
        outs = [image]
        out_specs = [vmem]
    elif last:
        if out is not None:
            aliases[len(args)] = 0
            args.append(out)
            specs.append(hbm)
        outs = [jax.ShapeDtypeStruct((shots, 2) + state.shape, jnp.float32)]
        out_specs = [hbm]
        scratch = [
            pltpu.VMEM(state.shape, jnp.float32),
            pltpu.SemaphoreType.DMA((1 + len(keeps) + both * layers,)),
        ]
    else:
        outs = [state]
        for group in send_groups:
            half = halo_shape(group, rows_y, cells_z)
            outs += [half, half]
        out_specs = [vmem] * len(outs)
    if framing:
        outs.append(jax.ShapeDtypeStruct((layers, model_y + 8, cells_z), jnp.float32))
        out_specs.append(vmem)
    elif with_image:
        outs.append(image)
        out_specs.append(vmem)
    if first:
        outs.append(image)
        out_specs.append(vmem)
    if framing:
        scratch.append(pltpu.VMEM(image.shape, jnp.float32))
    if step < 2:
        lead = (2,) if first else ()
        scratch = [pltpu.VMEM(lead + state.shape, jnp.float32), pltpu.SemaphoreType.DMA((1,))]
    return pl.pallas_call(
        functools.partial(
            step_kernel, shot, step, comps, got_groups, send_groups, out is None, frame is not None, lines,
            len(after), tuple(keep for keep, _ in keeps),
        ),
        in_specs=specs,
        out_specs=out_specs,
        out_shape=outs,
        scratch_shapes=scratch,
        input_output_aliases=aliases,
        compiler_params=params(),
        cost_estimate=cost(HEAVY if heavy else 0),
        name="step_%d_shot_%d" % (step, shot),
    )(*args)


def sum_kernel(scale, *refs):
    image_ref, sum_ref, sems = refs[-3:]
    frame_refs = refs[:-4]
    layers, model_y, _ = sum_ref.shape
    stores = []
    for layer in range(layers):
        for row in range(0, model_y, 16):
            rows = slice(row, row + 16)
            total = None
            for at in range(0, len(frame_refs), 2):
                pair = frame_refs[at][layer, rows] + frame_refs[at + 1][layer, rows]
                total = pair if total is None else total + pair
            sum_ref[layer, rows] = total * scale
        stores.append(
            pltpu.make_async_copy(sum_ref.at[layer], image_ref.at[layer], sems.at[layer])
        )
        stores[-1].start()
    for started in stores:
        started.wait()


def sum_frames(frames, others, scale, model_y, after):
    layers, _, cells_z = frames[0].shape
    vmem, hbm = pl.BlockSpec(memory_space=VMEM), pl.BlockSpec(memory_space=HBM)
    args = [value for pair in zip(frames, others) for value in pair]
    shape_out = jax.ShapeDtypeStruct((layers, model_y, cells_z), jnp.float32)
    return pl.pallas_call(
        functools.partial(sum_kernel, scale),
        in_specs=[vmem] * len(args) + [hbm],
        out_specs=hbm,
        out_shape=shape_out,
        scratch_shapes=[
            pltpu.VMEM(shape_out.shape, jnp.float32),
            pltpu.SemaphoreType.DMA((layers,)),
        ],
        compiler_params=params(),
        cost_estimate=cost(),
        name="sum_frames",
    )(*args, pltpu.with_memory_space_constraint(after, HBM))


def body(wavefields, courant, offsets, strip_lines, strip_ids, receiver_pos, traces):
    shots = wavefields.shape[0]
    layers = wavefields.shape[3]
    cells_z = wavefields.shape[5]
    model_y = courant.shape[1]
    per_owner = STEPS * EDGE * layers
    shot_devices = lax.axis_size("shot")
    scale = 1.0 / (shots * shot_devices)
    cap = strip_lines.shape[1] // lax.axis_size("space")

    def exchange(sends):
        return [
            (swap_pairs(sends[at], 0), swap_pairs(sends[at + 1], 1)) for at in range(0, len(sends), 2)
        ]

    sends = pack_halo(wavefields, 0, [])
    got = [exchange(sends)]
    message = pack_lines(strip_lines, strip_ids, per_owner, cap, sends[0])
    saved = deliver(message, cap, shots, per_owner)
    for shot in range(1, shots):
        got.append(exchange(pack_halo(wavefields, shot, [message])))
    groups = [BOTH] * shots
    now = [wavefields] * shots
    later = [wavefields] * shots
    contrib = [None] * shots
    speed = [courant] * shots
    out = None
    frame = None
    after = []
    for step in range(STEPS):
        for shot in range(shots):
            split = shot == shots - 1
            send_groups = SPLIT if split and step == STEPS - 2 else BOTH
            common = (wavefields, offsets, now[shot], later[shot])
            fixed = (receiver_pos, traces, speed[shot])
            if step < STEPS - 1:
                early = step == 0 and shot == 0
                made = one_step(
                    shot, step, BOTH[0], groups[shot], () if early else send_groups, *common,
                    got[shot], None if early else saved, *fixed, contrib[shot], None, None, after, early,
                    model_y,
                )
                later[shot], now[shot] = now[shot], made[0]
                if early:
                    made = [*finish_first(shot, made[0], saved), *made[1:]]
                    now[shot] = made[0]
                ends = 1 + 2 * len(send_groups)
                got[shot] = exchange(made[1:ends])
                groups[shot] = send_groups
                contrib[shot] = made[ends]
                if step == 0:
                    speed[shot] = made[ends + 1]
                after = [made[1]]
                continue
            keeps = [] if split and shots > 1 else [(shot, now[shot])]
            if shot == 0 and shots > 1:
                keeps.append((shots - 1, now[shots - 1]))
            field = None
            for group in groups[shot]:
                made = one_step(
                    shot, step, group, (group,), (), *common, got[shot][:1], saved, *fixed,
                    contrib[shot], frame if 1 in group else None, out, after, group == (0,), model_y,
                    () if group == (1,) else keeps, field,
                )
                got[shot] = got[shot][1:]
                if group == (1,):
                    field = made[0]
                else:
                    out = made[0]
                if 1 in group:
                    frame = made[1]
                    after = [made[1]]
    if shot_devices == 2:
        other = lax.ppermute(frame, "shot", [(0, 1), (1, 0)])
        image = sum_frames([frame], [other], scale, model_y, out)
    else:
        image = lax.psum(frame[:, :model_y], "shot") * scale
    return (out, image)


def solution(mesh):
    placed = (
        P("shot", None, None, "space", None, None),
        P("space", None, None),
        P("shot"),
        P("shot", "space", None),
        P("shot", "space"),
        P("shot", "space"),
        P("shot", None, "space"),
    )
    return jax.shard_map(
        body,
        mesh=mesh,
        in_specs=placed,
        out_specs=(P("shot", None, None, "space", None, None), P("space", None, None)),
        check_vma=False,
    )
```
